32 devices in a mesh: gx: 4 (over y, x), gy: 8 (over z, core).
Axes of the slice: x: 2, y: 2, z: 4, core: 2. Of those that a mesh axis runs over, the one named last changes fastest.
Arguments:
- hidden_in: bfloat16 [4096, 2048], P('gy', 'gx'), may hold values from -6 to 6
- expert_routes: int32 [4096, 6], P('gy'), may hold values from 0 to 63, all different within a row; in each aligned block of 512 rows (0 to 511, 512 to 1023, ...) at most 64 rows name the same one
- piece_starts: int32 [4, 2], P('gx'), may hold values from 0 to 768, as said below
- query_weight: bfloat16 [2048, 3072], P('gx', 'gy'), may hold values from -0.125 to 0.125
- latent_weight: bfloat16 [2048, 576], P('gx', 'gy'), may hold values from -0.125 to 0.125
- latent_gain: bfloat16 [512], replicated, may hold values from 0.5 to 1.5
- expand_weight: bfloat16 [512, 4096], P(None, 'gy'), may hold values from -0.25 to 0.25
- output_weight: bfloat16 [2048, 2048], P('gy', 'gx'), may hold values from -2 to 2
- attention_gain: bfloat16 [2048], P('gx'), may hold values from 0.5 to 1.5
- ffn_gain: bfloat16 [2048], P('gx'), may hold values from 0.5 to 1.5
- router_weight: bfloat16 [2048, 64], P('gx'), may hold values from -0.0625 to 0.0625
- gate_weight: bfloat16 [64, 2048, 1408], P('gy', 'gx'), may hold values from -0.125 to 0.125
- up_weight: bfloat16 [64, 2048, 1408], P('gy', 'gx'), may hold values from -0.125 to 0.125
- down_weight: bfloat16 [64, 1408, 2048], P('gy', None, 'gx'), may hold values from -2.5 to 2.5
- shared_gate: bfloat16 [2048, 2816], P('gx', 'gy'), may hold values from -0.125 to 0.125
- shared_up: bfloat16 [2048, 2816], P('gx', 'gy'), may hold values from -0.125 to 0.125
- shared_down: bfloat16 [2816, 2048], P('gy', 'gx'), may hold values from -0.21875 to 0.21875
- grad_out: bfloat16 [4096, 2048], P('gy', 'gx'), may hold values from -6 to 6
Outputs:
- mixed: bfloat16 [4096, 2048], P('gy', 'gx')
- grad_hidden: float32 [4096, 2048], P('gy', 'gx')
- grad_query: float32 [2048, 3072], P('gx', 'gy')
- grad_latent: float32 [2048, 576], P('gx', 'gy')
- grad_latent_gain: float32 [512], replicated
- grad_expand: float32 [512, 4096], P(None, 'gy')
- grad_output: float32 [2048, 2048], P('gy', 'gx')
- grad_attention_gain: float32 [2048], P('gx')
- grad_ffn_gain: float32 [2048], P('gx')
- grad_router: float32 [2048, 64], P('gx')
- grad_gate: float32 [64, 2048, 1408], P('gy', 'gx')
- grad_up: float32 [64, 2048, 1408], P('gy', 'gx')
- grad_down: float32 [64, 1408, 2048], P('gy', None, 'gx')
- grad_shared_gate: float32 [2048, 2816], P('gx', 'gy')
- grad_shared_up: float32 [2048, 2816], P('gx', 'gy')
- grad_shared_down: float32 [2816, 2048], P('gy', 'gx')
The draws below stay inside these ranges and needn't reach their ends.
Inputs may be any that keep to these rules, and one draw needn't show every extreme that they name: `expert_routes`: each row names 6 different experts. In each aligned block of 512 rows no expert is named by more than 64 rows, a bound that some block reaches. `piece_starts`: two pieces of 256 tokens per sequence: the first starts in the first half of the sequence and the second in the second half, so they never intersect and stay inside the sequence.
All inputs are finite; a program needn't handle non-finite values.
Results may differ from the reference program's by a relative error of at most 0.035.
Values may be sent and summed in bfloat16 or wider, within the bound.
A program may use at most 576 MiB of HBM per device.

```python
import math
import jax
import jax.numpy as jnp
import numpy as np
from jax import lax

D = 2048
H = 16
DN = 128
DR = 64
DV = 128
L = 512
EXPERTS = 64
FF = 1408
TOPK = 6
SEQ_LEN = 1024
PIECE = 256
FS = 2816
TOKENS = 4096
SEQS = 4
ROUTE_BLOCK = 512
CAP = 64
N_GY = 8


def draw_piece_starts(key, part):
    key = jax.random.fold_in(key, 7)
    half = SEQ_LEN // 2
    span = half - PIECE + 1
    first = jax.random.randint(jax.random.fold_in(key, 1), (SEQS,), 0, span)
    second = half + jax.random.randint(jax.random.fold_in(key, 2), (SEQS,), 0, span)
    lowest = jax.random.randint(jax.random.fold_in(key, 3), (), 0, SEQS)
    highest = jax.random.randint(jax.random.fold_in(key, 4), (), 0, SEQS)
    number = jnp.arange(SEQS)
    first = jnp.where(number == lowest, 0, first)
    second = jnp.where(number == highest, SEQ_LEN - PIECE, second)
    return jnp.stack([first, second], axis=1).astype(jnp.int32)


def block_levels(rng, shape, shards, smallest, top_value):
    factor_of, own = 1.0, jax.random.fold_in(rng, 6)
    for dim, shards_of in shards:
        heights = jnp.exp(jax.random.uniform(jax.random.fold_in(own, dim), (shards_of,), jnp.float32, smallest / len(shards), top_value / len(shards)))
        factor_of = factor_of * jnp.repeat(heights, shape[dim] // shards_of).reshape([-1 if axis == dim else 1 for axis in range(len(shape))])
    return factor_of


def routed_block(rng, own, number, rows, count, top, limit, skew):
    sequence = jax.random.permutation(rng, count)
    crowded, common = load_shares(count, rows * top, limit, skew, True), load_shares(count, rows * top, limit, skew, False)
    places = jnp.arange(count)

    def named(sizes, offset_by):
        used = int((sizes > 0).sum())
        fixed = max(1, used // 4)
        moved = fixed + (places - fixed + offset_by * (used - fixed)) % max(1, count - fixed)
        return jnp.zeros((count,), jnp.int32).at[sequence[jnp.where(places < fixed, places, moved)]].set(jnp.asarray(sizes, jnp.int32))

    sizes = jnp.where(number % 4 == 0, named(crowded, number // 4), named(common, number - number // 4 - 1))
    mixed = jax.random.permutation(jax.random.fold_in(own, 3), count)
    donor, sink = mixed[0:count // 2 * 2:2], mixed[1:count // 2 * 2:2]
    margin = jnp.minimum(sizes[donor] - 1, limit - sizes[sink]) // 2
    margin = jnp.where((donor == sequence[0]) | (sink == sequence[0]) | (sizes[sink] == 0), 0, jnp.maximum(margin, 0))
    moved = jax.random.randint(jax.random.fold_in(own, 4), (count // 2,), 0, 1 << 20) % (margin + 1)
    sizes = sizes.at[donor].add(-moved).at[sink].add(moved)
    items = jnp.searchsorted(jnp.cumsum(sizes), jnp.arange(rows * top), side="right").astype(jnp.int32)
    grid = items.reshape(top, rows).T
    grid = grid[jax.random.permutation(jax.random.fold_in(own, 1), rows)]
    offset_by = jax.random.randint(jax.random.fold_in(own, 2), (rows, 1), 0, top)
    return jnp.take_along_axis(grid, (jnp.arange(top)[None, :] + offset_by) % top, axis=1)


def load_shares(amount, total, reach, slope, full):
    weights = [(1 << 20) // math.isqrt(rank ** slope) + 1 for rank in range(1, amount + 1)]
    largest = reach if full else min(reach, max(-(-total // amount), total * weights[0] // sum(weights)))
    least = 1 if total - largest >= amount - 1 else 0
    holding, spare = [largest] + [least] * (amount - 1), total - largest - least * (amount - 1)
    while spare > 0:
        candidates = [i for i in range(1, amount) if holding[i] < largest] or [i for i in range(1, amount) if holding[i] < reach]
        whole, budget = sum([weights[i] for i in candidates]), spare
        for i in candidates:
            more = min(reach - holding[i], max(1, budget * weights[i] // whole), spare)
            holding[i] = holding[i] + more
            spare = spare - more
    return np.array(holding)


def normal_values(stream_key, extent, deviation, most, split=(), kind=jnp.bfloat16):
    result = jax.random.normal(stream_key, extent, jnp.float32) * deviation
    if len(split) > 0:
        result = block_levels(stream_key, extent, split, -0.22, 0.18) * result
    return jnp.clip(result, min=-most, max=most).astype(kind)


def setup_inputs(seed: int = 0) -> dict:
    key_list = jax.random.split(jax.random.key(seed), 19)
    hidden_in = normal_values(key_list[0], (TOKENS, D), 1.0, 6.0, ((0, 8), (1, 4)))
    expert_routes_keys = jax.random.split(jax.random.fold_in(key_list[1], 1), TOKENS // ROUTE_BLOCK)
    expert_routes_turns = jax.random.permutation(jax.random.fold_in(key_list[1], 3), TOKENS // ROUTE_BLOCK)
    expert_routes = jax.vmap(lambda own, number: routed_block(jax.random.fold_in(key_list[1], 2), own, number, ROUTE_BLOCK, EXPERTS, TOPK, CAP, 1))(expert_routes_keys, expert_routes_turns).reshape((TOKENS, TOPK))
    piece_starts = draw_piece_starts(jax.random.fold_in(key_list[18], 71), 0)
    query_weight = normal_values(key_list[3], (D, H * (DN + DR)), D ** -0.5, 0.125, ((0, 4), (1, 8)))
    latent_weight = normal_values(key_list[4], (D, L + DR), D ** -0.5, 0.125, ((0, 4), (1, 8)))
    latent_gain = jnp.clip(1.0 + 0.1 * jax.random.normal(key_list[5], (L,), jnp.float32), 0.5, 1.5).astype(jnp.bfloat16)
    expand_weight = normal_values(key_list[6], (L, H * (DN + DV)), L ** -0.5, 0.25, ((1, 8),))
    output_weight = normal_values(key_list[7], (H * DV, D), (H * DV // 256) ** -0.5, 2.0, ((0, 8), (1, 4)))
    attention_gain = jnp.clip(1.0 + 0.1 * jax.random.normal(key_list[8], (D,), jnp.float32), 0.5, 1.5).astype(jnp.bfloat16)
    ffn_gain = jnp.clip(1.0 + 0.1 * jax.random.normal(key_list[9], (D,), jnp.float32), 0.5, 1.5).astype(jnp.bfloat16)
    router_weight = normal_values(key_list[10], (D, EXPERTS), (4 * D) ** -0.5, 0.0625, ((0, 4),))
    gate_weight = normal_values(key_list[11], (EXPERTS, D, FF), D ** -0.5, 0.125, ((0, 8), (1, 4)))
    up_weight = normal_values(key_list[12], (EXPERTS, D, FF), D ** -0.5, 0.125, ((0, 8), (1, 4)))
    down_weight = normal_values(key_list[13], (EXPERTS, FF, D), (max(1, FF // 256)) ** -0.5, 2.5, ((0, 8), (2, 4)))
    shared_gate = normal_values(key_list[14], (D, FS), D ** -0.5, 0.125, ((0, 4), (1, 8)))
    shared_up = normal_values(key_list[15], (D, FS), D ** -0.5, 0.125, ((0, 4), (1, 8)))
    shared_down = normal_values(key_list[16], (FS, D), (FS // 4) ** -0.5, 0.21875, ((0, 8), (1, 4)))
    grad_out = normal_values(key_list[17], (TOKENS, D), 1.0, 6.0, ((0, 8), (1, 4)))
    return dict(hidden_in=hidden_in, expert_routes=expert_routes, piece_starts=piece_starts, query_weight=query_weight, latent_weight=latent_weight, latent_gain=latent_gain, expand_weight=expand_weight, output_weight=output_weight, attention_gain=attention_gain, ffn_gain=ffn_gain, router_weight=router_weight, gate_weight=gate_weight, up_weight=up_weight, down_weight=down_weight, shared_gate=shared_gate, shared_up=shared_up, shared_down=shared_down, grad_out=grad_out)


EPS = 1e-06
HIGH = lax.Precision.HIGHEST

@jax.custom_vjp
def low(v):
    return lax.optimization_barrier(v.astype(jnp.bfloat16)).astype(jnp.float32)

@jax.custom_vjp
def low_back(v):
    return v

def low_keep(v):
    return (low(v), None)

def low_pass(kept, grad):
    return (grad,)

def back_keep(v):
    return (v, None)

def back_low(kept, grad):
    return (low(grad),)
low.defvjp(low_keep, low_pass)
low_back.defvjp(back_keep, back_low)

def rms_norm(value, gain):
    return value * lax.rsqrt(lax.optimization_barrier(jnp.mean(value * value, axis=-1, keepdims=True)) + EPS) * gain

def silu(value):
    return value * jax.nn.sigmoid(value)

def rotate(value, cosine, sine):
    half = value.shape[-1] // 2
    first = value[..., :half]
    second = value[..., half:]
    return jnp.concatenate([first * cosine - second * sine, second * cosine + first * sine], axis=-1)

def rope_tables(length):
    half = DR // 2
    position = jnp.arange(length).astype(jnp.float32)
    inverse = jnp.exp(-math.log(10000.0) * jnp.arange(half).astype(jnp.float32) / half)
    angle = position[:, None] * inverse[None, :]
    return (jnp.cos(angle), jnp.sin(angle))

def piece_ids(starts, length):
    position = jnp.arange(length, dtype=jnp.int32)
    ids = jnp.zeros(starts.shape[:-1] + (length,), jnp.int32)
    for number in range(starts.shape[-1]):
        begin = starts[..., number:number + 1]
        inside = (position >= begin) & (position < begin + PIECE)
        ids = ids + jnp.where(inside, number + 1, 0)
    return ids

def allowed_keys(query_pos, key_pos, query_ids, key_ids):
    causal = key_pos[None, :] <= query_pos[:, None]
    same = (query_ids[:, None] == key_ids[None, :]) & (query_ids[:, None] > 0)
    return causal | same

def attend_item(item):
    query, keys, values, ids = item
    scale = (DN + DR) ** (-0.5)
    scores = low_back(jnp.einsum('qhc,khc->hqk', query, keys, precision=HIGH) * scale)
    position = jnp.arange(SEQ_LEN, dtype=jnp.int32)
    mask = allowed_keys(position, position, ids, ids)
    weights = jax.nn.softmax(jnp.where(mask[None], scores, -1e+30), axis=-1)
    return jnp.einsum('hqk,khc->qhc', low(weights), values, precision=HIGH)

def slot_tables(expert_routes):
    flat = expert_routes.reshape(N_GY, ROUTE_BLOCK * TOPK)
    hits = (flat[:, :, None] == jnp.arange(EXPERTS, dtype=jnp.int32)[None, None, :]).astype(jnp.int32)
    before = jnp.cumsum(hits, axis=1) - hits
    slot = lax.optimization_barrier(jnp.sum(before * hits, axis=2))
    group = jnp.arange(N_GY, dtype=jnp.int32)[:, None]
    destination = flat * (N_GY * CAP) + group * CAP + slot
    token = jnp.arange(TOKENS * TOPK, dtype=jnp.int32) // TOPK
    owner = jnp.full((EXPERTS * N_GY * CAP,), TOKENS, jnp.int32).at[destination.reshape(-1)].set(token)
    return (destination.reshape(TOKENS, TOPK), owner)

def expert_item(item):
    rows, gate_e, up_e, down_e = item
    gate_pre = low_back(jnp.dot(rows, gate_e, precision=HIGH))
    up_pre = low_back(jnp.dot(rows, up_e, precision=HIGH))
    inner = low(silu(gate_pre) * up_pre)
    return low_back(low(jnp.dot(inner, down_e, precision=HIGH)))

def forward(hidden, query_weight, latent_weight, latent_gain, expand_weight, output_weight, attention_gain, ffn_gain, router_weight, gate_weight, up_weight, down_weight, shared_gate, shared_up, shared_down, expert_routes, piece_starts):
    norm_one = low(rms_norm(hidden, attention_gain))
    query = low_back(jnp.dot(norm_one, query_weight, precision=HIGH))
    latent = low_back(low(jnp.dot(norm_one, latent_weight, precision=HIGH)))
    compressed = latent[:, :L]
    rope_key = latent[:, L:]
    latent_norm = low(rms_norm(compressed, latent_gain))
    expanded = low_back(jnp.dot(latent_norm, expand_weight, precision=HIGH)).reshape(TOKENS, H, DN + DV)
    cosine, sine = rope_tables(SEQ_LEN)
    cosine = jnp.tile(cosine, (SEQS, 1))
    sine = jnp.tile(sine, (SEQS, 1))
    query = query.reshape(TOKENS, H, DN + DR)
    query_full = low(jnp.concatenate([query[..., :DN], rotate(query[..., DN:], cosine[:, None], sine[:, None])], axis=-1))
    key_rope = rotate(rope_key, cosine, sine)
    key_full = low(jnp.concatenate([expanded[..., :DN], jnp.broadcast_to(key_rope[:, None, :], (TOKENS, H, DR))], axis=-1))
    value_full = low(expanded[..., DN:])
    ids = piece_ids(piece_starts, SEQ_LEN)
    attended = lax.map(jax.checkpoint(attend_item), (query_full.reshape(SEQS, SEQ_LEN, H, DN + DR), key_full.reshape(SEQS, SEQ_LEN, H, DN + DR), value_full.reshape(SEQS, SEQ_LEN, H, DV), ids))
    attended = low_back(low(attended.reshape(TOKENS, H * DV)))
    after_attention = hidden + low_back(jnp.dot(attended, output_weight, precision=HIGH))
    norm_two = low(rms_norm(after_attention, ffn_gain))
    logits = low_back(jnp.dot(norm_two, router_weight, precision=HIGH))
    probs = jax.nn.softmax(logits, axis=-1)
    gates = jnp.take_along_axis(probs, expert_routes, axis=1)
    destination, owner = slot_tables(expert_routes)
    padded = jnp.concatenate([norm_two, jnp.zeros((1, D), norm_two.dtype)], axis=0)
    rows = low_back(padded[owner]).reshape(EXPERTS, N_GY * CAP, D)
    outputs = lax.map(jax.checkpoint(expert_item), (rows, gate_weight, up_weight, down_weight))
    picked = outputs.reshape(EXPERTS * N_GY * CAP, D)[destination]
    routed = lax.optimization_barrier(jnp.sum(gates[:, :, None] * picked, axis=1))
    shared_gate_pre = low_back(jnp.dot(norm_two, shared_gate, precision=HIGH))
    shared_up_pre = low_back(jnp.dot(norm_two, shared_up, precision=HIGH))
    shared_hidden = low(silu(shared_gate_pre) * shared_up_pre)
    shared_out = low_back(jnp.dot(shared_hidden, shared_down, precision=HIGH))
    return after_attention + routed + shared_out

def reference(hidden_in, expert_routes, piece_starts, query_weight, latent_weight, latent_gain, expand_weight, output_weight, attention_gain, ffn_gain, router_weight, gate_weight, up_weight, down_weight, shared_gate, shared_up, shared_down, grad_out):

    def run(hidden, q_weight, l_weight, l_gain, e_weight, o_weight, a_gain, f_gain, r_weight, g_weight, u_weight, d_weight, s_gate, s_up, s_down):
        return forward(hidden, q_weight, l_weight, l_gain, e_weight, o_weight, a_gain, f_gain, r_weight, g_weight, u_weight, d_weight, s_gate, s_up, s_down, expert_routes, piece_starts)
    mixed, pull = jax.vjp(run, hidden_in.astype(jnp.float32), query_weight.astype(jnp.float32), latent_weight.astype(jnp.float32), latent_gain.astype(jnp.float32), expand_weight.astype(jnp.float32), output_weight.astype(jnp.float32), attention_gain.astype(jnp.float32), ffn_gain.astype(jnp.float32), router_weight.astype(jnp.float32), gate_weight.astype(jnp.float32), up_weight.astype(jnp.float32), down_weight.astype(jnp.float32), shared_gate.astype(jnp.float32), shared_up.astype(jnp.float32), shared_down.astype(jnp.float32))
    grads = pull(grad_out.astype(jnp.float32))
    return (mixed.astype(jnp.bfloat16), grads[0], grads[1], grads[2], grads[3], grads[4], grads[5], grads[6], grads[7], grads[8], grads[9], grads[10], grads[11], grads[12], grads[13], grads[14])
```

```python
import functools
import math

import jax
import jax.numpy as jnp
from jax import lax
from jax.experimental import pallas as pl
from jax.experimental.pallas import tpu as pltpu
from jax.sharding import PartitionSpec as P

D = 2048
DN = 128
DR = 64
DV = 128
L = 512
EXPERTS = 64
FF = 1408
TOPK = 6
SEQ_LEN = 1024
PIECE = 256


EPS = 1e-06
BF16 = jnp.bfloat16
F32 = jnp.float32
VMEM_LIMIT = 56 * 1024 * 1024


def params():
    return pltpu.CompilerParams(vmem_limit_bytes=VMEM_LIMIT)


def cost(flops, read, written):
    return pl.CostEstimate(flops=flops, bytes_accessed=read + written, transcendentals=0)


def after(value, *others):
    return lax.optimization_barrier((value, others))[0]


def swap(value, bit):
    return lax.ppermute(value, "gx", [(i, i ^ bit) for i in range(4)])


def square():
    return lax.axis_size("gx") == 4


def place():
    me = lax.axis_index("gx")
    return me & 1, me >> 1


def pick(value, index, axis):
    return lax.dynamic_index_in_dim(value, index, axis, keepdims=False)


def collect(block):
    if not square():
        return lax.all_gather(block, "gx", axis=0, tiled=False)
    half = block.shape[0] // 2
    from_x = swap(block, 1)
    from_y = swap(block, 2)
    across = jnp.concatenate([swap(from_y[:half], 1), swap(from_x[half:], 2)], axis=0)
    me = lax.axis_index("gx")
    whole = jnp.zeros((4,) + block.shape, block.dtype)
    for index, value in ((me, block), (me ^ 1, from_x), (me ^ 2, from_y), (me ^ 3, across)):
        whole = lax.dynamic_update_index_in_dim(whole, value, index, 0)
    return whole


def collect_rows(block):
    whole = collect(block)
    return whole.reshape((-1,) + block.shape[1:])


def feature_total(value):
    return lax.psum(value, "gx")


def square_total(value):
    if not square():
        return lax.psum(value, "gx")
    value = value + swap(value, 1)
    return value + swap(value, 2)


def spread_rows(value):
    return lax.all_gather(value, "gy", axis=0, tiled=True)


def outer_total(partial):
    total = lax.psum_scatter(partial.astype(BF16), "gy", scatter_dimension=0, tiled=True)
    return total.astype(F32)


def to_tokens(value):
    return lax.all_to_all(value, "gx", split_axis=0, concat_axis=1, tiled=True)


def to_features(value):
    return lax.all_to_all(value, "gx", split_axis=1, concat_axis=0, tiled=True)


def dot(a, b):
    return jnp.dot(a, b, preferred_element_type=F32)


def dot_nt(a, b):
    return lax.dot_general(a, b, (((1,), (1,)), ((), ())), preferred_element_type=F32)


def dot_tn(a, b):
    return lax.dot_general(a, b, (((0,), (0,)), ((), ())), preferred_element_type=F32)


def one_hot_kernel(cap, code_ref, out_ref):
    experts = code_ref.shape[1]
    tokens, slots = out_ref.shape
    column = lax.broadcasted_iota(jnp.int32, (experts, slots), 1)
    low = lax.broadcasted_iota(jnp.int32, (experts, slots), 0) * cap
    inside = (column >= low) & (column < low + cap)
    expand = jnp.where(inside, 1.0, 0.0).astype(BF16)
    offset = jnp.sum(jnp.where(inside, column - low, 0).astype(F32), axis=0, keepdims=True)
    wide = dot(code_ref[...].astype(BF16), expand)
    out_ref[...] = jnp.where(wide == offset, 1.0, 0.0).astype(BF16)


def one_hot(code, cap, blocks):
    tokens, experts = code.shape
    block = tokens // blocks
    return pl.pallas_call(
        functools.partial(one_hot_kernel, cap),
        grid=(blocks,),
        in_specs=[pl.BlockSpec((block, experts), lambda b: (b, 0))],
        out_specs=pl.BlockSpec((block, experts * cap), lambda b: (b, 0)),
        out_shape=jax.ShapeDtypeStruct((tokens, experts * cap), BF16),
        compiler_params=params(),
        name="one_hot",
    )(code)


def dispatch_kernel(chosen_ref, rows_ref, out_ref):
    moved = dot_tn(chosen_ref[...], rows_ref[...]).astype(BF16)
    out_ref[...] = moved.reshape(out_ref.shape)


def dispatch(chosen, rows, cap, blocks):
    tokens, width = rows.shape
    slots = chosen.shape[1]
    experts = slots // cap
    block = tokens // blocks
    return pl.pallas_call(
        dispatch_kernel,
        grid=(blocks,),
        in_specs=[
            pl.BlockSpec((block, slots), lambda b: (b, 0)),
            pl.BlockSpec((block, width), lambda b: (b, 0)),
        ],
        out_specs=pl.BlockSpec((experts, cap, width), lambda b: (0, b, 0)),
        out_shape=jax.ShapeDtypeStruct((experts, blocks * cap, width), BF16),
        compiler_params=params(),
        cost_estimate=cost(2 * tokens * slots * width, 4 * tokens * width, 2 * tokens * width),
        name="dispatch",
    )(chosen, rows)


def combine_kernel(groups, chosen_ref, *refs):
    out_ref = refs[-1]
    width = out_ref.shape[1]
    pieces = [ref[...].reshape(-1, width) for ref in refs[:groups]]
    slots = pieces[0] if groups == 1 else jnp.concatenate(pieces, axis=0)
    total = dot(chosen_ref[...], slots)
    for ref in refs[groups:-1]:
        total += ref[...].astype(F32)
    out_ref[...] = total.astype(out_ref.dtype)


def combine(chosen, pieces, cap, blocks, extra=()):
    tokens, slots = chosen.shape
    block = tokens // blocks
    width = pieces[0].shape[-1]
    specs = [pl.BlockSpec((block, slots), lambda b: (b, 0))]
    specs += [pl.BlockSpec((p.shape[0], cap, width), lambda b: (0, b, 0)) for p in pieces]
    specs += [pl.BlockSpec((block, width), lambda b: (b, 0)) for _ in extra]
    return pl.pallas_call(
        functools.partial(combine_kernel, len(pieces)),
        grid=(blocks,),
        in_specs=specs,
        out_specs=pl.BlockSpec((block, width), lambda b: (b, 0)),
        out_shape=jax.ShapeDtypeStruct((tokens, width), BF16),
        compiler_params=params(),
        cost_estimate=cost(2 * tokens * slots * width, 4 * tokens * width, 2 * tokens * width),
        name="combine",
    )(chosen, *pieces, *extra)


def group_kernel(parts, weights, adds, transposed, picks_ref, *refs):
    rows = [ref[0, 0] for ref in refs[:parts]]
    source = rows[0] if parts == 1 else jnp.concatenate(rows, axis=0)
    out_ref = refs[-1]
    extra = refs[parts + weights : parts + weights + adds]
    for number in range(weights):
        weight = refs[parts + number][0]
        total = dot_nt(source, weight) if transposed else dot(source, weight)
        for ref in extra:
            total += ref[0, number, 0].astype(F32)
        out_ref[0, number] = total.astype(out_ref.dtype).reshape(out_ref.shape[2:])


def group(rows, picks, parts, weights, first, count, transposed=False, adds=(), kind=BF16, by_quarter=False):
    slots, depth = rows.shape[2:]
    width = weights[0].shape[1] if transposed else weights[0].shape[2]
    many = len(weights)

    def row_spec(part):
        if by_quarter:
            return pl.BlockSpec((1, 1, slots, depth), lambda e, p: (p[part], first + e, 0, 0))
        return pl.BlockSpec((1, 1, slots, depth), lambda e, p: (first + e, p[part], 0, 0))

    def add_spec(number):
        return pl.BlockSpec((1, many, 1, slots, width), lambda e, p: (e, 0, p[parts + number], 0, 0))

    specs = [row_spec(part) for part in range(parts)]
    for weight in weights:
        if by_quarter:
            specs.append(pl.BlockSpec((1,) + weight.shape[1:], lambda e, p: (0, 0, 0)))
        else:
            specs.append(pl.BlockSpec((1,) + weight.shape[1:], lambda e, p: (first + e, 0, 0)))
    specs += [add_spec(number) for number in range(len(adds))]
    return pl.pallas_call(
        functools.partial(group_kernel, parts, many, len(adds), transposed),
        grid_spec=pltpu.PrefetchScalarGridSpec(
            num_scalar_prefetch=1,
            grid=(count,),
            in_specs=specs,
            out_specs=pl.BlockSpec((1, many, parts, slots, width), lambda e, p: (e, 0, 0, 0, 0)),
        ),
        out_shape=jax.ShapeDtypeStruct((count, many, parts, slots, width), kind),
        compiler_params=params(),
        cost_estimate=cost(
            2 * many * count * parts * slots * depth * width,
            2 * many * count * depth * width,
            2 * many * count * parts * slots * width,
        ),
        name="group",
    )(picks, *([rows] * parts), *weights, *adds)


def numbers(*values):
    return jnp.stack([jnp.asarray(value, jnp.int32) for value in values])


def halves(first, count):
    x, y = place()
    half = count // 2
    me = 2 * y + x
    return (
        (first, half, 1, numbers(1 - x, 3 - x), numbers(2 * (1 - y) + x, 1 - y), numbers(me, y, 0)),
        (first + half, half, 2, numbers(2 - 2 * y, 3 - 2 * y), numbers(2 * y + 1 - x, 1 - x), numbers(me, x, 0)),
    )


def expert_body(gate_pre, up_pre, grad_hidden, gate):
    sigma = jax.nn.sigmoid(gate_pre)
    act = gate_pre * sigma
    hidden = (act * up_pre).astype(BF16).astype(F32)
    grad_gate = jnp.sum(hidden * grad_hidden, axis=-1, keepdims=True)
    scaled = (gate * hidden).astype(BF16)
    grad = gate * grad_hidden
    grad_gate_pre = (grad * up_pre * sigma * (1.0 + gate_pre * (1.0 - sigma))).astype(BF16)
    grad_up_pre = (grad * act).astype(BF16)
    return scaled, grad_gate_pre, grad_up_pre, grad_gate


def neighbours():
    me = lax.axis_index("gx")
    x = me % 2
    y = me // 2
    return x, y, me + 1 - 2 * x, me + 2 - 4 * y


def greet(*others):
    barrier = pltpu.get_barrier_semaphore()
    for other in others:
        pl.semaphore_signal(
            barrier, inc=1, device_id={"gx": other}, device_id_type=pl.DeviceIdType.MESH
        )
    pl.semaphore_wait(barrier, len(others))


def remote(source, target, sent, received, other):
    return pltpu.make_async_remote_copy(
        src_ref=source,
        dst_ref=target,
        send_sem=sent,
        recv_sem=received,
        device_id={"gx": other},
        device_id_type=pl.DeviceIdType.MESH,
    )


def experts_kernel(
    rows,
    w_gate,
    w_up,
    grad_hidden,
    factors,
    own_out,
    x_out,
    y_out,
    d_out,
    hid_out,
    back_out,
    gate_out,
    first_sent,
    first,
    second,
    weights,
    loaded,
    first_send,
    first_recv,
    second_send,
    second_recv,
    x_send,
    x_recv,
    y_send,
    y_recv,
    d_send,
    d_recv,
    own_sem,
    weight_sem,
    load_sem,
):
    x, y, x_other, y_other = neighbours()
    me = 2 * y + x
    across = 3 - me
    pairs = rows.shape[0] // 2
    slots = rows.shape[2]
    greet(x_other, y_other)

    def side(odd):
        if odd:
            return y_other, x_other, (2 - 2 * y, 3 - 2 * y), 2 * y + 1 - x, 1 - x, x
        return x_other, y_other, (1 - x, 3 - x), 2 * (1 - y) + x, 1 - y, y

    def fetch(pair):
        for odd in range(2):
            expert = 2 * pair + odd
            pltpu.make_async_copy(w_gate.at[expert], weights.at[odd, 0], weight_sem.at[odd, 0]).start()
            pltpu.make_async_copy(w_up.at[expert], weights.at[odd, 1], weight_sem.at[odd, 1]).start()

    def fetched(pair, odd):
        expert = 2 * pair + odd
        pltpu.make_async_copy(w_gate.at[expert], weights.at[odd, 0], weight_sem.at[odd, 0]).wait()
        pltpu.make_async_copy(w_up.at[expert], weights.at[odd, 1], weight_sem.at[odd, 1]).wait()

    def first_copy(pair, odd):
        expert = 2 * pair + odd
        return remote(
            first_sent.at[pair % 2, odd],
            first.at[expert],
            first_send.at[expert],
            first_recv.at[expert],
            side(odd)[0],
        )

    def second_copy(pair, odd):
        expert = 2 * pair + odd
        return remote(
            first.at[expert, side(odd)[4]],
            second.at[expert],
            second_send.at[expert],
            second_recv.at[expert],
            side(odd)[1],
        )

    def x_copy(pair, odd):
        expert = 2 * pair + odd
        source = first.at[expert, side(odd)[5]]
        return remote(source, x_out.at[expert], x_send.at[expert], x_recv.at[expert], x_other)

    def y_copy(pair, odd):
        expert = 2 * pair + odd
        source = first.at[expert, side(odd)[5]]
        return remote(source, y_out.at[expert], y_send.at[expert], y_recv.at[expert], y_other)

    def own_copy(pair, odd):
        expert = 2 * pair + odd
        return pltpu.make_async_copy(
            first.at[expert, side(odd)[5]], own_out.at[expert], own_sem.at[expert]
        )

    def far_copy(pair, odd):
        expert = 2 * pair + odd
        source = x_out if odd else y_out
        return remote(
            source.at[expert],
            d_out.at[expert],
            d_send.at[expert],
            d_recv.at[expert],
            side(odd)[0],
        )

    def send_first(pair):
        fetch(pair)
        for odd in range(2):
            expert = 2 * pair + odd

            @pl.when(pair >= 2)
            def _(odd=odd):
                first_copy(pair - 2, odd).wait_send()

            low, high = side(odd)[2]
            source = jnp.concatenate([rows[expert, low], rows[expert, high]], axis=0)
            fetched(pair, odd)
            for number in range(2):
                out = dot(source, weights[odd, number]).astype(BF16)
                first_sent[pair % 2, odd, 0, number] = out[:slots]
                first_sent[pair % 2, odd, 1, number] = out[slots:]
            first_copy(pair, odd).start()

    def send_second(pair):
        fetch(pair)
        for odd in range(2):
            expert = 2 * pair + odd
            _, _, _, quarter, spot, _ = side(odd)
            fetched(pair, odd)
            first_copy(pair, odd).wait_recv()
            for number in range(2):
                out = dot(rows[expert, quarter], weights[odd, number])
                out += first[expert, spot, number].astype(F32)
                first[expert, spot, number] = out.astype(BF16)
            second_copy(pair, odd).start()

    def finish(pair):
        fetch(pair)
        for odd in range(2):
            expert = 2 * pair + odd
            spot = side(odd)[5]
            fetched(pair, odd)
            second_copy(pair, odd).wait_recv()
            scale = factors[expert, :, 1:2]
            source = rows[expert, me]
            gate_pre, up_pre = (
                dot(source, weights[odd, number])
                + first[expert, spot, number].astype(F32)
                + second[expert, number].astype(F32)
                for number in range(2)
            )
            scaled, grad_gate_pre, grad_up_pre, grad_gate = expert_body(
                gate_pre * scale,
                up_pre * scale,
                grad_hidden[expert].astype(F32),
                factors[expert, :, 0:1],
            )
            first[expert, spot, 0] = grad_gate_pre
            first[expert, spot, 1] = grad_up_pre
            x_copy(pair, odd).start()
            y_copy(pair, odd).start()
            own_copy(pair, odd).start()
            hid_out[expert, 0] = scaled
            gate_out[expert] = grad_gate

    def pass_on(pair):
        for odd in range(2):
            (x_copy if odd else y_copy)(pair, odd).wait_recv()
            far_copy(pair, odd).start()

    def load(pair, odd, number):
        expert = 2 * pair + odd
        source = (x_out, y_out, d_out)[number]
        return pltpu.make_async_copy(
            source.at[expert], loaded.at[odd, number], load_sem.at[odd, number]
        )

    def send_back(pair):
        fetch(pair)
        for odd in range(2):
            (y_copy if odd else x_copy)(pair, odd).wait_recv()
            load(pair, odd, 0).start()
            load(pair, odd, 1).start()
        for odd in range(2):
            far_copy(pair, odd).wait_recv()
            load(pair, odd, 2).start()
        for odd in range(2):
            expert = 2 * pair + odd
            fetched(pair, odd)
            for number in range(3):
                load(pair, odd, number).wait()
            spot = side(odd)[5]
            total = None
            for number in range(2):
                source = jnp.concatenate(
                    [first[expert, spot, number]] + [loaded[odd, part, number] for part in range(3)],
                    axis=0,
                )
                part = dot_nt(source, weights[odd, number])
                total = part if total is None else total + part
            total = total.astype(BF16)
            for number, quarter in enumerate((me, x_other, y_other, across)):
                back_out[expert, quarter] = total[number * slots : (number + 1) * slots]

    def step(number, _):
        for lag, stage in enumerate((send_first, send_second, finish, pass_on, send_back)):

            @pl.when((number >= lag) & (number < pairs + lag))
            def _(lag=lag, stage=stage):
                stage(number - lag)

        return 0

    lax.fori_loop(0, pairs + 4, step, 0)

    def drain(pair, _):
        for odd in range(2):

            @pl.when(pair >= pairs - 2)
            def _(odd=odd):
                first_copy(pair, odd).wait_send()

            second_copy(pair, odd).wait_send()
            own_copy(pair, odd).wait()
            x_copy(pair, odd).wait_send()
            y_copy(pair, odd).wait_send()
            far_copy(pair, odd).wait_send()
        return 0

    lax.fori_loop(0, pairs, drain, 0)


def routed_experts(rows, w_gate, w_up, grad_hidden, factors):
    experts, quarters, slots, depth = rows.shape
    width = w_gate.shape[2]
    vmem = pl.BlockSpec(memory_space=pltpu.VMEM)
    anywhere = pl.BlockSpec(memory_space=pl.ANY)
    block = jax.ShapeDtypeStruct((experts, 2, slots, width), BF16)
    dma = pltpu.SemaphoreType.DMA
    return pl.pallas_call(
        experts_kernel,
        in_specs=[vmem, anywhere, anywhere, vmem, vmem],
        out_specs=[anywhere] * 4 + [vmem] * 3,
        out_shape=[block] * 4
        + [
            jax.ShapeDtypeStruct((experts, 1, slots, width), BF16),
            jax.ShapeDtypeStruct((experts, quarters, slots, depth), BF16),
            jax.ShapeDtypeStruct((experts, slots, 1), F32),
        ],
        scratch_shapes=[
            pltpu.VMEM((2, 2, 2, 2, slots, width), BF16),
            pltpu.VMEM((experts, 2, 2, slots, width), BF16),
            pltpu.VMEM((experts, 2, slots, width), BF16),
            pltpu.VMEM((2, 2, depth, width), BF16),
            pltpu.VMEM((2, 3, 2, slots, width), BF16),
        ]
        + [dma((experts,))] * 11
        + [dma((2, 2)), dma((2, 3))],
        compiler_params=pltpu.CompilerParams(
            collective_id=0, has_side_effects=True, vmem_limit_bytes=VMEM_LIMIT
        ),
        cost_estimate=cost(
            12 * experts * quarters * slots * depth * width, 12 * experts * depth * width, 0
        ),
        name="routed_experts",
    )(rows, w_gate, w_up, grad_hidden, factors)


def sum_kernel(base, by_quarter, own_weights, transposed, rows, weight, out, sent, first, second, held, *sems):
    first_send, first_recv, second_send, second_recv, weight_sem = sems
    x, y, x_other, y_other = neighbours()
    me = 2 * y + x
    pairs = sent.shape[0] // 2
    slots = sent.shape[2]
    greet(x_other, y_other)

    def side(odd):
        if odd:
            return y_other, x_other, (2 - 2 * y, 3 - 2 * y), 2 * y + 1 - x, 1 - x, x
        return x_other, y_other, (1 - x, 3 - x), 2 * (1 - y) + x, 1 - y, y

    def source(item, quarter):
        return rows[quarter, item] if by_quarter else rows[base + item, quarter]

    def product(value, item):
        matrix = held[item] if own_weights else weight[...]
        return dot_nt(value, matrix) if transposed else dot(value, matrix)

    def weight_copy(item):
        return pltpu.make_async_copy(weight.at[base + item], held.at[item], weight_sem.at[item])

    def first_copy(item, odd):
        return remote(sent.at[item], first.at[item], first_send.at[item], first_recv.at[item], side(odd)[0])

    def second_copy(item, odd):
        return remote(
            first.at[item, side(odd)[4]],
            second.at[item],
            second_send.at[item],
            second_recv.at[item],
            side(odd)[1],
        )

    def send_first(pair):
        for odd in range(2):
            item = 2 * pair + odd
            low, high = side(odd)[2]
            if own_weights:
                weight_copy(item).wait()
            result = product(jnp.concatenate([source(item, low), source(item, high)], axis=0), item)
            sent[item, 0] = result[:slots].astype(BF16)
            sent[item, 1] = result[slots:].astype(BF16)
            first_copy(item, odd).start()

    def send_second(pair):
        for odd in range(2):
            item = 2 * pair + odd
            _, _, _, quarter, spot, _ = side(odd)
            result = product(source(item, quarter), item)
            first_copy(item, odd).wait_recv()
            first[item, spot] = (result + first[item, spot].astype(F32)).astype(BF16)
            second_copy(item, odd).start()

    def finish(pair):
        for odd in range(2):
            item = 2 * pair + odd
            result = product(source(item, me), item) + first[item, side(odd)[5]].astype(F32)
            second_copy(item, odd).wait_recv()
            out[item] = (result + second[item].astype(F32)).astype(out.dtype)

    def fetch(item, _):
        weight_copy(item).start()
        return 0

    if own_weights:
        lax.fori_loop(0, 2 * pairs, fetch, 0)

    def step(number, _):
        for lag, stage in enumerate((send_first, send_second, finish)):

            @pl.when((number >= lag) & (number < pairs + lag))
            def _(lag=lag, stage=stage):
                stage(number - lag)

        return 0

    lax.fori_loop(0, pairs + 2, step, 0)

    def drain(pair, _):
        for odd in range(2):
            item = 2 * pair + odd
            first_copy(item, odd).wait_send()
            second_copy(item, odd).wait_send()
        return 0

    lax.fori_loop(0, pairs, drain, 0)


def square_sum(rows, weight, base, items, number, transposed, by_quarter, kind):
    slots, depth = rows.shape[2:]
    own_weights = weight.ndim == 3
    width = weight.shape[-2] if transposed else weight.shape[-1]
    vmem = pl.BlockSpec(memory_space=pltpu.VMEM)
    dma = pltpu.SemaphoreType.DMA
    held = (items,) + weight.shape[1:] if own_weights else (8, 128)
    return pl.pallas_call(
        functools.partial(sum_kernel, base, by_quarter, own_weights, transposed),
        in_specs=[vmem, pl.BlockSpec(memory_space=pl.ANY) if own_weights else vmem],
        out_specs=vmem,
        out_shape=jax.ShapeDtypeStruct((items, slots, width), kind),
        scratch_shapes=[
            pltpu.VMEM((items, 2, slots, width), BF16),
            pltpu.VMEM((items, 2, slots, width), BF16),
            pltpu.VMEM((items, slots, width), BF16),
            pltpu.VMEM(held, BF16),
        ]
        + [dma((items,))] * 5,
        compiler_params=pltpu.CompilerParams(
            collective_id=number, has_side_effects=True, vmem_limit_bytes=VMEM_LIMIT
        ),
        cost_estimate=cost(8 * items * slots * depth * width, 2 * items * depth * width, 0),
        name="square_sum",
    )(rows, weight)


def band_total(rows, weight, number, transposed=False):
    if not square():
        whole = (dot_nt(rows, weight) if transposed else dot(rows, weight)).astype(BF16)
        return lax.psum_scatter(whole, "gx", scatter_dimension=0, tiled=True).astype(F32)
    source = rows.reshape(4, 4, rows.shape[0] // 16, rows.shape[1])
    out = square_sum(source, weight, 0, 4, number, transposed, True, F32)
    return out.reshape(-1, out.shape[2])


def hidden_kernel(base, hidden, weight, x_out, y_out, d_out, out, held, loaded, *sems):
    x_send, x_recv, y_send, y_recv, d_send, d_recv, weight_sem, load_sem = sems
    x, y, x_other, y_other = neighbours()
    me = 2 * y + x
    across = 3 - me
    pairs = out.shape[0] // 2
    slots = out.shape[2]
    greet(x_other, y_other)

    def x_copy(item):
        return remote(hidden.at[base + item], x_out.at[item], x_send.at[item], x_recv.at[item], x_other)

    def y_copy(item):
        return remote(hidden.at[base + item], y_out.at[item], y_send.at[item], y_recv.at[item], y_other)

    def far_copy(item, odd):
        source, other = (x_out, y_other) if odd else (y_out, x_other)
        return remote(source.at[item], d_out.at[item], d_send.at[item], d_recv.at[item], other)

    def weight_copy(item, odd):
        return pltpu.make_async_copy(weight.at[base + item], held.at[odd], weight_sem.at[odd])

    def load(item, odd, number):
        source = (hidden.at[base + item], x_out.at[item], y_out.at[item], d_out.at[item])[number]
        return pltpu.make_async_copy(source, loaded.at[odd, number], load_sem.at[odd, number])

    def begin(pair, _):
        for odd in range(2):
            x_copy(2 * pair + odd).start()
            y_copy(2 * pair + odd).start()
        return 0

    def pass_on(pair):
        for odd in range(2):
            item = 2 * pair + odd
            (x_copy if odd else y_copy)(item).wait_recv()
            far_copy(item, odd).start()

    def multiply(pair):
        for odd in range(2):
            item = 2 * pair + odd
            weight_copy(item, odd).start()
            (y_copy if odd else x_copy)(item).wait_recv()
            for number in range(3):
                load(item, odd, number).start()
        for odd in range(2):
            item = 2 * pair + odd
            far_copy(item, odd).wait_recv()
            load(item, odd, 3).start()
        for odd in range(2):
            item = 2 * pair + odd
            weight_copy(item, odd).wait()
            for number in range(4):
                load(item, odd, number).wait()
            source = jnp.concatenate([loaded[odd, number, 0] for number in range(4)], axis=0)
            total = dot(source, held[odd]).astype(BF16)
            for number, quarter in enumerate((me, x_other, y_other, across)):
                out[item, quarter] = total[number * slots : (number + 1) * slots]

    lax.fori_loop(0, pairs, begin, 0)

    def step(number, _):
        for lag, stage in enumerate((pass_on, multiply)):

            @pl.when((number >= lag) & (number < pairs + lag))
            def _(lag=lag, stage=stage):
                stage(number - lag)

        return 0

    lax.fori_loop(0, pairs + 1, step, 0)

    def drain(pair, _):
        for odd in range(2):
            item = 2 * pair + odd
            x_copy(item).wait_send()
            y_copy(item).wait_send()
            far_copy(item, odd).wait_send()
        return 0

    lax.fori_loop(0, pairs, drain, 0)


def hidden_products(hidden, weight, base, items, number):
    slots, width = hidden.shape[2:]
    depth = weight.shape[2]
    anywhere = pl.BlockSpec(memory_space=pl.ANY)
    block = jax.ShapeDtypeStruct((items, 1, slots, width), BF16)
    dma = pltpu.SemaphoreType.DMA
    return pl.pallas_call(
        functools.partial(hidden_kernel, base),
        in_specs=[anywhere, anywhere],
        out_specs=[anywhere] * 3 + [pl.BlockSpec(memory_space=pltpu.VMEM)],
        out_shape=[block] * 3 + [jax.ShapeDtypeStruct((items, 4, slots, depth), BF16)],
        scratch_shapes=[
            pltpu.VMEM((2,) + weight.shape[1:], BF16),
            pltpu.VMEM((2, 4, 1, slots, width), BF16),
        ]
        + [dma((items,))] * 6
        + [dma((2,)), dma((2, 4))],
        compiler_params=pltpu.CompilerParams(
            collective_id=number, has_side_effects=True, vmem_limit_bytes=VMEM_LIMIT
        ),
        cost_estimate=cost(8 * items * slots * depth * width, 2 * items * depth * width, 0),
        name="hidden_products",
    )(hidden, weight)


def group_specs(groups):
    specs, values = [], []
    base = groups[0][0]
    for first, count, blocks in groups:
        for value, start in blocks:

            def index(e, p, low=first - base, top=count - 1, start=start):
                return (jnp.clip(e - low, 0, top) + start, 0, 0, 0)

            specs.append(pl.BlockSpec((1,) + value.shape[1:], index))
            values.append(value)
    return specs, values


def for_group(groups, refs, body):
    base = groups[0][0]
    each = len(groups[0][2])
    if len(groups) == 1:
        body(refs[:each])
        return
    step = pl.program_id(0)
    for number, (first, count, _) in enumerate(groups):
        low = first - base

        @pl.when((step >= low) & (step < low + count))
        def _(number=number):
            body(refs[number * each : (number + 1) * each])


def back_kernel(groups, transposed, picks_ref, *refs):
    terms, slots = groups[0][2][0][1:3]
    out_ref = refs[-1]
    weights = refs[-1 - terms : -1]

    def body(pieces):
        total = None
        for term in range(terms):
            source = jnp.concatenate([ref[0, term] for ref in pieces], axis=0)
            part = dot_nt(source, weights[term][0]) if transposed else dot(source, weights[term][0])
            total = part if total is None else total + part
        total = total.astype(BF16)
        for quarter in range(len(pieces)):
            rows = total[quarter * slots : (quarter + 1) * slots]
            out_ref[0, pl.ds(picks_ref[quarter], 1)] = rows[None]

    for_group(groups, refs, body)


def shapes_of(groups):
    return tuple(
        (first, count, tuple(b.shape for b, _ in blocks))
        for first, count, blocks in groups
    )


def back(groups, picks, weights, transposed):
    first = groups[0][0]
    count = sum(g[1] for g in groups)
    quarters = len(groups[0][2])
    terms, slots, depth = groups[0][2][0][0].shape[1:]
    width = weights[0].shape[1] if transposed else weights[0].shape[2]
    specs, values = group_specs(groups)
    specs += [pl.BlockSpec((1,) + w.shape[1:], lambda e, p: (first + e, 0, 0)) for w in weights]
    return pl.pallas_call(
        functools.partial(back_kernel, shapes_of(groups), transposed),
        grid_spec=pltpu.PrefetchScalarGridSpec(
            num_scalar_prefetch=1,
            grid=(count,),
            in_specs=specs,
            out_specs=pl.BlockSpec((1, quarters, slots, width), lambda e, p: (e, 0, 0, 0)),
        ),
        out_shape=jax.ShapeDtypeStruct((count, quarters, slots, width), BF16),
        compiler_params=params(),
        cost_estimate=cost(
            2 * terms * count * quarters * slots * depth * width,
            2 * terms * count * (quarters * slots + width) * depth,
            2 * count * quarters * slots * width,
        ),
        name="back",
    )(picks, *values, *weights)


def weight_grad_kernel(groups, flip, picks_ref, *refs):
    terms = groups[0][2][0][1]
    quarters = len(groups[0][2])
    outs = refs[-terms:]
    rows = jnp.concatenate([ref[0, 0] for ref in refs[:quarters]], axis=0)

    def body(pieces):
        for term in range(terms):
            others = jnp.concatenate([ref[0, term] for ref in pieces], axis=0)
            outs[term][0] = dot_tn(others, rows) if flip else dot_tn(rows, others)

    for_group(groups, refs[quarters:], body)


def weight_grad(rows, groups, picks, flip):
    first = groups[0][0]
    count = sum(g[1] for g in groups)
    quarters = len(groups[0][2])
    slots, depth = rows.shape[2:]
    terms, _, width = groups[0][2][0][0].shape[1:]
    specs = [
        pl.BlockSpec((1, 1, slots, depth), lambda e, p, q=quarter: (first + e, p[q], 0, 0))
        for quarter in range(quarters)
    ]
    more, values = group_specs(groups)
    shape = (width, depth) if flip else (depth, width)
    return pl.pallas_call(
        functools.partial(weight_grad_kernel, shapes_of(groups), flip),
        grid_spec=pltpu.PrefetchScalarGridSpec(
            num_scalar_prefetch=1,
            grid=(count,),
            in_specs=specs + more,
            out_specs=[pl.BlockSpec((1,) + shape, lambda e, p: (e, 0, 0))] * terms,
        ),
        out_shape=[jax.ShapeDtypeStruct((count,) + shape, F32)] * terms,
        compiler_params=params(),
        cost_estimate=cost(
            2 * terms * count * quarters * slots * depth * width,
            2 * count * quarters * slots * (depth + terms * width),
            4 * terms * count * depth * width,
        ),
        name="weight_grad",
    )(picks, *([rows] * quarters), *values)


def silu(value):
    return value * jax.nn.sigmoid(value)


def silu_grad(value):
    sigma = jax.nn.sigmoid(value)
    return sigma * (1.0 + value * (1.0 - sigma))


def rope_tables(length):
    half = DR // 2
    position = jnp.arange(length).astype(F32)
    inverse = jnp.exp(-math.log(10000.0) * jnp.arange(half).astype(F32) / half)
    angle = position[:, None] * inverse[None, :]
    cosine, sine = jnp.cos(angle), jnp.sin(angle)
    return jnp.concatenate([cosine, cosine], axis=1), jnp.concatenate([-sine, sine], axis=1)


def turn(value, cosine, sine):
    half = DR // 2
    other = jnp.concatenate([value[:, half:], value[:, :half]], axis=1)
    return value * cosine + other * sine


def visible(starts_ref, sequence):
    length = SEQ_LEN
    query = lax.broadcasted_iota(jnp.int32, (length, 1), 0)
    key = lax.broadcasted_iota(jnp.int32, (1, length), 1)
    seen = key <= query
    for number in range(2):
        low = starts_ref[sequence, number]
        seen |= ((query >= low) & (query < low + PIECE)) & ((key >= low) & (key < low + PIECE))
    return seen


def attention_kernel(heads, starts_ref, proj, latent, gain, w_expand, cos, sin, out, logs, q_out, k_out, v_out, n_out):
    scale = (DN + DR) ** (-0.5)
    cosine, sine = cos[...], sin[...]
    lat = latent[...].astype(F32)
    compressed = lat[:, :L]
    root = lax.rsqrt(jnp.mean(compressed * compressed, axis=1, keepdims=True) + EPS)
    normed = (compressed * root * gain[...].astype(F32)).astype(BF16)
    n_out[...] = normed
    key_rope = turn(lat[:, L:], cosine, sine).astype(BF16)
    expanded = dot(normed, w_expand[...]).astype(BF16)
    seen = visible(starts_ref, pl.program_id(0))
    for head in range(heads):
        plain = proj[:, head * DN : (head + 1) * DN].astype(BF16)
        start = heads * DN + head * DR
        query = jnp.concatenate([plain, turn(proj[:, start : start + DR], cosine, sine).astype(BF16)], axis=1)
        start = head * (DN + DV)
        key = jnp.concatenate([expanded[:, start : start + DN], key_rope], axis=1)
        value = expanded[:, start + DN : start + DN + DV]
        q_out[0, head] = query
        k_out[0, head] = key
        v_out[0, head] = value
        scores = jnp.where(seen, dot_nt(query, key) * scale, -1e30)
        peak = jnp.max(scores, axis=1, keepdims=True)
        expo = jnp.exp(scores - peak)
        total = jnp.sum(expo, axis=1, keepdims=True)
        weights = (expo / total).astype(BF16)
        out[:, head * DV : (head + 1) * DV] = dot(weights, value).astype(BF16)
        logs[0, head] = peak + jnp.log(total)


def attention_forward(starts, proj, latent, gain, w_expand, cosine, sine, heads):
    band = proj.shape[0]
    seqs = band // SEQ_LEN

    def rows(width):
        return pl.BlockSpec((SEQ_LEN, width), lambda s, p: (s, 0))

    def whole(shape):
        return pl.BlockSpec(shape, lambda s, p: (0, 0))

    def by_head(width):
        return pl.BlockSpec((1, heads, SEQ_LEN, width), lambda s, p: (s, 0, 0, 0))

    def head_shape(width, kind=BF16):
        return jax.ShapeDtypeStruct((seqs, heads, SEQ_LEN, width), kind)

    return pl.pallas_call(
        functools.partial(attention_kernel, heads),
        grid_spec=pltpu.PrefetchScalarGridSpec(
            num_scalar_prefetch=1,
            grid=(seqs,),
            in_specs=[
                rows(proj.shape[1]),
                rows(L + DR),
                whole((1, L)),
                whole(w_expand.shape),
                whole((SEQ_LEN, DR)),
                whole((SEQ_LEN, DR)),
            ],
            out_specs=[rows(heads * DV), by_head(1), by_head(DN + DR), by_head(DN + DR), by_head(DV), rows(L)],
        ),
        out_shape=[
            jax.ShapeDtypeStruct((band, heads * DV), BF16),
            head_shape(1, F32),
            head_shape(DN + DR),
            head_shape(DN + DR),
            head_shape(DV),
            jax.ShapeDtypeStruct((band, L), BF16),
        ],
        compiler_params=params(),
        name="attention",
    )(starts, proj, latent, gain[None], w_expand, cosine, sine)


def attention_back_kernel(heads, starts_ref, q_ref, k_ref, v_ref, logs, grad, w_expand, cos, sin, dq_out, de_out, dl_out):
    scale = (DN + DR) ** (-0.5)
    cosine, sine = cos[...], -sin[...]
    seen = visible(starts_ref, pl.program_id(0))
    rope = None
    latent = None
    for head in range(heads):
        query, key, value = q_ref[0, head], k_ref[0, head], v_ref[0, head]
        grad_here = grad[:, head * DV : (head + 1) * DV]
        scores = jnp.where(seen, dot_nt(query, key) * scale, -1e30)
        weights = jnp.exp(scores - logs[0, head])
        grad_weights = dot_nt(grad_here, value)
        centre = jnp.sum(weights * grad_weights, axis=1, keepdims=True)
        grad_scores = (weights * (grad_weights - centre)).astype(BF16)
        grad_query = dot(grad_scores, key) * scale
        grad_key = dot_tn(grad_scores, query) * scale
        grad_value = dot_tn(weights.astype(BF16), grad_here)
        dq_out[:, head * DN : (head + 1) * DN] = grad_query[:, :DN].astype(BF16)
        start = heads * DN + head * DR
        dq_out[:, start : start + DR] = turn(grad_query[:, DN:], cosine, sine).astype(BF16)
        part = turn(grad_key[:, DN:], cosine, sine)
        rope = part if rope is None else rope + part
        both = jnp.concatenate([grad_key[:, :DN].astype(BF16), grad_value.astype(BF16)], axis=1)
        start = head * (DN + DV)
        de_out[:, start : start + DN + DV] = both
        part = dot_nt(both, w_expand[:, start : start + DN + DV])
        latent = part if latent is None else latent + part
    dl_out[:, :L] = latent.astype(BF16)
    dl_out[:, L:] = rope.astype(BF16)


def attention_backward(starts, query, key, value, logs, grad, w_expand, cosine, sine):
    seqs, heads = query.shape[:2]
    band = seqs * SEQ_LEN

    def rows(width):
        return pl.BlockSpec((SEQ_LEN, width), lambda s, p: (s, 0))

    def whole(shape):
        return pl.BlockSpec(shape, lambda s, p: (0, 0))

    def by_head(width):
        return pl.BlockSpec((1, heads, SEQ_LEN, width), lambda s, p: (s, 0, 0, 0))

    widths = (heads * (DN + DR), heads * (DN + DV), L + DR)
    return pl.pallas_call(
        functools.partial(attention_back_kernel, heads),
        grid_spec=pltpu.PrefetchScalarGridSpec(
            num_scalar_prefetch=1,
            grid=(seqs,),
            in_specs=[
                by_head(DN + DR),
                by_head(DN + DR),
                by_head(DV),
                by_head(1),
                rows(heads * DV),
                whole(w_expand.shape),
                whole((SEQ_LEN, DR)),
                whole((SEQ_LEN, DR)),
            ],
            out_specs=[rows(width) for width in widths],
        ),
        out_shape=[jax.ShapeDtypeStruct((band, width), BF16) for width in widths],
        compiler_params=params(),
        name="attention_back",
    )(starts, query, key, value, logs, grad, w_expand, cosine, sine)


def norm_backward(value, scale, gain, grad_norm, row_total, width):
    return (
        scale[:, None] * gain * grad_norm - value * (scale**3 / width)[:, None] * row_total[:, None]
    )


def widen(value, width):
    return jnp.pad(value, ((0, 0), (0, width - value.shape[1])))


def up_to(width):
    return 128 * ((width + 127) // 128)


def per_device(
    hidden_in,
    expert_routes,
    piece_starts,
    query_weight,
    latent_weight,
    latent_gain,
    expand_weight,
    output_weight,
    attention_gain,
    ffn_gain,
    router_weight,
    gate_weight,
    up_weight,
    down_weight,
    shared_gate,
    shared_up,
    shared_down,
    grad_out,
):
    row_parts = lax.axis_size("gx")
    column_parts = lax.axis_size("gy")
    here_x = lax.axis_index("gx")
    here_y = lax.axis_index("gy")
    local_rows = hidden_in.shape[0]
    all_tokens = local_rows * column_parts
    band_rows = all_tokens // row_parts
    head_width = query_weight.shape[1]
    heads_here = head_width // (DN + DR)
    latent_width = latent_weight.shape[1]
    experts_here = gate_weight.shape[0]
    shared_width = shared_gate.shape[1]
    cap = 16 * ((local_rows * TOPK * 5 + 64 * EXPERTS - 1) // (64 * EXPERTS))
    blocks = column_parts
    quarter_blocks = blocks // row_parts
    quarter_slots = quarter_blocks * cap
    on_square = square()

    hidden_all = spread_rows(hidden_in)
    hidden = hidden_in.astype(F32)
    grad_top = grad_out.astype(F32)
    wide = up_to(shared_width)
    shared_weight = jnp.concatenate(
        [widen(shared_gate, wide), widen(shared_up, wide), widen(shared_down.T, wide)], axis=1
    )
    scale_one = lax.rsqrt(feature_total(jnp.sum(hidden * hidden, axis=1)) / D + EPS)
    grad_top_tokens = to_tokens(after(grad_out, scale_one))
    shared_weight = collect_rows(after(shared_weight, scale_one))
    sent = jnp.concatenate([expert_routes.T.astype(F32), scale_one[None]], axis=0)
    gathered = lax.all_gather(sent, "gy", axis=1, tiled=True)
    routes_all = gathered[:TOPK].astype(jnp.int32)
    scale_one_all = gathered[TOPK]
    mine = here_y * experts_here + jnp.arange(experts_here, dtype=jnp.int32)
    named = jnp.any(routes_all[:, :, None] == mine[None, None, :], axis=0)
    named_blocks = named.astype(BF16).reshape(blocks, local_rows, experts_here)
    order = jnp.arange(local_rows, dtype=jnp.int32)
    earlier = (order[None, :] < order[:, None]).astype(BF16)
    slot = jnp.einsum("ts,bse->bte", earlier, named_blocks, preferred_element_type=F32)
    code = jnp.where(named, slot.reshape(all_tokens, experts_here), -1.0)
    chosen = one_hot(code, cap, blocks)
    code_here = pick(code.reshape(row_parts, quarter_blocks, local_rows, experts_here), here_x, 0)
    spots = jnp.arange(cap, dtype=jnp.int32).astype(F32)
    at_slot = code_here[:, :, :, None] == spots
    hidden_all = after(hidden_all, chosen, grad_top_tokens)

    norm_one_all = (hidden_all.astype(F32) * scale_one_all[:, None] * attention_gain).astype(BF16)
    by_head = query_weight.reshape(-1, heads_here, DN + DR)
    used = head_width + latent_width
    in_weight = jnp.concatenate(
        [
            by_head[:, :, :DN].reshape(-1, heads_here * DN),
            by_head[:, :, DN:].reshape(-1, heads_here * DR),
            widen(latent_weight, up_to(used) - head_width),
        ],
        axis=1,
    )
    projected = band_total(norm_one_all, in_weight, 1)
    latent_part = projected[:, head_width:used].astype(BF16)
    latent_all = lax.all_gather(latent_part, "gy", axis=1, tiled=True)

    grad_top_all = spread_rows(after(grad_out, hidden_all))
    grad_rows = dispatch(after(chosen, latent_part), grad_top_all, cap, blocks)
    grad_rows = grad_rows.reshape(experts_here, row_parts, quarter_slots, -1)

    if on_square:
        late = experts_here - 2
        grad_hidden_pre = [square_sum(grad_rows, down_weight, 0, 2, 2, True, False, BF16)]
        latent_all = after(latent_all, grad_hidden_pre[0])
    grad_top_band = spread_rows(after(grad_top_tokens, latent_all))

    cosine, sine = rope_tables(SEQ_LEN)
    attended, logs, query_seq, key_seq, value_seq, latent_norm = attention_forward(
        piece_starts, projected, latent_all, latent_gain, expand_weight, cosine, sine, heads_here
    )
    attended_all = collect_rows(attended)
    attended_all = after(attended_all, shared_weight)
    attention_part = dot(attended_all, output_weight).astype(BF16)
    after_attention = hidden + outer_total(attention_part)

    if on_square:
        rows = after(grad_rows, attention_part)
        grad_hidden_pre.append(square_sum(rows, down_weight, 2, late - 2, 3, True, False, BF16))
        after_attention, rows = lax.optimization_barrier((after_attention, rows, grad_hidden_pre[1]))[:2]
        last_steps = halves(late, 2)
        last_sent = [
            group(rows, away, 2, (down_weight,), start, half, True)
            for start, half, bit, away, _, _ in last_steps
        ]
        last_ones = [swap(value, step[2]) for value, step in zip(last_sent, last_steps)]

    gained = (after_attention * ffn_gain).astype(BF16)
    gained_all = spread_rows(gained)
    squares = jnp.sum(after_attention * after_attention, axis=1, keepdims=True)
    logits = dot(after(gained, squares), router_weight)
    totals = square_total(widen(jnp.concatenate([logits, squares], axis=1), 128))
    scale_two = lax.rsqrt(totals[:, EXPERTS] / D + EPS)
    probs = jax.nn.softmax(totals[:, :EXPERTS] * scale_two[:, None], axis=-1)
    norm_two = (after_attention * scale_two[:, None] * ffn_gain).astype(BF16)
    sent = jnp.concatenate(
        [
            probs.reshape(local_rows, column_parts, experts_here),
            jnp.broadcast_to(scale_two[:, None, None], (local_rows, column_parts, 1)),
        ],
        axis=2,
    ).transpose(1, 0, 2)
    received = lax.all_to_all(sent, "gy", split_axis=0, concat_axis=0, tiled=True)
    scale_two_all = received[:, :, experts_here].reshape(all_tokens)
    received = pick(received.reshape(row_parts, quarter_blocks, local_rows, experts_here + 1), here_x, 0)
    factors = jnp.stack(
        [
            jnp.sum(jnp.where(at_slot, value[:, :, :, None], 0.0), axis=1)
            .transpose(1, 0, 2)
            .reshape(experts_here, quarter_slots)
            for value in (received[:, :, :experts_here], received[:, :, experts_here:])
        ],
        axis=2,
    )
    norm_two_tokens = to_tokens(norm_two)
    if on_square:
        rows = after(grad_rows, factors)
        last_twos = [
            swap(group(rows, second, 1, (down_weight,), start, half, True, (one,)), 3 - bit)
            for (start, half, bit, _, second, _), one in zip(last_steps, last_ones)
        ]
        gained_all = after(gained_all, norm_two_tokens)
    rows_two = dispatch(chosen, gained_all, cap, blocks)
    rows_two = rows_two.reshape(experts_here, row_parts, quarter_slots, -1)
    norm_two_band = spread_rows(after(norm_two_tokens, gained_all))

    both_weights = (gate_weight, up_weight)
    if on_square:
        rows = after(grad_rows, rows_two)
        grad_hidden_pre += [
            group(rows, third, 1, (down_weight,), start, half, True, (one, two)).reshape(1, quarter_slots, -1)
            for (start, half, _, _, _, third), one, two in zip(last_steps, last_ones, last_twos)
        ]
        grad_hidden_pre = jnp.concatenate(grad_hidden_pre, axis=0)
        order_of = numbers(here_x, here_x ^ 1, here_x ^ 2, here_x ^ 3)
        own, from_x, from_y, across, scaled, back_rows, slot_grad = routed_experts(
            rows_two, gate_weight, up_weight, grad_hidden_pre, factors
        )
        whole = [(own, 0), (from_x, 0), (from_y, 0), (across, 0)]
        grad_groups = [(0, experts_here, whole)]
    else:
        everything = jnp.arange(row_parts, dtype=jnp.int32)
        order_of = everything

        def whole_total(rows, weight, transposed):
            out = group(rows, everything, row_parts, (weight,), 0, experts_here, transposed)
            out = out.reshape((experts_here,) + out.shape[2:])
            return lax.psum_scatter(out, "gx", scatter_dimension=1, tiled=True)[:, 0].astype(F32)

        scale = factors[:, :, 1:2]
        scaled, grad_gate_pre, grad_up_pre, slot_grad = expert_body(
            whole_total(rows_two, gate_weight, False) * scale,
            whole_total(rows_two, up_weight, False) * scale,
            whole_total(grad_rows, down_weight, True),
            factors[:, :, 0:1],
        )
        grads = jnp.stack([grad_gate_pre, grad_up_pre], axis=1)
        whole = lax.all_gather(grads, "gx", axis=0, tiled=False)
        grad_groups = [(0, experts_here, [(whole[q], 0) for q in range(row_parts)])]
        whole = lax.all_gather(scaled[:, None], "gx", axis=0, tiled=False)
        hidden_groups = [(0, experts_here, [(whole[q], 0) for q in range(row_parts)])]

        back_rows = back(grad_groups, order_of, both_weights, True)

    back_rows = back_rows.reshape(experts_here, blocks * cap, -1)
    grad_norm_part = combine(chosen, [back_rows], cap, blocks)
    grad_norm_routed = outer_total(grad_norm_part)

    shared_gate_all = shared_weight[:, :wide]
    shared_up_all = shared_weight[:, wide : 2 * wide]
    shared_down_all = shared_weight[:, 2 * wide :]
    norm_two_band = after(norm_two_band, grad_norm_part)
    shared_gate_pre = dot(norm_two_band, shared_gate_all)
    shared_up_pre = dot(norm_two_band, shared_up_all)
    shared_hidden = (silu(shared_gate_pre) * shared_up_pre).astype(BF16)
    grad_shared_hidden = dot(grad_top_band, shared_down_all)
    grad_shared_gate_pre = (
        grad_shared_hidden * shared_up_pre * silu_grad(shared_gate_pre)
    ).astype(BF16)
    grad_shared_up_pre = (grad_shared_hidden * silu(shared_gate_pre)).astype(BF16)
    grad_shared_both = jnp.concatenate([grad_shared_gate_pre, grad_shared_up_pre], axis=1)
    grad_shared_part = dot_nt(grad_shared_both, shared_weight[:, : 2 * wide]).astype(BF16)
    grad_norm_shared = outer_total(grad_shared_part)
    grad_shared = dot_tn(after(norm_two_band, grad_shared_part), grad_shared_both).astype(BF16)
    grad_shared = lax.psum_scatter(
        after(grad_shared, grad_norm_shared), "gx", scatter_dimension=0, tiled=True
    ).astype(F32)

    slot_grad = after(slot_grad, grad_norm_part)
    slot_grad = slot_grad.reshape(experts_here, quarter_blocks, cap).transpose(1, 0, 2)
    grad_probs = jnp.sum(jnp.where(at_slot, slot_grad[:, None], 0.0), axis=3)
    grad_probs = grad_probs.reshape(band_rows, experts_here)
    grad_probs = collect(grad_probs.T).transpose(0, 2, 1).reshape(blocks, local_rows, experts_here)
    grad_probs = lax.all_to_all(grad_probs, "gy", split_axis=0, concat_axis=2, tiled=True)
    grad_probs = grad_probs.reshape(local_rows, EXPERTS)
    centre = jnp.sum(probs * grad_probs, axis=1, keepdims=True)
    grad_logits = (probs * (grad_probs - centre)).astype(BF16)
    grad_norm_router = dot_nt(grad_logits, router_weight)
    grad_router_part = dot_tn(norm_two, grad_logits)
    waits = [grad_norm_router]
    if on_square:
        half = experts_here // 2
        hidden_x, hidden_y, hidden_d, out_low = hidden_products(
            after(scaled, grad_shared_part), down_weight, 0, half, 4
        )
        hidden_groups = [(0, half, [(scaled, 0), (hidden_x, 0), (hidden_y, 0), (hidden_d, 0)])]
        waits.append(out_low)
    grad_norm_shared = to_features(grad_norm_shared.astype(BF16)).astype(F32)
    grad_norm_routed = after(grad_norm_routed, *waits)
    grad_norm_two = grad_norm_routed + grad_norm_shared + grad_norm_router

    scaled_after = after_attention * ffn_gain
    row_two = feature_total(jnp.sum(scaled_after * grad_norm_two, axis=1))
    grad_after = grad_top + norm_backward(
        after_attention, scale_two, ffn_gain, grad_norm_two, row_two, D
    )
    grad_ffn_part = jnp.sum(grad_norm_two * after_attention * scale_two[:, None], axis=0)
    grad_after_sent = grad_after.astype(BF16)
    grad_after_all = spread_rows(grad_after_sent)

    if on_square:
        hidden_x, hidden_y, hidden_d, out_high = hidden_products(
            after(scaled, grad_after_sent), down_weight, half, half, 5
        )
        hidden_groups.append((half, half, [(scaled, half), (hidden_x, 0), (hidden_y, 0), (hidden_d, 0)]))
        out = [out_low, out_high]
        grad_after_all = after(grad_after_all, out_high)
    else:
        out = [back(hidden_groups, order_of, (down_weight,), False)]
    out = [value.reshape(value.shape[0], blocks * cap, -1) for value in out]

    grad_attended = band_total(grad_after_all, output_weight, 6, True).astype(BF16)
    shared_hidden_all = collect(after(shared_hidden, grad_attended)).reshape(row_parts, blocks, -1, wide)
    shared_hidden_all = shared_hidden_all.transpose(1, 0, 2, 3).reshape(all_tokens, wide)
    shared_down_wide = jnp.pad(shared_down, ((0, wide - shared_width), (0, 0)))
    shared_out = dot(shared_hidden_all, shared_down_wide).astype(BF16)
    routed_part = combine(chosen, out, cap, blocks, (shared_out,))
    routed = outer_total(routed_part)
    mixed = (after_attention + routed).astype(BF16)
    grad_query_pre, grad_expanded, latent_grads = attention_backward(
        piece_starts, query_seq, key_seq, value_seq, logs, grad_attended, expand_weight, cosine, sine
    )
    latent_sums = lax.psum(latent_grads, "gy").astype(F32)
    norm_two_all = (gained_all.astype(F32) * scale_two_all[:, None]).astype(BF16)
    rows_norm = dispatch(after(chosen, latent_grads), norm_two_all, cap, blocks)
    rows_norm = rows_norm.reshape(experts_here, row_parts, quarter_slots, -1)
    grad_gate, grad_up = weight_grad(rows_norm, grad_groups, order_of, False)
    latent_grads = after(latent_sums, grad_gate, grad_up)
    grad_query_all = collect_rows(grad_query_pre)
    latent_f32 = latent_all.astype(F32)
    compressed = latent_f32[:, :L]
    latent_scale = lax.rsqrt(jnp.mean(compressed * compressed, axis=1) + EPS)
    grad_latent_norm, grad_rope_key = latent_grads[:, :L], latent_grads[:, L:]
    latent_row = jnp.sum(compressed * latent_gain * grad_latent_norm, axis=1)
    grad_compressed = norm_backward(
        compressed, latent_scale, latent_gain, grad_latent_norm, latent_row, L
    )
    grad_gain_part = jnp.sum(grad_latent_norm * compressed * latent_scale[:, None], axis=0)
    grad_latent_pre = jnp.concatenate([grad_compressed, grad_rope_key], axis=1)
    grad_latent_own = lax.dynamic_slice_in_dim(
        grad_latent_pre, here_y * latent_width, latent_width, 1
    ).astype(BF16)
    grad_latent_own = widen(grad_latent_own, up_to(used) - head_width)
    grad_latent_all = collect_rows(grad_latent_own)
    grad_norm_part = (
        dot_nt(grad_query_all, in_weight[:, :head_width])
        + dot_nt(grad_latent_all, in_weight[:, head_width:])
    ).astype(BF16)
    grad_norm_one = outer_total(grad_norm_part)

    norm_one_all = after(norm_one_all, grad_norm_part)
    grad_query = dot_tn(norm_one_all, grad_query_all)
    grad_query = jnp.concatenate(
        [
            grad_query[:, : heads_here * DN].reshape(-1, heads_here, DN),
            grad_query[:, heads_here * DN :].reshape(-1, heads_here, DR),
        ],
        axis=2,
    ).reshape(-1, head_width)
    grad_latent = dot_tn(norm_one_all, grad_latent_all)[:, :latent_width]
    grad_output = dot_tn(attended_all, after(grad_after_all, grad_norm_part))
    (grad_down,) = weight_grad(after(grad_rows, grad_norm_part), hidden_groups, order_of, True)
    grad_expand = square_total(dot_tn(latent_norm, grad_expanded).astype(BF16)).astype(F32)
    grad_shared_down = dot_tn(shared_hidden_all, grad_top_all)[:shared_width]
    pieces = grad_router_part.reshape(column_parts, -1, EXPERTS)
    pieces = lax.all_to_all(pieces, "gy", split_axis=0, concat_axis=0, tiled=True)
    grad_router = lax.all_gather(jnp.sum(pieces, axis=0), "gy", axis=0, tiled=True)
    (
        grad_norm_one,
        grad_query,
        grad_latent,
        grad_output,
        grad_down,
        grad_expand,
        grad_router,
        grad_shared_down,
    ) = lax.optimization_barrier(
        (
            grad_norm_one,
            grad_query,
            grad_latent,
            grad_output,
            grad_down,
            grad_expand,
            grad_router,
            grad_shared_down,
        )
    )
    row_one, grad_latent_gain = feature_total(
        (jnp.sum(hidden * attention_gain * grad_norm_one, axis=1), grad_gain_part)
    )
    grad_hidden = grad_after + norm_backward(
        hidden, scale_one, attention_gain, grad_norm_one, row_one, D
    )
    grad_attention_part = jnp.sum(grad_norm_one * hidden * scale_one[:, None], axis=0)
    grad_attention_gain, grad_ffn_gain = lax.psum((grad_attention_part, grad_ffn_part), "gy")
    grad_shared_gate = grad_shared[:, :shared_width]
    grad_shared_up = grad_shared[:, wide : wide + shared_width]
    return (
        mixed,
        grad_hidden,
        grad_query,
        grad_latent,
        grad_latent_gain,
        grad_expand,
        grad_output,
        grad_attention_gain,
        grad_ffn_gain,
        grad_router,
        grad_gate,
        grad_up,
        grad_down,
        grad_shared_gate,
        grad_shared_up,
        grad_shared_down,
    )


def solution(mesh):
    return jax.shard_map(
        per_device,
        mesh=mesh,
        in_specs=(
            P("gy", "gx"),
            P("gy", None),
            P("gx", None),
            P("gx", "gy"),
            P("gx", "gy"),
            P(),
            P(None, "gy"),
            P("gy", "gx"),
            P("gx"),
            P("gx"),
            P("gx", None),
            P("gy", "gx", None),
            P("gy", "gx", None),
            P("gy", None, "gx"),
            P("gx", "gy"),
            P("gx", "gy"),
            P("gy", "gx"),
            P("gy", "gx"),
        ),
        out_specs=(
            P("gy", "gx"),
            P("gy", "gx"),
            P("gx", "gy"),
            P("gx", "gy"),
            P(),
            P(None, "gy"),
            P("gy", "gx"),
            P("gx"),
            P("gx"),
            P("gx", None),
            P("gy", "gx", None),
            P("gy", "gx", None),
            P("gy", None, "gx"),
            P("gx", "gy"),
            P("gx", "gy"),
            P("gy", "gx"),
        ),
        check_vma=False,
    )
```

```python
import functools
import math

import jax
import jax.numpy as jnp
from jax import lax
from jax.experimental import pallas as pl
from jax.experimental.pallas import tpu as pltpu
from jax.sharding import PartitionSpec as P

D = 2048
DN = 128
DR = 64
DV = 128
L = 512
EXPERTS = 64
FF = 1408
TOPK = 6
SEQ_LEN = 1024
PIECE = 256


EPS = 1e-06
BF16 = jnp.bfloat16
F32 = jnp.float32
VMEM_LIMIT = 56 * 1024 * 1024


def params():
    return pltpu.CompilerParams(vmem_limit_bytes=VMEM_LIMIT)


def cost(microseconds):
    return pl.CostEstimate(flops=int(microseconds * 0.575e9), bytes_accessed=0, transcendentals=0)


waited = []


def after(value, *others):
    value, others = lax.optimization_barrier((value, others))
    waited.extend(jax.tree.leaves(others))
    return value


def together(*values):
    return lax.optimization_barrier(values)


def settle_kernel(value, *refs):
    refs[-1][...] = value[...]


def settle(value):
    vmem = pl.BlockSpec(memory_space=pltpu.VMEM)
    return pl.pallas_call(
        settle_kernel,
        in_specs=[vmem] + [pl.BlockSpec(memory_space=pl.ANY)] * len(waited),
        out_specs=vmem,
        out_shape=jax.ShapeDtypeStruct(value.shape, value.dtype),
        cost_estimate=cost(1),
        name="settle",
    )(value, *waited)


def swap(value, bit):
    return lax.ppermute(value, "gx", [(i, i ^ bit) for i in range(4)])


def square():
    return lax.axis_size("gx") == 4


def place():
    me = lax.axis_index("gx")
    return me & 1, me >> 1


def pick(value, index, axis):
    return lax.dynamic_index_in_dim(value, index, axis, keepdims=False)


def from_others(block):
    half = block.shape[0] // 2
    from_x = swap(block, 1)
    from_y = swap(block, 2)
    return from_x, from_y, swap(from_y[:half], 1), swap(from_x[half:], 2)


def collect(block):
    if not square():
        return lax.all_gather(block, "gx", axis=0, tiled=False)
    return stacked(block, *from_others(block))


def stacked(block, from_x, from_y, low, high):
    across = jnp.concatenate([low, high], axis=0)
    me = lax.axis_index("gx")
    whole = jnp.zeros((4,) + block.shape, block.dtype)
    for index, value in ((me, block), (me ^ 1, from_x), (me ^ 2, from_y), (me ^ 3, across)):
        whole = lax.dynamic_update_index_in_dim(whole, value, index, 0)
    return whole


def collect_rows(block):
    whole = collect(block)
    return whole.reshape((-1,) + block.shape[1:])


def feature_total(value):
    return lax.psum(value, "gx")


def square_total(value):
    if not square():
        return lax.psum(value, "gx")
    value = value + swap(value, 1)
    return value + swap(value, 2)


def inner_rows(value):
    parts = lax.axis_size("gx")
    value = value.reshape(parts, -1, value.shape[1])
    return lax.all_to_all(value, "gx", split_axis=0, concat_axis=0, tiled=True)


def tower_step(value, step):
    size, bit = lax.axis_size("gy"), 2**step
    if bit >= size:
        return value
    return value + lax.ppermute(value, "gy", [(i, i ^ bit) for i in range(size)])


def spread_rows(value):
    return lax.all_gather(value, "gy", axis=0, tiled=True)


def outer_total(partial):
    return lax.psum_scatter(partial.astype(BF16), "gy", scatter_dimension=0, tiled=True)


def to_tokens(value):
    return lax.all_to_all(value, "gx", split_axis=0, concat_axis=1, tiled=True)


def to_features(value):
    return lax.all_to_all(value, "gx", split_axis=1, concat_axis=0, tiled=True)


def dot(a, b):
    return jnp.dot(a, b, preferred_element_type=F32)


def dot_nt(a, b):
    return lax.dot_general(a, b, (((1,), (1,)), ((), ())), preferred_element_type=F32)


def dot_tn(a, b):
    return lax.dot_general(a, b, (((0,), (0,)), ((), ())), preferred_element_type=F32)


def one_hot_kernel(cap, code_ref, out_ref):
    experts = code_ref.shape[1]
    tokens, slots = out_ref.shape
    column = lax.broadcasted_iota(jnp.int32, (experts, slots), 1)
    low = lax.broadcasted_iota(jnp.int32, (experts, slots), 0) * cap
    inside = (column >= low) & (column < low + cap)
    expand = jnp.where(inside, 1.0, 0.0).astype(BF16)
    offset = jnp.sum(jnp.where(inside, column - low, 0).astype(F32), axis=0, keepdims=True)
    wide = dot(code_ref[...].astype(BF16), expand)
    out_ref[...] = jnp.where(wide == offset, 1.0, 0.0).astype(BF16)


def one_hot(code, cap, blocks):
    tokens, experts = code.shape
    block = tokens // blocks
    return pl.pallas_call(
        functools.partial(one_hot_kernel, cap),
        grid=(blocks,),
        in_specs=[pl.BlockSpec((block, experts), lambda b: (b, 0))],
        out_specs=pl.BlockSpec((block, experts * cap), lambda b: (b, 0)),
        out_shape=jax.ShapeDtypeStruct((tokens, experts * cap), BF16),
        compiler_params=params(),
        cost_estimate=cost(7),
        name="one_hot",
    )(code)


def dispatch_kernel(chosen_ref, rows_ref, out_ref):
    moved = dot_tn(chosen_ref[...], rows_ref[...]).astype(BF16)
    out_ref[...] = moved.reshape(out_ref.shape)


def dispatch_scaled_kernel(chosen_ref, rows_ref, scale_ref, out_ref, scale_out_ref):
    dispatch_kernel(chosen_ref, rows_ref, out_ref)
    high, middle, low = thirds(scale_ref[...])
    parts = jnp.concatenate([high, middle, low], axis=1)
    moved = dot_tn(chosen_ref[...], parts)
    moved = moved[:, 0:1] + moved[:, 1:2] + moved[:, 2:3]
    scale_out_ref[...] = moved.reshape(scale_out_ref.shape)


def thirds(value):
    high = value.astype(BF16)
    rest = value - high.astype(F32)
    middle = rest.astype(BF16)
    return high, middle, (rest - middle.astype(F32)).astype(BF16)


def dispatch(chosen, rows, cap, blocks, scale=None):
    tokens, width = rows.shape
    slots = chosen.shape[1]
    experts = slots // cap
    block = tokens // blocks
    specs = [
        pl.BlockSpec((block, slots), lambda b: (b, 0)),
        pl.BlockSpec((block, width), lambda b: (b, 0)),
    ]
    out_specs = [pl.BlockSpec((experts, cap, width), lambda b: (0, b, 0))]
    shapes = [jax.ShapeDtypeStruct((experts, blocks * cap, width), BF16)]
    values = [chosen, rows]
    if scale is not None:
        specs.append(pl.BlockSpec((block, 1), lambda b: (b, 0)))
        out_specs.append(pl.BlockSpec((experts, cap, 1), lambda b: (0, b, 0)))
        shapes.append(jax.ShapeDtypeStruct((experts, blocks * cap, 1), F32))
        values.append(scale)
    outs = pl.pallas_call(
        dispatch_kernel if scale is None else dispatch_scaled_kernel,
        grid=(blocks,),
        in_specs=specs,
        out_specs=out_specs,
        out_shape=shapes,
        compiler_params=params(),
        cost_estimate=cost(10),
        name="dispatch",
    )(*values)
    return outs[0] if scale is None else outs


def combine_kernel(groups, chosen_ref, *refs):
    out_ref = refs[-1]
    width = out_ref.shape[1]
    pieces = [ref[...].reshape(-1, width) for ref in refs[:groups]]
    slots = pieces[0] if groups == 1 else jnp.concatenate(pieces, axis=0)
    total = dot(chosen_ref[...], slots)
    for ref in refs[groups:-1]:
        total += ref[...].astype(F32)
    out_ref[...] = total.astype(out_ref.dtype)


def combine(chosen, pieces, cap, blocks, extra=()):
    tokens, slots = chosen.shape
    block = tokens // blocks
    width = pieces[0].shape[-1]
    specs = [pl.BlockSpec((block, slots), lambda b: (b, 0))]
    specs += [pl.BlockSpec((p.shape[0], cap, width), lambda b: (0, b, 0)) for p in pieces]
    specs += [pl.BlockSpec((block, width), lambda b: (b, 0)) for _ in extra]
    return pl.pallas_call(
        functools.partial(combine_kernel, len(pieces)),
        grid=(blocks,),
        in_specs=specs,
        out_specs=pl.BlockSpec((block, width), lambda b: (b, 0)),
        out_shape=jax.ShapeDtypeStruct((tokens, width), BF16),
        compiler_params=params(),
        cost_estimate=cost(9),
        name="combine",
    )(chosen, *pieces, *extra)


def group_kernel(parts, weights, adds, transposed, picks_ref, *refs):
    rows = [ref[0, 0] for ref in refs[:parts]]
    source = rows[0] if parts == 1 else jnp.concatenate(rows, axis=0)
    out_ref = refs[-1]
    extra = refs[parts + weights : parts + weights + adds]
    for number in range(weights):
        weight = refs[parts + number][0]
        total = dot_nt(source, weight) if transposed else dot(source, weight)
        for ref in extra:
            total += ref[0, number, 0].astype(F32)
        out_ref[0, number] = total.astype(out_ref.dtype).reshape(out_ref.shape[2:])


def group(rows, picks, parts, weights, first, count, transposed=False, adds=(), kind=BF16, by_quarter=False):
    slots, depth = rows.shape[2:]
    width = weights[0].shape[1] if transposed else weights[0].shape[2]
    many = len(weights)

    def row_spec(part):
        if by_quarter:
            return pl.BlockSpec((1, 1, slots, depth), lambda e, p: (p[part], first + e, 0, 0))
        return pl.BlockSpec((1, 1, slots, depth), lambda e, p: (first + e, p[part], 0, 0))

    def add_spec(number):
        return pl.BlockSpec((1, many, 1, slots, width), lambda e, p: (e, 0, p[parts + number], 0, 0))

    specs = [row_spec(part) for part in range(parts)]
    for weight in weights:
        if by_quarter:
            specs.append(pl.BlockSpec((1,) + weight.shape[1:], lambda e, p: (0, 0, 0)))
        else:
            specs.append(pl.BlockSpec((1,) + weight.shape[1:], lambda e, p: (first + e, 0, 0)))
    specs += [add_spec(number) for number in range(len(adds))]
    return pl.pallas_call(
        functools.partial(group_kernel, parts, many, len(adds), transposed),
        grid_spec=pltpu.PrefetchScalarGridSpec(
            num_scalar_prefetch=1,
            grid=(count,),
            in_specs=specs,
            out_specs=pl.BlockSpec((1, many, parts, slots, width), lambda e, p: (e, 0, 0, 0, 0)),
        ),
        out_shape=jax.ShapeDtypeStruct((count, many, parts, slots, width), kind),
        compiler_params=params(),
        cost_estimate=cost(4),
        name="group",
    )(picks, *([rows] * parts), *weights, *adds)


def numbers(*values):
    return jnp.stack([jnp.asarray(value, jnp.int32) for value in values])


def halves(first, count):
    x, y = place()
    half = count // 2
    me = 2 * y + x
    return (
        (first, half, 1, numbers(1 - x, 3 - x), numbers(2 * (1 - y) + x, 1 - y), numbers(me, y, 0)),
        (first + half, half, 2, numbers(2 - 2 * y, 3 - 2 * y), numbers(2 * y + 1 - x, 1 - x), numbers(me, x, 0)),
    )


def expert_body(gate_pre, up_pre, grad_hidden, gate):
    sigma = jax.nn.sigmoid(gate_pre)
    act = gate_pre * sigma
    hidden = (act * up_pre).astype(BF16).astype(F32)
    grad_gate = jnp.sum(hidden * grad_hidden, axis=-1, keepdims=True)
    scaled = (gate * hidden).astype(BF16)
    grad = gate * grad_hidden
    grad_gate_pre = (grad * up_pre * sigma * (1.0 + gate_pre * (1.0 - sigma))).astype(BF16)
    grad_up_pre = (grad * act).astype(BF16)
    return scaled, grad_gate_pre, grad_up_pre, grad_gate


def neighbours():
    me = lax.axis_index("gx")
    x = me % 2
    y = me // 2
    return x, y, me + 1 - 2 * x, me + 2 - 4 * y


def greet(*others):
    barrier = pltpu.get_barrier_semaphore()
    for other in others:
        pl.semaphore_signal(
            barrier, inc=1, device_id={"gx": other}, device_id_type=pl.DeviceIdType.MESH
        )
    pl.semaphore_wait(barrier, len(others))


def remote(source, target, sent, received, other):
    return pltpu.make_async_remote_copy(
        src_ref=source,
        dst_ref=target,
        send_sem=sent,
        recv_sem=received,
        device_id={"gx": other},
        device_id_type=pl.DeviceIdType.MESH,
    )


def experts_kernel(
    rows,
    w_gate,
    w_up,
    grad_low,
    grad_high,
    factors,
    own_out,
    x_out,
    y_out,
    d_out,
    hid_out,
    back_out,
    gate_out,
    first_sent,
    first,
    second,
    weights,
    loaded,
    first_send,
    first_recv,
    second_send,
    second_recv,
    x_send,
    x_recv,
    y_send,
    y_recv,
    d_send,
    d_recv,
    own_sem,
    weight_sem,
    load_sem,
):
    x, y, x_other, y_other = neighbours()
    me = 2 * y + x
    across = 3 - me
    pairs = rows.shape[0] // 2
    slots = rows.shape[2]
    greet(x_other, y_other)

    def side(odd):
        if odd:
            return y_other, x_other, (2 - 2 * y, 3 - 2 * y), 2 * y + 1 - x, 1 - x, x
        return x_other, y_other, (1 - x, 3 - x), 2 * (1 - y) + x, 1 - y, y

    def fetch(pair):
        for odd in range(2):
            expert = 2 * pair + odd
            pltpu.make_async_copy(w_gate.at[expert], weights.at[odd, 0], weight_sem.at[odd, 0]).start()
            pltpu.make_async_copy(w_up.at[expert], weights.at[odd, 1], weight_sem.at[odd, 1]).start()

    def fetched(pair, odd):
        expert = 2 * pair + odd
        pltpu.make_async_copy(w_gate.at[expert], weights.at[odd, 0], weight_sem.at[odd, 0]).wait()
        pltpu.make_async_copy(w_up.at[expert], weights.at[odd, 1], weight_sem.at[odd, 1]).wait()

    def first_copy(pair, odd):
        expert = 2 * pair + odd
        return remote(
            first_sent.at[pair % 2, odd],
            first.at[expert],
            first_send.at[expert],
            first_recv.at[expert],
            side(odd)[0],
        )

    def second_copy(pair, odd):
        expert = 2 * pair + odd
        return remote(
            first.at[expert, side(odd)[4]],
            second.at[expert],
            second_send.at[expert],
            second_recv.at[expert],
            side(odd)[1],
        )

    def x_copy(pair, odd):
        expert = 2 * pair + odd
        source = first.at[expert, side(odd)[5]]
        return remote(source, x_out.at[expert], x_send.at[expert], x_recv.at[expert], x_other)

    def y_copy(pair, odd):
        expert = 2 * pair + odd
        source = first.at[expert, side(odd)[5]]
        return remote(source, y_out.at[expert], y_send.at[expert], y_recv.at[expert], y_other)

    def own_copy(pair, odd):
        expert = 2 * pair + odd
        return pltpu.make_async_copy(
            first.at[expert, side(odd)[5]], own_out.at[expert], own_sem.at[expert]
        )

    def far_copy(pair, odd):
        expert = 2 * pair + odd
        source = x_out if odd else y_out
        return remote(
            source.at[expert],
            d_out.at[expert],
            d_send.at[expert],
            d_recv.at[expert],
            side(odd)[0],
        )

    def send_first(pair):
        fetch(pair)
        for odd in range(2):
            expert = 2 * pair + odd

            @pl.when(pair >= 2)
            def _(odd=odd):
                first_copy(pair - 2, odd).wait_send()

            low, high = side(odd)[2]
            source = jnp.concatenate([rows[expert, low], rows[expert, high]], axis=0)
            fetched(pair, odd)
            for number in range(2):
                out = dot(source, weights[odd, number]).astype(BF16)
                first_sent[pair % 2, odd, 0, number] = out[:slots]
                first_sent[pair % 2, odd, 1, number] = out[slots:]
            first_copy(pair, odd).start()

    def send_second(pair):
        fetch(pair)
        for odd in range(2):
            expert = 2 * pair + odd
            _, _, _, quarter, spot, _ = side(odd)
            fetched(pair, odd)
            first_copy(pair, odd).wait_recv()
            for number in range(2):
                out = dot(rows[expert, quarter], weights[odd, number])
                out += first[expert, spot, number].astype(F32)
                first[expert, spot, number] = out.astype(BF16)
            second_copy(pair, odd).start()

    def hidden_gradient(expert):
        half = grad_low.shape[0]
        low = grad_low[jnp.minimum(expert, half - 1)].astype(F32)
        high = grad_high[jnp.maximum(expert - half, 0)].astype(F32)
        return jnp.where(expert < half, low, high)

    def finish(pair):
        fetch(pair)
        for odd in range(2):
            expert = 2 * pair + odd
            spot = side(odd)[5]
            fetched(pair, odd)
            second_copy(pair, odd).wait_recv()
            scale = factors[expert, :, 1:2]
            source = rows[expert, me]
            gate_pre, up_pre = (
                dot(source, weights[odd, number])
                + first[expert, spot, number].astype(F32)
                + second[expert, number].astype(F32)
                for number in range(2)
            )
            scaled, grad_gate_pre, grad_up_pre, grad_gate = expert_body(
                gate_pre * scale,
                up_pre * scale,
                hidden_gradient(expert),
                factors[expert, :, 0:1],
            )
            first[expert, spot, 0] = grad_gate_pre
            first[expert, spot, 1] = grad_up_pre
            x_copy(pair, odd).start()
            y_copy(pair, odd).start()
            own_copy(pair, odd).start()
            hid_out[expert, 0] = scaled
            gate_out[expert] = grad_gate

    def pass_on(pair):
        for odd in range(2):
            (x_copy if odd else y_copy)(pair, odd).wait_recv()
            far_copy(pair, odd).start()

    def load(pair, odd, number):
        expert = 2 * pair + odd
        source = (x_out, y_out, d_out)[number]
        return pltpu.make_async_copy(
            source.at[expert], loaded.at[odd, number], load_sem.at[odd, number]
        )

    def send_back(pair):
        fetch(pair)
        for odd in range(2):
            (y_copy if odd else x_copy)(pair, odd).wait_recv()
            load(pair, odd, 0).start()
            load(pair, odd, 1).start()
        for odd in range(2):
            far_copy(pair, odd).wait_recv()
            load(pair, odd, 2).start()
        for odd in range(2):
            expert = 2 * pair + odd
            fetched(pair, odd)
            for number in range(3):
                load(pair, odd, number).wait()
            spot = side(odd)[5]
            total = None
            for number in range(2):
                source = jnp.concatenate(
                    [first[expert, spot, number]] + [loaded[odd, part, number] for part in range(3)],
                    axis=0,
                )
                part = dot_nt(source, weights[odd, number])
                total = part if total is None else total + part
            total = total.astype(BF16)
            for number, quarter in enumerate((me, x_other, y_other, across)):
                back_out[expert, quarter] = total[number * slots : (number + 1) * slots]

    def step(number, _):
        for lag, stage in enumerate((send_first, send_second, finish, pass_on, send_back)):

            @pl.when((number >= lag) & (number < pairs + lag))
            def _(lag=lag, stage=stage):
                stage(number - lag)

        return 0

    lax.fori_loop(0, pairs + 4, step, 0)

    def drain(pair, _):
        for odd in range(2):

            @pl.when(pair >= pairs - 2)
            def _(odd=odd):
                first_copy(pair, odd).wait_send()

            second_copy(pair, odd).wait_send()
            own_copy(pair, odd).wait()
            x_copy(pair, odd).wait_send()
            y_copy(pair, odd).wait_send()
            far_copy(pair, odd).wait_send()
        return 0

    lax.fori_loop(0, pairs, drain, 0)


def routed_experts(rows, w_gate, w_up, grad_low, grad_high, factors):
    experts, quarters, slots, depth = rows.shape
    width = w_gate.shape[2]
    vmem = pl.BlockSpec(memory_space=pltpu.VMEM)
    anywhere = pl.BlockSpec(memory_space=pl.ANY)
    block = jax.ShapeDtypeStruct((experts, 2, slots, width), BF16)
    dma = pltpu.SemaphoreType.DMA
    return pl.pallas_call(
        experts_kernel,
        in_specs=[vmem, anywhere, anywhere, vmem, vmem, vmem],
        out_specs=[anywhere] * 4 + [vmem] * 3,
        out_shape=[block] * 4
        + [
            jax.ShapeDtypeStruct((experts, 1, slots, width), BF16),
            jax.ShapeDtypeStruct((experts, quarters, slots, depth), BF16),
            jax.ShapeDtypeStruct((experts, slots, 1), F32),
        ],
        scratch_shapes=[
            pltpu.VMEM((2, 2, 2, 2, slots, width), BF16),
            pltpu.VMEM((experts, 2, 2, slots, width), BF16),
            pltpu.VMEM((experts, 2, slots, width), BF16),
            pltpu.VMEM((2, 2, depth, width), BF16),
            pltpu.VMEM((2, 3, 2, slots, width), BF16),
        ]
        + [dma((experts,))] * 11
        + [dma((2, 2)), dma((2, 3))],
        compiler_params=pltpu.CompilerParams(
            collective_id=0, has_side_effects=True, vmem_limit_bytes=VMEM_LIMIT
        ),
        cost_estimate=cost(390),
        name="routed_experts",
    )(rows, w_gate, w_up, grad_low, grad_high, factors)


def sum_kernel(base, by_quarter, own_weights, transposed, rows, weight, out, sent, first, second, held, *sems):
    first_send, first_recv, second_send, second_recv, weight_sem = sems
    x, y, x_other, y_other = neighbours()
    me = 2 * y + x
    pairs = sent.shape[0] // 2
    slots = sent.shape[2]
    greet(x_other, y_other)

    def side(odd):
        if odd:
            return y_other, x_other, (2 - 2 * y, 3 - 2 * y), 2 * y + 1 - x, 1 - x, x
        return x_other, y_other, (1 - x, 3 - x), 2 * (1 - y) + x, 1 - y, y

    def source(item, quarter):
        return rows[quarter, item] if by_quarter else rows[base + item, quarter]

    def product(value, item):
        matrix = held[item] if own_weights else weight[...]
        return dot_nt(value, matrix) if transposed else dot(value, matrix)

    def weight_copy(item):
        return pltpu.make_async_copy(weight.at[base + item], held.at[item], weight_sem.at[item])

    def first_copy(item, odd):
        return remote(sent.at[item], first.at[item], first_send.at[item], first_recv.at[item], side(odd)[0])

    def second_copy(item, odd):
        return remote(
            first.at[item, side(odd)[4]],
            second.at[item],
            second_send.at[item],
            second_recv.at[item],
            side(odd)[1],
        )

    def send_first(pair):
        for odd in range(2):
            item = 2 * pair + odd
            low, high = side(odd)[2]
            if own_weights:
                weight_copy(item).wait()
            result = product(jnp.concatenate([source(item, low), source(item, high)], axis=0), item)
            sent[item, 0] = result[:slots].astype(BF16)
            sent[item, 1] = result[slots:].astype(BF16)
            first_copy(item, odd).start()

    def send_second(pair):
        for odd in range(2):
            item = 2 * pair + odd
            _, _, _, quarter, spot, _ = side(odd)
            result = product(source(item, quarter), item)
            first_copy(item, odd).wait_recv()
            first[item, spot] = (result + first[item, spot].astype(F32)).astype(BF16)
            second_copy(item, odd).start()

    def finish(pair):
        for odd in range(2):
            item = 2 * pair + odd
            result = product(source(item, me), item) + first[item, side(odd)[5]].astype(F32)
            second_copy(item, odd).wait_recv()
            out[item] = (result + second[item].astype(F32)).astype(out.dtype)

    def fetch(item, _):
        weight_copy(item).start()
        return 0

    if own_weights:
        lax.fori_loop(0, 2 * pairs, fetch, 0)

    def step(number, _):
        for lag, stage in enumerate((send_first, send_second, finish)):

            @pl.when((number >= lag) & (number < pairs + lag))
            def _(lag=lag, stage=stage):
                stage(number - lag)

        return 0

    lax.fori_loop(0, pairs + 2, step, 0)

    def drain(pair, _):
        for odd in range(2):
            item = 2 * pair + odd
            first_copy(item, odd).wait_send()
            second_copy(item, odd).wait_send()
        return 0

    lax.fori_loop(0, pairs, drain, 0)


def square_sum(rows, weight, base, items, number, transposed, by_quarter, kind):
    slots, depth = rows.shape[2:]
    own_weights = weight.ndim == 3
    width = weight.shape[-2] if transposed else weight.shape[-1]
    vmem = pl.BlockSpec(memory_space=pltpu.VMEM)
    dma = pltpu.SemaphoreType.DMA
    held = (items,) + weight.shape[1:] if own_weights else (8, 128)
    return pl.pallas_call(
        functools.partial(sum_kernel, base, by_quarter, own_weights, transposed),
        in_specs=[vmem, pl.BlockSpec(memory_space=pl.ANY) if own_weights else vmem],
        out_specs=vmem,
        out_shape=jax.ShapeDtypeStruct((items, slots, width), kind),
        scratch_shapes=[
            pltpu.VMEM((items, 2, slots, width), BF16),
            pltpu.VMEM((items, 2, slots, width), BF16),
            pltpu.VMEM((items, slots, width), BF16),
            pltpu.VMEM(held, BF16),
        ]
        + [dma((items,))] * 5,
        compiler_params=pltpu.CompilerParams(
            collective_id=number, has_side_effects=True, vmem_limit_bytes=VMEM_LIMIT
        ),
        cost_estimate=cost(13.5 * items if own_weights else 20 + 25 * width // 512),
        name="square_sum",
    )(rows, weight)


def band_total(rows, weight, number, transposed=False, kind=F32):
    if not square():
        whole = (dot_nt(rows, weight) if transposed else dot(rows, weight)).astype(BF16)
        return lax.psum_scatter(whole, "gx", scatter_dimension=0, tiled=True).astype(kind)
    source = rows.reshape(4, 4, rows.shape[0] // 16, rows.shape[1])
    out = square_sum(source, weight, 0, 4, number, transposed, True, kind)
    return out.reshape(-1, out.shape[2])


def small_kernel(both, inner_ref, outer_ref, inner_out, outer_out, inner_land, outer_land, send, recv, far_send, far_recv):
    x, y, x_other, y_other = neighbours()
    me = 2 * y + x
    peers = (x_other, y_other, 3 - me)
    here = lax.axis_index("gy")
    size = outer_land.shape[0]
    barrier = pltpu.get_barrier_semaphore()
    for other in peers:
        pl.semaphore_signal(barrier, inc=1, device_id={"gx": other}, device_id_type=pl.DeviceIdType.MESH)
    for step in range(1, size if both else 1):
        pl.semaphore_signal(
            barrier, inc=1, device_id={"gy": (here + step) % size}, device_id_type=pl.DeviceIdType.MESH
        )
    pl.semaphore_wait(barrier, 3 + (size - 1 if both else 0))

    inner_land[me] = inner_ref[...]

    def inner_copy(number):
        return remote(inner_ref, inner_land.at[me], send.at[number], recv.at[number], peers[number])

    for number in range(3):
        inner_copy(number).start()
    for number in range(3):
        inner_copy(number).wait()
    total = inner_land[0]
    for number in range(1, 4):
        total = total + inner_land[number]
    inner_out[...] = total
    if not both:
        outer_out[...] = outer_ref[...]
        return
    outer_land[here, 0:8] = outer_ref[...]
    outer_land[here, 8:16] = total

    def outer_copy(step):
        return pltpu.make_async_remote_copy(
            src_ref=outer_land.at[here],
            dst_ref=outer_land.at[here],
            send_sem=far_send.at[step - 1],
            recv_sem=far_recv.at[step - 1],
            device_id={"gy": (here + step) % size},
            device_id_type=pl.DeviceIdType.MESH,
        )

    for step in range(1, size):
        outer_copy(step).start()
    for step in range(1, size):
        outer_copy(step).wait()
    total = outer_land[0]
    for number in range(1, size):
        total = total + outer_land[number]
    outer_out[...] = total


def small_totals(inner, outer, number):
    both = outer is not None
    size = lax.axis_size("gy")
    dma = pltpu.SemaphoreType.DMA
    vmem = pl.BlockSpec(memory_space=pltpu.VMEM)
    return pl.pallas_call(
        functools.partial(small_kernel, both),
        in_specs=[vmem, vmem],
        out_specs=[vmem, vmem],
        out_shape=[
            jax.ShapeDtypeStruct((8, 128), F32),
            jax.ShapeDtypeStruct((16, 128) if both else (8, 128), F32),
        ],
        scratch_shapes=[
            pltpu.VMEM((4, 8, 128), F32),
            pltpu.VMEM((size, 16, 128), F32),
            dma((3,)),
            dma((3,)),
            dma((size - 1,)),
            dma((size - 1,)),
        ],
        compiler_params=pltpu.CompilerParams(
            collective_id=number, has_side_effects=True, vmem_limit_bytes=VMEM_LIMIT
        ),
        cost_estimate=cost(6),
        name="small_totals",
    )(inner, outer if both else jnp.zeros((8, 128), F32))


def shared_sums_kernel(parts, gate, up, down):
    width = gate.shape[0]
    wide = parts.shape[2] // 3
    total = parts[0].astype(F32)
    for number in range(1, parts.shape[0]):
        total = total + parts[number].astype(F32)
    total = total.T
    gate[...] = total[:width]
    up[...] = total[wide : wide + width]
    down[...] = total[2 * wide : 2 * wide + width]


def shared_sums(parts, width):
    rows = parts.shape[1]
    block = 128
    many = parts.shape[0]
    return pl.pallas_call(
        shared_sums_kernel,
        grid=(rows // block,),
        in_specs=[pl.BlockSpec((many, block, parts.shape[2]), lambda i: (0, i, 0))],
        out_specs=[pl.BlockSpec((width, block), lambda i: (0, i))] * 3,
        out_shape=[jax.ShapeDtypeStruct((width, rows), F32)] * 3,
        compiler_params=params(),
        cost_estimate=cost(5),
        name="shared_sums",
    )(parts)


def group_specs(groups):
    specs, values = [], []
    base = groups[0][0]
    for first, count, blocks in groups:
        for value, start in blocks:

            def index(e, p, low=first - base, top=count - 1, start=start):
                return (jnp.clip(e - low, 0, top) + start, 0, 0, 0)

            specs.append(pl.BlockSpec((1,) + value.shape[1:], index))
            values.append(value)
    return specs, values


def for_group(groups, refs, body):
    base = groups[0][0]
    each = len(groups[0][2])
    if len(groups) == 1:
        body(refs[:each])
        return
    step = pl.program_id(0)
    for number, (first, count, _) in enumerate(groups):
        low = first - base

        @pl.when((step >= low) & (step < low + count))
        def _(number=number):
            body(refs[number * each : (number + 1) * each])


def back_kernel(groups, transposed, picks_ref, *refs):
    terms, slots = groups[0][2][0][1:3]
    out_ref = refs[-1]
    weights = refs[-1 - terms : -1]

    def body(pieces):
        total = None
        for term in range(terms):
            source = jnp.concatenate([ref[0, term] for ref in pieces], axis=0)
            part = dot_nt(source, weights[term][0]) if transposed else dot(source, weights[term][0])
            total = part if total is None else total + part
        total = total.astype(BF16)
        for quarter in range(len(pieces)):
            rows = total[quarter * slots : (quarter + 1) * slots]
            out_ref[0, pl.ds(picks_ref[quarter], 1)] = rows[None]

    for_group(groups, refs, body)


def shapes_of(groups):
    return tuple(
        (first, count, tuple(b.shape for b, _ in blocks))
        for first, count, blocks in groups
    )


def back(groups, picks, weights, transposed):
    first = groups[0][0]
    count = sum(g[1] for g in groups)
    quarters = len(groups[0][2])
    terms, slots, depth = groups[0][2][0][0].shape[1:]
    width = weights[0].shape[1] if transposed else weights[0].shape[2]
    specs, values = group_specs(groups)
    specs += [pl.BlockSpec((1,) + w.shape[1:], lambda e, p: (first + e, 0, 0)) for w in weights]
    return pl.pallas_call(
        functools.partial(back_kernel, shapes_of(groups), transposed),
        grid_spec=pltpu.PrefetchScalarGridSpec(
            num_scalar_prefetch=1,
            grid=(count,),
            in_specs=specs,
            out_specs=pl.BlockSpec((1, quarters, slots, width), lambda e, p: (e, 0, 0, 0)),
        ),
        out_shape=jax.ShapeDtypeStruct((count, quarters, slots, width), BF16),
        compiler_params=params(),
        cost_estimate=cost(4 * count),
        name="back",
    )(picks, *values, *weights)


def weight_grad_kernel(groups, flip, scaled, picks_ref, *refs):
    terms = groups[0][2][0][1]
    quarters = len(groups[0][2])
    outs = refs[-terms:]
    rows = [ref[0, 0] for ref in refs[:quarters]]
    if scaled:
        scales = refs[quarters : 2 * quarters]
        rows = [(row.astype(F32) * ref[0, 0]).astype(BF16) for row, ref in zip(rows, scales)]
        refs = refs[quarters:]
    rows = jnp.concatenate(rows, axis=0)

    def body(pieces):
        for term in range(terms):
            others = jnp.concatenate([ref[0, term] for ref in pieces], axis=0)
            outs[term][0] = dot_tn(others, rows) if flip else dot_tn(rows, others)

    for_group(groups, refs[quarters:], body)


def weight_grad(rows, groups, picks, flip, scale=None):
    first = groups[0][0]
    count = sum(g[1] for g in groups)
    quarters = len(groups[0][2])
    slots, depth = rows.shape[2:]
    terms, _, width = groups[0][2][0][0].shape[1:]
    specs = [
        pl.BlockSpec((1, 1, slots, depth), lambda e, p, q=quarter: (first + e, p[q], 0, 0))
        for quarter in range(quarters)
    ]
    values = [rows] * quarters
    if scale is not None:
        specs += [
            pl.BlockSpec((1, 1, slots, 1), lambda e, p, q=quarter: (first + e, p[q], 0, 0))
            for quarter in range(quarters)
        ]
        values += [scale] * quarters
    more, others = group_specs(groups)
    shape = (width, depth) if flip else (depth, width)
    return pl.pallas_call(
        functools.partial(weight_grad_kernel, shapes_of(groups), flip, scale is not None),
        grid_spec=pltpu.PrefetchScalarGridSpec(
            num_scalar_prefetch=1,
            grid=(count,),
            in_specs=specs + more,
            out_specs=[pl.BlockSpec((1,) + shape, lambda e, p: (e, 0, 0))] * terms,
        ),
        out_shape=[jax.ShapeDtypeStruct((count,) + shape, F32)] * terms,
        compiler_params=params(),
        cost_estimate=cost(1),
        name="weight_grad",
    )(picks, *values, *others)


def side_by_side_kernel(gate, up, down, out):
    width = gate.shape[1]
    wide = out.shape[1] // 3
    out[...] = jnp.zeros_like(out)
    out[:, :width] = gate[...]
    out[:, wide : wide + width] = up[...]
    out[:, 2 * wide : 2 * wide + width] = down[...].T


def side_by_side(gate, up, down, wide):
    return pl.pallas_call(
        side_by_side_kernel,
        out_shape=jax.ShapeDtypeStruct((gate.shape[0], 3 * wide), BF16),
        compiler_params=params(),
        cost_estimate=cost(3),
        name="side_by_side",
    )(gate, up, down)


def shared_kernel(picks_ref, norm, scale, grad, *refs):
    blocks, (hidden_out, grads_out, part_out, forward_out, weight) = refs[:-5], refs[-5:]
    wide = hidden_out.shape[1]

    @pl.when(pl.program_id(0) == 0)
    def _():
        rows = blocks[0].shape[0]
        if len(blocks) == 1:
            weight[...] = blocks[0][...]
        else:
            half = rows // 2
            for number in range(3):
                start = pl.multiple_of(picks_ref[number] * rows, rows)
                weight[pl.ds(start, rows)] = blocks[number][...]
            start = pl.multiple_of(picks_ref[3] * rows, rows)
            weight[pl.ds(start, half)] = blocks[3][...]
            weight[pl.ds(start + half, half)] = blocks[4][...]

    both = dot(norm[...], weight[:, : 2 * wide]) * scale[...]
    gate_pre, up_pre = both[:, :wide], both[:, wide:]
    grad_hidden = dot(grad[...], weight[:, 2 * wide :])
    sigma = jax.nn.sigmoid(gate_pre)
    act = gate_pre * sigma
    hidden = (act * up_pre).astype(BF16)
    hidden_out[...] = hidden
    forward_out[...] = dot_nt(hidden, weight[:, 2 * wide :]).astype(BF16)
    grads = jnp.concatenate(
        [
            (grad_hidden * up_pre * sigma * (1.0 + gate_pre * (1.0 - sigma))).astype(BF16),
            (grad_hidden * act).astype(BF16),
        ],
        axis=1,
    )
    grads_out[...] = (grads.astype(F32) * scale[...]).astype(BF16)
    part_out[...] = dot_nt(grads, weight[:, : 2 * wide]).astype(BF16)


def shared_experts(norm, scale, grad, weights, picks):
    rows, depth = norm.shape
    wide = weights[0].shape[1] // 3
    block = 256
    return pl.pallas_call(
        shared_kernel,
        grid_spec=pltpu.PrefetchScalarGridSpec(
            num_scalar_prefetch=1,
            grid=(rows // block,),
            in_specs=[
                pl.BlockSpec((block, depth), lambda i, p: (i, 0)),
                pl.BlockSpec((block, 1), lambda i, p: (i, 0)),
                pl.BlockSpec((block, depth), lambda i, p: (i, 0)),
            ]
            + [pl.BlockSpec(weight.shape, lambda i, p: (0, 0)) for weight in weights],
            out_specs=[
                pl.BlockSpec((block, wide), lambda i, p: (i, 0)),
                pl.BlockSpec((block, 2 * wide), lambda i, p: (i, 0)),
                pl.BlockSpec((block, depth), lambda i, p: (i, 0)),
                pl.BlockSpec((block, depth), lambda i, p: (i, 0)),
            ],
            scratch_shapes=[pltpu.VMEM((depth, 3 * wide), BF16)],
        ),
        out_shape=[
            jax.ShapeDtypeStruct((rows, wide), BF16),
            jax.ShapeDtypeStruct((rows, 2 * wide), BF16),
            jax.ShapeDtypeStruct((rows, depth), BF16),
            jax.ShapeDtypeStruct((rows, depth), BF16),
        ],
        compiler_params=params(),
        cost_estimate=cost(16),
        name="shared_experts",
    )(picks, norm, scale, grad, *weights)


def shared_weights_kernel(norm, grads, grad, hidden, out):
    both = grads.shape[1]
    out[:, :both] = dot_tn(norm[...], grads[...]).astype(BF16)
    out[:, both:] = dot_tn(grad[...], hidden[...]).astype(BF16)


def shared_weights(norm, grads, grad, hidden):
    rows, depth = norm.shape
    block = 256
    width = grads.shape[1] + hidden.shape[1]
    return pl.pallas_call(
        shared_weights_kernel,
        grid=(depth // block,),
        in_specs=[
            pl.BlockSpec((rows, block), lambda i: (0, i)),
            pl.BlockSpec(grads.shape, lambda i: (0, 0)),
            pl.BlockSpec((rows, block), lambda i: (0, i)),
            pl.BlockSpec(hidden.shape, lambda i: (0, 0)),
        ],
        out_specs=pl.BlockSpec((block, width), lambda i: (i, 0)),
        out_shape=jax.ShapeDtypeStruct((depth, width), BF16),
        compiler_params=params(),
        cost_estimate=cost(10),
        name="shared_weights",
    )(norm, grads, grad, hidden)


def rope_tables(length):
    half = DR // 2
    position = jnp.arange(length).astype(F32)
    inverse = jnp.exp(-math.log(10000.0) * jnp.arange(half).astype(F32) / half)
    angle = position[:, None] * inverse[None, :]
    cosine, sine = jnp.cos(angle), jnp.sin(angle)
    return jnp.concatenate([cosine, cosine], axis=1), jnp.concatenate([-sine, sine], axis=1)


def turn(value, cosine, sine):
    half = DR // 2
    other = jnp.concatenate([value[:, half:], value[:, :half]], axis=1)
    return value * cosine + other * sine


def visible(starts_ref, sequence):
    length = SEQ_LEN
    query = lax.broadcasted_iota(jnp.int32, (length, 1), 0)
    key = lax.broadcasted_iota(jnp.int32, (1, length), 1)
    seen = key <= query
    for number in range(2):
        low = starts_ref[sequence, number]
        seen |= ((query >= low) & (query < low + PIECE)) & ((key >= low) & (key < low + PIECE))
    return seen


def attention_kernel(heads, starts_ref, proj_ref, rows_scale, latent, gain, w_expand, cos, sin, out, logs, q_out, k_out, v_out, n_out):
    scale = (DN + DR) ** (-0.5)
    cosine, sine = cos[...], sin[...]
    proj = proj_ref[...] * rows_scale[...]
    lat = latent[...].astype(F32)
    compressed = lat[:, :L]
    root = lax.rsqrt(jnp.mean(compressed * compressed, axis=1, keepdims=True) + EPS)
    normed = (compressed * root * gain[...].astype(F32)).astype(BF16)
    n_out[...] = normed
    key_rope = turn(lat[:, L:], cosine, sine).astype(BF16)
    expanded = dot(normed, w_expand[...]).astype(BF16)
    seen = visible(starts_ref, pl.program_id(0))
    for head in range(heads):
        plain = proj[:, head * DN : (head + 1) * DN].astype(BF16)
        start = heads * DN + head * DR
        query = jnp.concatenate([plain, turn(proj[:, start : start + DR], cosine, sine).astype(BF16)], axis=1)
        start = head * (DN + DV)
        key = jnp.concatenate([expanded[:, start : start + DN], key_rope], axis=1)
        value = expanded[:, start + DN : start + DN + DV]
        q_out[0, head] = query
        k_out[0, head] = key
        v_out[0, head] = value
        scores = jnp.where(seen, dot_nt(query, key) * scale, -1e30)
        peak = jnp.max(scores, axis=1, keepdims=True)
        expo = jnp.exp(scores - peak)
        total = jnp.sum(expo, axis=1, keepdims=True)
        weights = (expo / total).astype(BF16)
        out[:, head * DV : (head + 1) * DV] = dot(weights, value).astype(BF16)
        logs[0, head] = peak + jnp.log(total)


def attention_forward(starts, proj, rows_scale, latent, gain, w_expand, cosine, sine, heads):
    band = proj.shape[0]
    seqs = band // SEQ_LEN

    def rows(width):
        return pl.BlockSpec((SEQ_LEN, width), lambda s, p: (s, 0))

    def whole(shape):
        return pl.BlockSpec(shape, lambda s, p: (0, 0))

    def by_head(width):
        return pl.BlockSpec((1, heads, SEQ_LEN, width), lambda s, p: (s, 0, 0, 0))

    def head_shape(width, kind=BF16):
        return jax.ShapeDtypeStruct((seqs, heads, SEQ_LEN, width), kind)

    return pl.pallas_call(
        functools.partial(attention_kernel, heads),
        grid_spec=pltpu.PrefetchScalarGridSpec(
            num_scalar_prefetch=1,
            grid=(seqs,),
            in_specs=[
                rows(proj.shape[1]),
                rows(1),
                rows(L + DR),
                whole((1, L)),
                whole(w_expand.shape),
                whole((SEQ_LEN, DR)),
                whole((SEQ_LEN, DR)),
            ],
            out_specs=[rows(heads * DV), by_head(1), by_head(DN + DR), by_head(DN + DR), by_head(DV), rows(L)],
        ),
        out_shape=[
            jax.ShapeDtypeStruct((band, heads * DV), BF16),
            head_shape(1, F32),
            head_shape(DN + DR),
            head_shape(DN + DR),
            head_shape(DV),
            jax.ShapeDtypeStruct((band, L), BF16),
        ],
        compiler_params=params(),
        cost_estimate=cost(12),
        name="attention",
    )(starts, proj, rows_scale, latent, gain[None], w_expand, cosine, sine)


def attention_back_kernel(heads, starts_ref, q_ref, k_ref, v_ref, logs, grad, w_expand, cos, sin, dq_out, de_out, dl_out):
    scale = (DN + DR) ** (-0.5)
    cosine, sine = cos[...], -sin[...]
    seen = visible(starts_ref, pl.program_id(0))
    rope = None
    latent = None
    for head in range(heads):
        query, key, value = q_ref[0, head], k_ref[0, head], v_ref[0, head]
        grad_here = grad[:, head * DV : (head + 1) * DV]
        scores = jnp.where(seen, dot_nt(query, key) * scale, -1e30)
        weights = jnp.exp(scores - logs[0, head])
        grad_weights = dot_nt(grad_here, value)
        centre = jnp.sum(weights * grad_weights, axis=1, keepdims=True)
        grad_scores = (weights * (grad_weights - centre)).astype(BF16)
        grad_query = dot(grad_scores, key) * scale
        grad_key = dot_tn(grad_scores, query) * scale
        grad_value = dot_tn(weights.astype(BF16), grad_here)
        dq_out[:, head * DN : (head + 1) * DN] = grad_query[:, :DN].astype(BF16)
        start = heads * DN + head * DR
        dq_out[:, start : start + DR] = turn(grad_query[:, DN:], cosine, sine).astype(BF16)
        part = turn(grad_key[:, DN:], cosine, sine)
        rope = part if rope is None else rope + part
        both = jnp.concatenate([grad_key[:, :DN].astype(BF16), grad_value.astype(BF16)], axis=1)
        start = head * (DN + DV)
        de_out[:, start : start + DN + DV] = both
        part = dot_nt(both, w_expand[:, start : start + DN + DV])
        latent = part if latent is None else latent + part
    dl_out[:, :L] = latent.astype(BF16)
    dl_out[:, L:] = rope.astype(BF16)


def attention_backward(starts, query, key, value, logs, grad, w_expand, cosine, sine):
    seqs, heads = query.shape[:2]
    band = seqs * SEQ_LEN

    def rows(width):
        return pl.BlockSpec((SEQ_LEN, width), lambda s, p: (s, 0))

    def whole(shape):
        return pl.BlockSpec(shape, lambda s, p: (0, 0))

    def by_head(width):
        return pl.BlockSpec((1, heads, SEQ_LEN, width), lambda s, p: (s, 0, 0, 0))

    widths = (heads * (DN + DR), heads * (DN + DV), L + DR)
    return pl.pallas_call(
        functools.partial(attention_back_kernel, heads),
        grid_spec=pltpu.PrefetchScalarGridSpec(
            num_scalar_prefetch=1,
            grid=(seqs,),
            in_specs=[
                by_head(DN + DR),
                by_head(DN + DR),
                by_head(DV),
                by_head(1),
                rows(heads * DV),
                whole(w_expand.shape),
                whole((SEQ_LEN, DR)),
                whole((SEQ_LEN, DR)),
            ],
            out_specs=[rows(width) for width in widths],
        ),
        out_shape=[jax.ShapeDtypeStruct((band, width), BF16) for width in widths],
        compiler_params=params(),
        cost_estimate=cost(14),
        name="attention_back",
    )(starts, query, key, value, logs, grad, w_expand, cosine, sine)


def norm_products_kernel(picks_ref, *refs):
    query, latent = refs[:5], refs[5:10]
    weight, whole_out, part_out = refs[10:]
    half = query[3].shape[0]

    def write(number, start, query_rows, latent_rows):
        both = jnp.concatenate([query_rows, latent_rows], axis=1)
        place_of = pl.ds(picks_ref[number], 1)
        whole_out[place_of, start : start + half] = both[None]
        part_out[place_of, start : start + half] = dot_nt(both, weight[...]).astype(BF16)[None]

    for number in range(3):
        for start in (0, half):
            rows = slice(start, start + half)
            write(number, start, query[number][rows], latent[number][rows])
    write(3, 0, query[3][...], latent[3][...])
    write(3, half, query[4][...], latent[4][...])


def norm_products(query, latent, weight, picks):
    rows = query[0].shape[0]
    width = weight.shape[1]
    vmem = pl.BlockSpec(memory_space=pltpu.VMEM)
    return pl.pallas_call(
        norm_products_kernel,
        in_specs=[pl.BlockSpec(memory_space=pltpu.SMEM)] + [vmem] * 11,
        out_specs=[vmem, vmem],
        out_shape=[
            jax.ShapeDtypeStruct((4, rows, width), BF16),
            jax.ShapeDtypeStruct((4, rows, weight.shape[0]), BF16),
        ],
        compiler_params=params(),
        cost_estimate=cost(8),
        name="norm_products",
    )(picks, *query, *latent, weight)


def norm_backward(value, scale, gain, grad_norm, row_total, width):
    return (
        scale[:, None] * gain * grad_norm - value * (scale**3 / width)[:, None] * row_total[:, None]
    )


def widen(value, width):
    return jnp.pad(value, ((0, 0), (0, width - value.shape[1])))


def up_to(width):
    return 128 * ((width + 127) // 128)


def per_device(
    hidden_in,
    expert_routes,
    piece_starts,
    query_weight,
    latent_weight,
    latent_gain,
    expand_weight,
    output_weight,
    attention_gain,
    ffn_gain,
    router_weight,
    gate_weight,
    up_weight,
    down_weight,
    shared_gate,
    shared_up,
    shared_down,
    grad_out,
):
    row_parts = lax.axis_size("gx")
    column_parts = lax.axis_size("gy")
    here_x = lax.axis_index("gx")
    here_y = lax.axis_index("gy")
    local_rows, local_width = hidden_in.shape
    all_tokens = local_rows * column_parts
    band_rows = all_tokens // row_parts
    head_width = query_weight.shape[1]
    heads_here = head_width // (DN + DR)
    latent_width = latent_weight.shape[1]
    experts_here = gate_weight.shape[0]
    shared_width = shared_gate.shape[1]
    cap = 16 * ((local_rows * TOPK * 5 + 64 * EXPERTS - 1) // (64 * EXPERTS))
    blocks = column_parts
    quarter_blocks = blocks // row_parts
    quarter_slots = quarter_blocks * cap
    on_square = square()
    if on_square:
        order_of = numbers(here_x, here_x ^ 1, here_x ^ 2, here_x ^ 3)
    else:
        order_of = jnp.arange(row_parts, dtype=jnp.int32)

    waited.clear()
    hidden_all = spread_rows(hidden_in)
    hidden = hidden_in.astype(F32)
    grad_top = grad_out.astype(F32)
    wide = up_to(shared_width)
    shared_weight = side_by_side(shared_gate, shared_up, shared_down, wide)
    scale_one = lax.rsqrt(feature_total(jnp.sum(hidden * hidden, axis=1)) / D + EPS)
    sent = jnp.concatenate([expert_routes.T.astype(F32), scale_one[None]], axis=0)
    gathered = jnp.broadcast_to(sent[None], (column_parts,) + sent.shape)
    gathered = lax.all_to_all(gathered, "gy", split_axis=0, concat_axis=0, tiled=True)
    grad_top_tokens = to_tokens(after(grad_out, gathered))
    gathered = gathered.transpose(1, 0, 2).reshape(TOPK + 1, all_tokens)
    routes_all = gathered[:TOPK].astype(jnp.int32)
    scale_one_all = gathered[TOPK]
    mine = here_y * experts_here + jnp.arange(experts_here, dtype=jnp.int32)
    named = jnp.any(routes_all[:, :, None] == mine[None, None, :], axis=0)
    named_blocks = named.astype(BF16).reshape(blocks, local_rows, experts_here)
    order = jnp.arange(local_rows, dtype=jnp.int32)
    earlier = (order[None, :] < order[:, None]).astype(BF16)
    slot = jnp.einsum("ts,bse->bte", earlier, named_blocks, preferred_element_type=F32)
    code = jnp.where(named, slot.reshape(all_tokens, experts_here), -1.0)
    chosen = one_hot(code, cap, blocks)
    code_here = pick(code.reshape(row_parts, quarter_blocks, local_rows, experts_here), here_x, 0)
    spots = jnp.arange(cap, dtype=jnp.int32).astype(F32)
    at_slot = code_here[:, :, :, None] == spots
    by_head = query_weight.reshape(-1, heads_here, DN + DR)
    used = head_width + latent_width
    in_weight = jnp.concatenate(
        [
            by_head[:, :, :DN].reshape(-1, heads_here * DN),
            by_head[:, :, DN:].reshape(-1, heads_here * DR),
            widen(latent_weight, up_to(used) - head_width),
        ],
        axis=1,
    )
    cosine, sine = rope_tables(SEQ_LEN)
    if on_square:
        shared_weight = after(shared_weight, gathered)
        shared_x, shared_y = swap(shared_weight, 1), swap(shared_weight, 2)
        hidden_all, shared_x, shared_y, chosen = together(hidden_all, shared_x, shared_y, chosen)
    hidden_all, in_weight, cosine, sine = together(hidden_all, in_weight, cosine, sine)

    gained_one_all = (hidden_all.astype(F32) * attention_gain).astype(BF16)
    projected = band_total(gained_one_all, in_weight, 1)
    band_one = pick(scale_one_all.reshape(row_parts, band_rows), here_x, 0)[:, None]
    grad_top_all = spread_rows(after(grad_out, hidden_all))
    latent_part = (projected[:, head_width:used] * band_one).astype(BF16)
    latent_part = after(latent_part, grad_top_all)
    latent_all = lax.all_gather(latent_part, "gy", axis=1, tiled=True)


    if on_square:
        middle = shared_weight.shape[0] // 2
        shared_x, shared_y = after((shared_x, shared_y), latent_part)
        far = swap(shared_y[:middle], 1), swap(shared_x[middle:], 2)
    else:
        weights_of_shared = (lax.all_gather(shared_weight, "gx", axis=0, tiled=True),)
    grad_top_band = spread_rows(after(grad_top_tokens, latent_all))

    attended, logs, query_seq, key_seq, value_seq, latent_norm = attention_forward(
        piece_starts, projected, band_one, latent_all, latent_gain, expand_weight, cosine, sine, heads_here
    )
    if on_square:
        attended, *far = together(attended, *far)
        weights_of_shared = (shared_weight, shared_x, shared_y, *far)
    grad_rows = dispatch(after(chosen, attended), grad_top_all, cap, blocks)
    grad_rows = grad_rows.reshape(experts_here, row_parts, quarter_slots, -1)
    attended_all = after(collect_rows(attended), grad_rows)
    attention_part = dot(attended_all, output_weight).astype(BF16)
    after_attention = hidden + outer_total(attention_part).astype(F32)

    if on_square:
        half = experts_here // 2
        rows = after(grad_rows, attention_part, grad_top_band)
        grad_hidden_low = square_sum(rows, down_weight, 0, half, 2, True, False, BF16)
        after_attention = after(after_attention, grad_hidden_low)

    gained = (after_attention * ffn_gain).astype(BF16)
    gained_all = spread_rows(gained)
    gained_tokens = to_tokens(gained)
    gained_band = spread_rows(gained_tokens)
    squares = jnp.sum(after_attention * after_attention, axis=1, keepdims=True)
    logits = dot(gained, router_weight)
    totals = widen(jnp.concatenate([logits, squares], axis=1), 128)
    if on_square:
        norm_one_all = hidden_all.astype(F32) * scale_one_all[:, None] * attention_gain
        norm_one_all = after(norm_one_all.astype(BF16), totals)
        rows, norm_one_all = together(after(grad_rows, totals), norm_one_all)
        grad_hidden_high = square_sum(rows, down_weight, half, half, 3, True, False, BF16)
    totals = square_total(totals)
    scale_two = lax.rsqrt(totals[:, EXPERTS] / D + EPS)
    probs = jax.nn.softmax(totals[:, :EXPERTS] * scale_two[:, None], axis=-1)
    norm_two = (after_attention * scale_two[:, None] * ffn_gain).astype(BF16)
    sent = jnp.concatenate(
        [
            probs.reshape(local_rows, column_parts, experts_here),
            jnp.broadcast_to(scale_two[:, None, None], (local_rows, column_parts, 1)),
        ],
        axis=2,
    ).transpose(1, 0, 2)
    received = lax.all_to_all(sent, "gy", split_axis=0, concat_axis=0, tiled=True)
    scale_two_all = received[:, :, experts_here].reshape(all_tokens)
    received = pick(received.reshape(row_parts, quarter_blocks, local_rows, experts_here + 1), here_x, 0)
    factors = jnp.stack(
        [
            jnp.sum(jnp.where(at_slot, value[:, :, :, None], 0.0), axis=1)
            .transpose(1, 0, 2)
            .reshape(experts_here, quarter_slots)
            for value in (received[:, :, :experts_here], received[:, :, experts_here:])
        ],
        axis=2,
    )
    if on_square:
        gained_all, factors = lax.optimization_barrier((gained_all, factors, grad_hidden_high))[:2]
    rows_two, slot_scale = dispatch(chosen, gained_all, cap, blocks, scale_two_all[:, None])
    rows_two = rows_two.reshape(experts_here, row_parts, quarter_slots, -1)
    slot_scale = slot_scale.reshape(experts_here, row_parts, quarter_slots, 1)

    band_scale = scale_two_all.reshape(blocks, row_parts, -1)
    band_scale = pick(band_scale, here_x, 1).reshape(-1, 1)
    shared_hidden, grad_shared_both, grad_shared_part, shared_part = shared_experts(
        after(gained_band, rows_two), band_scale, grad_top_band, weights_of_shared, order_of
    )
    grad_norm_shared = outer_total(grad_shared_part)
    shared_out = outer_total(shared_part)

    both_weights = (gate_weight, up_weight)
    if on_square:
        own, from_x, from_y, across, scaled, back_rows, slot_grad = routed_experts(
            after(rows_two, shared_part), gate_weight, up_weight, grad_hidden_low, grad_hidden_high, factors
        )
        whole = [(own, 0), (from_x, 0), (from_y, 0), (across, 0)]
        grad_groups = [(0, experts_here, whole)]
    else:
        everything = order_of

        def whole_total(rows, weight, transposed):
            out = group(rows, everything, row_parts, (weight,), 0, experts_here, transposed)
            out = out.reshape((experts_here,) + out.shape[2:])
            return lax.psum_scatter(out, "gx", scatter_dimension=1, tiled=True)[:, 0].astype(F32)

        scale = factors[:, :, 1:2]
        scaled, grad_gate_pre, grad_up_pre, slot_grad = expert_body(
            whole_total(rows_two, gate_weight, False) * scale,
            whole_total(rows_two, up_weight, False) * scale,
            whole_total(grad_rows, down_weight, True),
            factors[:, :, 0:1],
        )
        grads = jnp.stack([grad_gate_pre, grad_up_pre], axis=1)
        whole = lax.all_gather(grads, "gx", axis=0, tiled=False)
        grad_groups = [(0, experts_here, [(whole[q], 0) for q in range(row_parts)])]
        whole = lax.all_gather(scaled[:, None], "gx", axis=0, tiled=False)
        hidden_groups = [(0, experts_here, [(whole[q], 0) for q in range(row_parts)])]

        back_rows = back(grad_groups, order_of, both_weights, True)

    back_rows = back_rows.reshape(experts_here, blocks * cap, -1)
    grad_norm_part = combine(after(chosen, shared_out), [back_rows], cap, blocks)
    grad_norm_routed = outer_total(grad_norm_part)

    both_shared = after(jnp.stack([grad_norm_shared, shared_out]), grad_norm_part)
    both_shared = lax.all_to_all(both_shared, "gx", split_axis=2, concat_axis=1, tiled=True)
    grad_norm_shared, shared_out = both_shared[0].astype(F32), both_shared[1].astype(F32)
    if on_square:
        scaled = after(scaled, grad_norm_shared)
        low, high = scaled[:half], scaled[half:]
        low_x, low_y, high_x, high_y = swap(low, 1), swap(low, 2), swap(high, 1), swap(high, 2)
    slot_grad = after(slot_grad, grad_norm_part)
    slot_grad = slot_grad.reshape(experts_here, quarter_blocks, cap).transpose(1, 0, 2)
    grad_probs = jnp.sum(jnp.where(at_slot, slot_grad[:, None], 0.0), axis=3)
    grad_probs = grad_probs.reshape(band_rows, experts_here)
    grad_probs = collect(grad_probs.T).transpose(0, 2, 1).reshape(blocks, local_rows, experts_here)
    grad_probs = lax.all_to_all(grad_probs, "gy", split_axis=0, concat_axis=2, tiled=True)
    grad_probs = grad_probs.reshape(local_rows, EXPERTS)
    centre = jnp.sum(probs * grad_probs, axis=1, keepdims=True)
    grad_logits = (probs * (grad_probs - centre)).astype(BF16)
    grad_norm_router = dot_nt(grad_logits, router_weight)
    grad_router_part = dot_tn(norm_two, grad_logits)
    grad_shared = shared_weights(
        after(gained_band, grad_norm_shared), grad_shared_both, grad_top_band, shared_hidden
    )
    grad_norm_routed, grad_norm_router, grad_shared = lax.optimization_barrier(
        (grad_norm_routed, grad_norm_router, grad_shared)
    )
    grad_norm_two = grad_norm_routed.astype(F32) + grad_norm_shared + grad_norm_router

    scaled_after = after_attention * ffn_gain
    row_two = jnp.sum(scaled_after * grad_norm_two, axis=1)
    if on_square and local_rows == 512:
        row_two = small_totals(jnp.pad(row_two.reshape(4, 128), ((0, 4), (0, 0))), None, 4)[0][:4].reshape(-1)
    else:
        row_two = feature_total(row_two)
    grad_after = grad_top + norm_backward(
        after_attention, scale_two, ffn_gain, grad_norm_two, row_two, D
    )
    grad_ffn_part = jnp.sum(grad_norm_two * after_attention * scale_two[:, None], axis=0)
    grad_after_sent = grad_after.astype(BF16)
    grad_after_all = spread_rows(grad_after_sent)

    grad_router = tower_step(after(grad_router_part, grad_after_sent), 0)
    grad_after_all, grad_router = together(grad_after_all, grad_router)
    waiting = after(rows_two, grad_after_sent)
    grad_gate, grad_up = weight_grad(waiting, grad_groups, order_of, False, slot_scale)
    grad_after_all, grad_gate, grad_up = lax.optimization_barrier(
        (grad_after_all, grad_gate, grad_up)
    )
    if on_square:
        grad_after_all, low_x, low_y, high_x, high_y = together(
            grad_after_all, low_x, low_y, high_x, high_y
        )

    grad_attended = band_total(grad_after_all, output_weight, 6, True, BF16)
    if on_square:
        low_y, high_x = after((low_y, high_x), grad_attended)
        low_far, high_far = swap(low_y, 1), swap(high_x, 2)
        hidden_groups = [
            (0, half, [(low, 0), (low_x, 0), (low_y, 0), (low_far, 0)]),
            (half, half, [(high, 0), (high_x, 0), (high_y, 0), (high_far, 0)]),
        ]
    grad_query_pre, grad_expanded, latent_grads = attention_backward(
        piece_starts, query_seq, key_seq, value_seq, logs, grad_attended, expand_weight, cosine, sine
    )
    own_rows = band_rows // column_parts
    latent_sums = outer_total(latent_grads).astype(F32)
    grad_router = tower_step(after(grad_router, latent_grads), 1)
    expand_part = dot_tn(latent_norm, grad_expanded).astype(BF16)
    if on_square:
        expand_away = swap(expand_part, 1)

    if on_square:
        query_x, query_y = swap(grad_query_pre, 1), swap(grad_query_pre, 2)
    waiting = after(down_weight, latent_grads)
    out = back(hidden_groups, order_of, (waiting,), False)
    if on_square:
        out, query_x, query_y = together(out, query_x, query_y)
        middle = band_rows // 2
        far = swap(query_y[:middle], 1), swap(query_x[middle:], 2)
        query_blocks = (grad_query_pre, query_x, query_y, *far)
    out = out.reshape(experts_here, blocks * cap, -1)
    routed_part = combine(chosen, [out], cap, blocks)
    if on_square:
        routed_part, expand_away = together(routed_part, expand_away)
        expand_x = expand_part + expand_away
    routed_part, grad_router = together(routed_part, grad_router)
    latent_sums, routed_part = together(latent_sums, routed_part)
    routed = outer_total(routed_part)
    latent_f32 = lax.dynamic_slice_in_dim(latent_all, here_y * own_rows, own_rows, 0).astype(F32)
    compressed = latent_f32[:, :L]
    latent_scale = lax.rsqrt(jnp.mean(compressed * compressed, axis=1) + EPS)
    grad_latent_norm, grad_rope_key = latent_sums[:, :L], latent_sums[:, L:]
    latent_row = jnp.sum(compressed * latent_gain * grad_latent_norm, axis=1)
    grad_compressed = norm_backward(
        compressed, latent_scale, latent_gain, grad_latent_norm, latent_row, L
    )
    grad_gain_part = jnp.sum(grad_latent_norm * compressed * latent_scale[:, None], axis=0)
    grad_latent_pre = jnp.concatenate([grad_compressed, grad_rope_key], axis=1).astype(BF16)
    grad_latent_own = grad_latent_pre.reshape(own_rows, column_parts, latent_width).transpose(1, 0, 2)
    grad_latent_own = lax.all_to_all(grad_latent_own, "gy", split_axis=0, concat_axis=0, tiled=True)
    if on_square:
        expand_y = swap(after(expand_x, grad_latent_pre), 2)
        grad_latent_own, expand_y = together(grad_latent_own, expand_y)
    grad_latent_own = grad_latent_own.reshape(band_rows, latent_width)
    grad_latent_own = widen(grad_latent_own, up_to(used) - head_width)
    if on_square:
        latent_blocks = (grad_latent_own, *from_others(grad_latent_own))
        grad_projected_all, grad_norm_part = norm_products(
            query_blocks, latent_blocks, in_weight, order_of
        )
        grad_projected_all = grad_projected_all.reshape(all_tokens, -1)
        grad_norm_part = grad_norm_part.reshape(all_tokens, -1)
    else:
        grad_projected = jnp.concatenate([grad_query_pre, grad_latent_own], axis=1)
        grad_projected_all = collect_rows(grad_projected)
        grad_norm_part = dot_nt(grad_projected_all, in_weight).astype(BF16)
    grad_norm_one = outer_total(grad_norm_part).astype(F32)

    mixed = (after_attention + routed.astype(F32) + shared_out).astype(BF16)
    if not on_square:
        norm_one_all = hidden_all.astype(F32) * scale_one_all[:, None] * attention_gain
        norm_one_all = norm_one_all.astype(BF16)
    norm_one_all = after(norm_one_all, grad_norm_part)
    grad_projected = dot_tn(norm_one_all, grad_projected_all)
    grad_query = grad_projected[:, :head_width]
    grad_query = jnp.concatenate(
        [
            grad_query[:, : heads_here * DN].reshape(-1, heads_here, DN),
            grad_query[:, heads_here * DN :].reshape(-1, heads_here, DR),
        ],
        axis=2,
    ).reshape(-1, head_width)
    grad_latent = grad_projected[:, head_width:used]
    grad_output = dot_tn(attended_all, after(grad_after_all, grad_norm_part))
    if on_square:
        grad_expand = expand_x.astype(F32) + expand_y.astype(F32)
    else:
        grad_expand = lax.psum(expand_part, "gx").astype(F32)
    grad_router = tower_step(tower_step(after(grad_router, grad_norm_part), 2), 3)
    grad_shared = inner_rows(after(grad_shared, grad_norm_part))
    (grad_down,) = weight_grad(after(grad_rows, grad_norm_part), hidden_groups, order_of, True)
    grad_norm_one, grad_query, grad_latent, grad_output, grad_expand, grad_down = together(
        grad_norm_one, grad_query, grad_latent, grad_output, grad_expand, grad_down
    )
    row_one = jnp.sum(hidden * attention_gain * grad_norm_one, axis=1)
    grad_attention_part = jnp.sum(grad_norm_one * hidden * scale_one[:, None], axis=0)
    if on_square and local_rows == 512 and local_width == 512:
        inner = jnp.concatenate([row_one, grad_gain_part]).reshape(8, 128)
        outer = jnp.concatenate([grad_attention_part, grad_ffn_part]).reshape(8, 128)
        inner, outer = small_totals(inner, outer, 5)
        row_one = inner[:4].reshape(-1)
        grad_attention_gain = outer[:4].reshape(-1)
        grad_ffn_gain = outer[4:8].reshape(-1)
        grad_latent_gain = outer[12:].reshape(-1)
    else:
        row_one, grad_latent_gain = feature_total((row_one, grad_gain_part))
        grad_attention_gain, grad_ffn_gain, grad_latent_gain = lax.psum(
            (grad_attention_part, grad_ffn_part, grad_latent_gain), "gy"
        )
    grad_hidden = grad_after + norm_backward(
        hidden, scale_one, attention_gain, grad_norm_one, row_one, D
    )
    grad_shared_gate, grad_shared_up, grad_shared_down = shared_sums(
        after(grad_shared, row_one), shared_width
    )
    grad_shared_gate, grad_shared_up = grad_shared_gate.T, grad_shared_up.T
    grad_latent_gain = settle(grad_latent_gain)
    return (
        mixed,
        grad_hidden,
        grad_query,
        grad_latent,
        grad_latent_gain,
        grad_expand,
        grad_output,
        grad_attention_gain,
        grad_ffn_gain,
        grad_router,
        grad_gate,
        grad_up,
        grad_down,
        grad_shared_gate,
        grad_shared_up,
        grad_shared_down,
    )


def solution(mesh):
    return jax.shard_map(
        per_device,
        mesh=mesh,
        in_specs=(
            P("gy", "gx"),
            P("gy", None),
            P("gx", None),
            P("gx", "gy"),
            P("gx", "gy"),
            P(),
            P(None, "gy"),
            P("gy", "gx"),
            P("gx"),
            P("gx"),
            P("gx", None),
            P("gy", "gx", None),
            P("gy", "gx", None),
            P("gy", None, "gx"),
            P("gx", "gy"),
            P("gx", "gy"),
            P("gy", "gx"),
            P("gy", "gx"),
        ),
        out_specs=(
            P("gy", "gx"),
            P("gy", "gx"),
            P("gx", "gy"),
            P("gx", "gy"),
            P(),
            P(None, "gy"),
            P("gy", "gx"),
            P("gx"),
            P("gx"),
            P("gx", None),
            P("gy", "gx", None),
            P("gy", "gx", None),
            P("gy", None, "gx"),
            P("gx", "gy"),
            P("gx", "gy"),
            P("gy", "gx"),
        ),
        check_vma=False,
    )
```

```python
import functools
import math

import jax
import jax.numpy as jnp
from jax import lax
from jax.experimental import pallas as pl
from jax.experimental.pallas import tpu as pltpu
from jax.sharding import PartitionSpec as P

D = 2048
DN = 128
DR = 64
DV = 128
L = 512
EXPERTS = 64
FF = 1408
TOPK = 6
SEQ_LEN = 1024
PIECE = 256


EPS = 1e-06
BF16 = jnp.bfloat16
F32 = jnp.float32
VMEM_LIMIT = 56 * 1024 * 1024


def params():
    return pltpu.CompilerParams(vmem_limit_bytes=VMEM_LIMIT)


def cost(microseconds):
    return pl.CostEstimate(flops=int(microseconds * 0.575e9), bytes_accessed=0, transcendentals=0)


waited = []


def after(value, *others):
    value, others = lax.optimization_barrier((value, others))
    waited.extend(jax.tree.leaves(others))
    return value


def together(*values):
    return lax.optimization_barrier(values)


def settle_kernel(value, *refs):
    refs[-1][...] = value[...]


def settle(value):
    vmem = pl.BlockSpec(memory_space=pltpu.VMEM)
    return pl.pallas_call(
        settle_kernel,
        in_specs=[vmem] + [pl.BlockSpec(memory_space=pl.ANY)] * len(waited),
        out_specs=vmem,
        out_shape=jax.ShapeDtypeStruct(value.shape, value.dtype),
        cost_estimate=cost(1),
        name="settle",
    )(value, *waited)


def swap(value, bit):
    return lax.ppermute(value, "gx", [(i, i ^ bit) for i in range(4)])


def square():
    return lax.axis_size("gx") == 4


def place():
    me = lax.axis_index("gx")
    return me & 1, me >> 1


def pick(value, index, axis):
    return lax.dynamic_index_in_dim(value, index, axis, keepdims=False)


def from_others(block):
    half = block.shape[0] // 2
    from_x = swap(block, 1)
    from_y = swap(block, 2)
    return from_x, from_y, swap(from_y[:half], 1), swap(from_x[half:], 2)


def collect(block):
    if not square():
        return lax.all_gather(block, "gx", axis=0, tiled=False)
    return stacked(block, *from_others(block))


def stacked(block, from_x, from_y, low, high):
    across = jnp.concatenate([low, high], axis=0)
    me = lax.axis_index("gx")
    whole = jnp.zeros((4,) + block.shape, block.dtype)
    for index, value in ((me, block), (me ^ 1, from_x), (me ^ 2, from_y), (me ^ 3, across)):
        whole = lax.dynamic_update_index_in_dim(whole, value, index, 0)
    return whole


def collect_rows(block):
    whole = collect(block)
    return whole.reshape((-1,) + block.shape[1:])


def feature_total(value):
    return lax.psum(value, "gx")


def square_total(value):
    if not square():
        return lax.psum(value, "gx")
    value = value + swap(value, 1)
    return value + swap(value, 2)


def inner_rows(value):
    parts = lax.axis_size("gx")
    value = value.reshape(parts, -1, value.shape[1])
    return lax.all_to_all(value, "gx", split_axis=0, concat_axis=0, tiled=True)


def tower_step(value, step):
    size, bit = lax.axis_size("gy"), 2**step
    if bit >= size:
        return value
    return value + lax.ppermute(value, "gy", [(i, i ^ bit) for i in range(size)])


def spread_rows(value):
    return lax.all_gather(value, "gy", axis=0, tiled=True)


def outer_total(partial):
    return lax.psum_scatter(partial.astype(BF16), "gy", scatter_dimension=0, tiled=True)


def to_tokens(value):
    return lax.all_to_all(value, "gx", split_axis=0, concat_axis=1, tiled=True)


def to_features(value):
    return lax.all_to_all(value, "gx", split_axis=1, concat_axis=0, tiled=True)


def dot(a, b):
    return jnp.dot(a, b, preferred_element_type=F32)


def dot_nt(a, b):
    return lax.dot_general(a, b, (((1,), (1,)), ((), ())), preferred_element_type=F32)


def dot_tn(a, b):
    return lax.dot_general(a, b, (((0,), (0,)), ((), ())), preferred_element_type=F32)


def one_hot_kernel(cap, code_ref, out_ref):
    experts = code_ref.shape[1]
    tokens, slots = out_ref.shape
    column = lax.broadcasted_iota(jnp.int32, (experts, slots), 1)
    low = lax.broadcasted_iota(jnp.int32, (experts, slots), 0) * cap
    inside = (column >= low) & (column < low + cap)
    expand = jnp.where(inside, 1.0, 0.0).astype(BF16)
    offset = jnp.sum(jnp.where(inside, column - low, 0).astype(F32), axis=0, keepdims=True)
    wide = dot(code_ref[...].astype(BF16), expand)
    out_ref[...] = jnp.where(wide == offset, 1.0, 0.0).astype(BF16)


def one_hot(code, cap, blocks):
    tokens, experts = code.shape
    block = tokens // blocks
    return pl.pallas_call(
        functools.partial(one_hot_kernel, cap),
        grid=(blocks,),
        in_specs=[pl.BlockSpec((block, experts), lambda b: (b, 0))],
        out_specs=pl.BlockSpec((block, experts * cap), lambda b: (b, 0)),
        out_shape=jax.ShapeDtypeStruct((tokens, experts * cap), BF16),
        compiler_params=params(),
        cost_estimate=cost(7),
        name="one_hot",
    )(code)


def dispatch_kernel(chosen_ref, rows_ref, out_ref):
    moved = dot_tn(chosen_ref[...], rows_ref[...]).astype(BF16)
    out_ref[...] = moved.reshape(out_ref.shape)


def dispatch_scaled_kernel(chosen_ref, rows_ref, scale_ref, out_ref, scale_out_ref):
    dispatch_kernel(chosen_ref, rows_ref, out_ref)
    high, middle, low = thirds(scale_ref[...])
    parts = jnp.concatenate([high, middle, low], axis=1)
    moved = dot_tn(chosen_ref[...], parts)
    moved = moved[:, 0:1] + moved[:, 1:2] + moved[:, 2:3]
    scale_out_ref[...] = moved.reshape(scale_out_ref.shape)


def thirds(value):
    high = value.astype(BF16)
    rest = value - high.astype(F32)
    middle = rest.astype(BF16)
    return high, middle, (rest - middle.astype(F32)).astype(BF16)


def dispatch(chosen, rows, cap, blocks, scale=None):
    tokens, width = rows.shape
    slots = chosen.shape[1]
    experts = slots // cap
    block = tokens // blocks
    specs = [
        pl.BlockSpec((block, slots), lambda b: (b, 0)),
        pl.BlockSpec((block, width), lambda b: (b, 0)),
    ]
    out_specs = [pl.BlockSpec((experts, cap, width), lambda b: (0, b, 0))]
    shapes = [jax.ShapeDtypeStruct((experts, blocks * cap, width), BF16)]
    values = [chosen, rows]
    if scale is not None:
        specs.append(pl.BlockSpec((block, 1), lambda b: (b, 0)))
        out_specs.append(pl.BlockSpec((experts, cap, 1), lambda b: (0, b, 0)))
        shapes.append(jax.ShapeDtypeStruct((experts, blocks * cap, 1), F32))
        values.append(scale)
    outs = pl.pallas_call(
        dispatch_kernel if scale is None else dispatch_scaled_kernel,
        grid=(blocks,),
        in_specs=specs,
        out_specs=out_specs,
        out_shape=shapes,
        compiler_params=params(),
        cost_estimate=cost(10),
        name="dispatch",
    )(*values)
    return outs[0] if scale is None else outs


def combine_kernel(groups, chosen_ref, *refs):
    out_ref = refs[-1]
    width = out_ref.shape[1]
    pieces = [ref[...].reshape(-1, width) for ref in refs[:groups]]
    slots = pieces[0] if groups == 1 else jnp.concatenate(pieces, axis=0)
    total = dot(chosen_ref[...], slots)
    for ref in refs[groups:-1]:
        total += ref[...].astype(F32)
    out_ref[...] = total.astype(out_ref.dtype)


def combine(chosen, pieces, cap, blocks, extra=()):
    tokens, slots = chosen.shape
    block = tokens // blocks
    width = pieces[0].shape[-1]
    specs = [pl.BlockSpec((block, slots), lambda b: (b, 0))]
    specs += [pl.BlockSpec((p.shape[0], cap, width), lambda b: (0, b, 0)) for p in pieces]
    specs += [pl.BlockSpec((block, width), lambda b: (b, 0)) for _ in extra]
    return pl.pallas_call(
        functools.partial(combine_kernel, len(pieces)),
        grid=(blocks,),
        in_specs=specs,
        out_specs=pl.BlockSpec((block, width), lambda b: (b, 0)),
        out_shape=jax.ShapeDtypeStruct((tokens, width), BF16),
        compiler_params=params(),
        cost_estimate=cost(9),
        name="combine",
    )(chosen, *pieces, *extra)


def group_kernel(parts, weights, adds, transposed, picks_ref, *refs):
    rows = [ref[0, 0] for ref in refs[:parts]]
    source = rows[0] if parts == 1 else jnp.concatenate(rows, axis=0)
    out_ref = refs[-1]
    extra = refs[parts + weights : parts + weights + adds]
    for number in range(weights):
        weight = refs[parts + number][0]
        total = dot_nt(source, weight) if transposed else dot(source, weight)
        for ref in extra:
            total += ref[0, number, 0].astype(F32)
        out_ref[0, number] = total.astype(out_ref.dtype).reshape(out_ref.shape[2:])


def group(rows, picks, parts, weights, first, count, transposed=False, adds=(), kind=BF16, by_quarter=False):
    slots, depth = rows.shape[2:]
    width = weights[0].shape[1] if transposed else weights[0].shape[2]
    many = len(weights)

    def row_spec(part):
        if by_quarter:
            return pl.BlockSpec((1, 1, slots, depth), lambda e, p: (p[part], first + e, 0, 0))
        return pl.BlockSpec((1, 1, slots, depth), lambda e, p: (first + e, p[part], 0, 0))

    def add_spec(number):
        return pl.BlockSpec((1, many, 1, slots, width), lambda e, p: (e, 0, p[parts + number], 0, 0))

    specs = [row_spec(part) for part in range(parts)]
    for weight in weights:
        if by_quarter:
            specs.append(pl.BlockSpec((1,) + weight.shape[1:], lambda e, p: (0, 0, 0)))
        else:
            specs.append(pl.BlockSpec((1,) + weight.shape[1:], lambda e, p: (first + e, 0, 0)))
    specs += [add_spec(number) for number in range(len(adds))]
    return pl.pallas_call(
        functools.partial(group_kernel, parts, many, len(adds), transposed),
        grid_spec=pltpu.PrefetchScalarGridSpec(
            num_scalar_prefetch=1,
            grid=(count,),
            in_specs=specs,
            out_specs=pl.BlockSpec((1, many, parts, slots, width), lambda e, p: (e, 0, 0, 0, 0)),
        ),
        out_shape=jax.ShapeDtypeStruct((count, many, parts, slots, width), kind),
        compiler_params=params(),
        cost_estimate=cost(4),
        name="group",
    )(picks, *([rows] * parts), *weights, *adds)


def numbers(*values):
    return jnp.stack([jnp.asarray(value, jnp.int32) for value in values])


def halves(first, count):
    x, y = place()
    half = count // 2
    me = 2 * y + x
    return (
        (first, half, 1, numbers(1 - x, 3 - x), numbers(2 * (1 - y) + x, 1 - y), numbers(me, y, 0)),
        (first + half, half, 2, numbers(2 - 2 * y, 3 - 2 * y), numbers(2 * y + 1 - x, 1 - x), numbers(me, x, 0)),
    )


def expert_body(gate_pre, up_pre, grad_hidden, gate):
    sigma = jax.nn.sigmoid(gate_pre)
    act = gate_pre * sigma
    hidden = (act * up_pre).astype(BF16).astype(F32)
    grad_gate = jnp.sum(hidden * grad_hidden, axis=-1, keepdims=True)
    scaled = (gate * hidden).astype(BF16)
    grad = gate * grad_hidden
    grad_gate_pre = (grad * up_pre * sigma * (1.0 + gate_pre * (1.0 - sigma))).astype(BF16)
    grad_up_pre = (grad * act).astype(BF16)
    return scaled, grad_gate_pre, grad_up_pre, grad_gate


def neighbours():
    me = lax.axis_index("gx")
    x = me % 2
    y = me // 2
    return x, y, me + 1 - 2 * x, me + 2 - 4 * y


def greet(*others):
    barrier = pltpu.get_barrier_semaphore()
    for other in others:
        pl.semaphore_signal(
            barrier, inc=1, device_id={"gx": other}, device_id_type=pl.DeviceIdType.MESH
        )
    pl.semaphore_wait(barrier, len(others))


def remote(source, target, sent, received, other):
    return pltpu.make_async_remote_copy(
        src_ref=source,
        dst_ref=target,
        send_sem=sent,
        recv_sem=received,
        device_id={"gx": other},
        device_id_type=pl.DeviceIdType.MESH,
    )


def experts_kernel(
    rows,
    w_gate,
    w_up,
    grad_low,
    grad_high,
    factors,
    chosen,
    own_out,
    x_out,
    y_out,
    d_out,
    hid_out,
    tokens_out,
    gate_out,
    hidden_x_out,
    hidden_y_out,
    back_out,
    chosen_held,
    first_sent,
    first,
    second,
    weights,
    loaded,
    first_send,
    first_recv,
    second_send,
    second_recv,
    x_send,
    x_recv,
    y_send,
    y_recv,
    d_send,
    d_recv,
    own_sem,
    weight_sem,
    load_sem,
    chosen_sem,
    hidden_x_send,
    hidden_x_recv,
    hidden_y_send,
    hidden_y_recv,
):
    x, y, x_other, y_other = neighbours()
    me = 2 * y + x
    across = 3 - me
    pairs = rows.shape[0] // 2
    slots = rows.shape[2]
    greet(x_other, y_other)

    def side(odd):
        if odd:
            return y_other, x_other, (2 - 2 * y, 3 - 2 * y), 2 * y + 1 - x, 1 - x, x
        return x_other, y_other, (1 - x, 3 - x), 2 * (1 - y) + x, 1 - y, y

    def fetch(pair):
        for odd in range(2):
            expert = 2 * pair + odd
            pltpu.make_async_copy(w_gate.at[expert], weights.at[odd, 0], weight_sem.at[odd, 0]).start()
            pltpu.make_async_copy(w_up.at[expert], weights.at[odd, 1], weight_sem.at[odd, 1]).start()

    def fetched(pair, odd):
        expert = 2 * pair + odd
        pltpu.make_async_copy(w_gate.at[expert], weights.at[odd, 0], weight_sem.at[odd, 0]).wait()
        pltpu.make_async_copy(w_up.at[expert], weights.at[odd, 1], weight_sem.at[odd, 1]).wait()

    def first_copy(pair, odd):
        expert = 2 * pair + odd
        return remote(
            first_sent.at[pair % 2, odd],
            first.at[expert],
            first_send.at[expert],
            first_recv.at[expert],
            side(odd)[0],
        )

    def second_copy(pair, odd):
        expert = 2 * pair + odd
        return remote(
            first.at[expert, side(odd)[4]],
            second.at[expert],
            second_send.at[expert],
            second_recv.at[expert],
            side(odd)[1],
        )

    def x_copy(pair, odd):
        expert = 2 * pair + odd
        source = first.at[expert, side(odd)[5]]
        return remote(source, x_out.at[expert], x_send.at[expert], x_recv.at[expert], x_other)

    def y_copy(pair, odd):
        expert = 2 * pair + odd
        source = first.at[expert, side(odd)[5]]
        return remote(source, y_out.at[expert], y_send.at[expert], y_recv.at[expert], y_other)

    def own_copy(pair, odd):
        expert = 2 * pair + odd
        return pltpu.make_async_copy(
            first.at[expert, side(odd)[5]], own_out.at[expert], own_sem.at[expert]
        )

    def far_copy(pair, odd):
        expert = 2 * pair + odd
        source = x_out if odd else y_out
        return remote(
            source.at[expert],
            d_out.at[expert],
            d_send.at[expert],
            d_recv.at[expert],
            side(odd)[0],
        )

    def send_first(pair):
        fetch(pair)
        for odd in range(2):
            expert = 2 * pair + odd

            @pl.when(pair >= 2)
            def _(odd=odd):
                first_copy(pair - 2, odd).wait_send()

            low, high = side(odd)[2]
            source = jnp.concatenate([rows[expert, low], rows[expert, high]], axis=0)
            fetched(pair, odd)
            for number in range(2):
                out = dot(source, weights[odd, number]).astype(BF16)
                first_sent[pair % 2, odd, 0, number] = out[:slots]
                first_sent[pair % 2, odd, 1, number] = out[slots:]
            first_copy(pair, odd).start()

    def send_second(pair):
        fetch(pair)
        for odd in range(2):
            expert = 2 * pair + odd
            _, _, _, quarter, spot, _ = side(odd)
            fetched(pair, odd)
            first_copy(pair, odd).wait_recv()
            for number in range(2):
                out = dot(rows[expert, quarter], weights[odd, number])
                out += first[expert, spot, number].astype(F32)
                first[expert, spot, number] = out.astype(BF16)
            second_copy(pair, odd).start()

    def hidden_gradient(expert):
        half = grad_low.shape[0]
        low = grad_low[jnp.minimum(expert, half - 1)].astype(F32)
        high = grad_high[jnp.maximum(expert - half, 0)].astype(F32)
        return jnp.where(expert < half, low, high)

    def finish(pair):
        fetch(pair)
        for odd in range(2):
            expert = 2 * pair + odd
            spot = side(odd)[5]
            fetched(pair, odd)
            second_copy(pair, odd).wait_recv()
            scale = factors[expert, :, 1:2]
            source = rows[expert, me]
            gate_pre, up_pre = (
                dot(source, weights[odd, number])
                + first[expert, spot, number].astype(F32)
                + second[expert, number].astype(F32)
                for number in range(2)
            )
            scaled, grad_gate_pre, grad_up_pre, grad_gate = expert_body(
                gate_pre * scale,
                up_pre * scale,
                hidden_gradient(expert),
                factors[expert, :, 0:1],
            )
            first[expert, spot, 0] = grad_gate_pre
            first[expert, spot, 1] = grad_up_pre
            x_copy(pair, odd).start()
            y_copy(pair, odd).start()
            own_copy(pair, odd).start()
            hid_out[expert, 0] = scaled
            gate_out[expert] = grad_gate

    def pass_on(pair):
        for odd in range(2):
            (x_copy if odd else y_copy)(pair, odd).wait_recv()
            far_copy(pair, odd).start()

        @pl.when(pair == pairs - 1)
        def _():
            for odd in range(2):
                hidden_x_copy(odd).start()
                hidden_y_copy(odd).start()

    def hidden_x_copy(odd):
        return remote(
            hid_out.at[odd], hidden_x_out.at[odd], hidden_x_send.at[odd], hidden_x_recv.at[odd], x_other
        )

    def hidden_y_copy(odd):
        return remote(
            hid_out.at[odd], hidden_y_out.at[odd], hidden_y_send.at[odd], hidden_y_recv.at[odd], y_other
        )

    def load(pair, odd, number):
        expert = 2 * pair + odd
        source = (x_out, y_out, d_out)[number]
        return pltpu.make_async_copy(
            source.at[expert], loaded.at[odd, number], load_sem.at[odd, number]
        )

    def send_back(pair):
        fetch(pair)
        for odd in range(2):
            (y_copy if odd else x_copy)(pair, odd).wait_recv()
            load(pair, odd, 0).start()
            load(pair, odd, 1).start()
        for odd in range(2):
            far_copy(pair, odd).wait_recv()
            load(pair, odd, 2).start()
        for odd in range(2):
            expert = 2 * pair + odd
            fetched(pair, odd)
            for number in range(3):
                load(pair, odd, number).wait()
            spot = side(odd)[5]
            total = None
            for number in range(2):
                source = jnp.concatenate(
                    [first[expert, spot, number]] + [loaded[odd, part, number] for part in range(3)],
                    axis=0,
                )
                part = dot_nt(source, weights[odd, number])
                total = part if total is None else total + part
            total = total.astype(BF16)
            for number, quarter in enumerate((me, x_other, y_other, across)):
                back_out[expert, quarter] = total[number * slots : (number + 1) * slots]

    def step(number, _):
        for lag, stage in enumerate((send_first, send_second, finish, pass_on, send_back)):

            @pl.when((number >= lag) & (number < pairs + lag))
            def _(lag=lag, stage=stage):
                stage(number - lag)

        return 0

    experts, quarters = rows.shape[:2]
    block, cap = chosen_held.shape[1], chosen.shape[1] // experts
    per_quarter = slots // cap
    blocks = quarters * per_quarter

    def chosen_copy(number):
        return pltpu.make_async_copy(
            chosen.at[pl.ds(number * block, block)], chosen_held.at[number % 2], chosen_sem.at[number % 2]
        )

    def to_tokens_of(number, _):
        chosen_copy(number).wait()

        @pl.when(number + 1 < blocks)
        def _():
            chosen_copy(number + 1).start()

        spots = pl.ds((number % per_quarter) * cap, cap)
        pieces = [back_out[expert, number // per_quarter, spots] for expert in range(experts)]
        total = dot(chosen_held[number % 2], jnp.concatenate(pieces, axis=0))
        tokens_out[pl.ds(number * block, block)] = total.astype(BF16)
        return 0

    chosen_copy(0).start()
    lax.fori_loop(0, pairs + 4, step, 0)
    lax.fori_loop(0, blocks, to_tokens_of, 0)
    for odd in range(2):
        hidden_x_copy(odd).wait()
        hidden_y_copy(odd).wait()

    def drain(pair, _):
        for odd in range(2):

            @pl.when(pair >= pairs - 2)
            def _(odd=odd):
                first_copy(pair, odd).wait_send()

            second_copy(pair, odd).wait_send()
            own_copy(pair, odd).wait()
            x_copy(pair, odd).wait_send()
            y_copy(pair, odd).wait_send()
            far_copy(pair, odd).wait_send()
        return 0

    lax.fori_loop(0, pairs, drain, 0)


def routed_experts(rows, w_gate, w_up, grad_low, grad_high, factors, chosen, blocks):
    experts, quarters, slots, depth = rows.shape
    width = w_gate.shape[2]
    vmem = pl.BlockSpec(memory_space=pltpu.VMEM)
    anywhere = pl.BlockSpec(memory_space=pl.ANY)
    block = jax.ShapeDtypeStruct((experts, 2, slots, width), BF16)
    dma = pltpu.SemaphoreType.DMA
    return pl.pallas_call(
        experts_kernel,
        in_specs=[vmem, anywhere, anywhere, vmem, vmem, vmem, anywhere],
        out_specs=[anywhere] * 4 + [vmem] * 3 + [anywhere] * 2,
        out_shape=[block] * 4
        + [
            jax.ShapeDtypeStruct((experts, 1, slots, width), BF16),
            jax.ShapeDtypeStruct((chosen.shape[0], depth), BF16),
            jax.ShapeDtypeStruct((experts, slots, 1), F32),
            jax.ShapeDtypeStruct((2, 1, slots, width), BF16),
            jax.ShapeDtypeStruct((2, 1, slots, width), BF16),
        ],
        scratch_shapes=[
            pltpu.VMEM((experts, quarters, slots, depth), BF16),
            pltpu.VMEM((2, chosen.shape[0] // blocks, chosen.shape[1]), BF16),
            pltpu.VMEM((2, 2, 2, 2, slots, width), BF16),
            pltpu.VMEM((experts, 2, 2, slots, width), BF16),
            pltpu.VMEM((experts, 2, slots, width), BF16),
            pltpu.VMEM((2, 2, depth, width), BF16),
            pltpu.VMEM((2, 3, 2, slots, width), BF16),
        ]
        + [dma((experts,))] * 11
        + [dma((2, 2)), dma((2, 3))]
        + [dma((2,))] * 5,
        compiler_params=pltpu.CompilerParams(
            collective_id=0, has_side_effects=True, vmem_limit_bytes=VMEM_LIMIT
        ),
        cost_estimate=cost(390),
        name="routed_experts",
    )(rows, w_gate, w_up, grad_low, grad_high, factors, chosen)


def sum_kernel(base, by_quarter, own_weights, transposed, rows, weight, out, sent, first, second, held, *sems):
    first_send, first_recv, second_send, second_recv, weight_sem = sems
    x, y, x_other, y_other = neighbours()
    me = 2 * y + x
    pairs = sent.shape[0] // 2
    slots = sent.shape[2]

    def side(odd):
        if odd:
            return y_other, x_other, (2 - 2 * y, 3 - 2 * y), 2 * y + 1 - x, 1 - x, x
        return x_other, y_other, (1 - x, 3 - x), 2 * (1 - y) + x, 1 - y, y

    def source(item, quarter):
        return rows[quarter, item] if by_quarter else rows[base + item, quarter]

    def product(value, item):
        matrix = held[item] if own_weights else weight[...]
        return dot_nt(value, matrix) if transposed else dot(value, matrix)

    def weight_copy(item):
        return pltpu.make_async_copy(weight.at[base + item], held.at[item], weight_sem.at[item])

    def first_copy(item, odd):
        return remote(sent.at[item], first.at[item], first_send.at[item], first_recv.at[item], side(odd)[0])

    def second_copy(item, odd):
        return remote(
            first.at[item, side(odd)[4]],
            second.at[item],
            second_send.at[item],
            second_recv.at[item],
            side(odd)[1],
        )

    def send_first(pair):
        for odd in range(2):
            item = 2 * pair + odd
            low, high = side(odd)[2]
            if own_weights:
                weight_copy(item).wait()
            result = product(jnp.concatenate([source(item, low), source(item, high)], axis=0), item)
            sent[item, 0] = result[:slots].astype(BF16)
            sent[item, 1] = result[slots:].astype(BF16)
            first_copy(item, odd).start()

    def send_second(pair):
        for odd in range(2):
            item = 2 * pair + odd
            _, _, _, quarter, spot, _ = side(odd)
            result = product(source(item, quarter), item)
            first_copy(item, odd).wait_recv()
            first[item, spot] = (result + first[item, spot].astype(F32)).astype(BF16)
            second_copy(item, odd).start()

    def finish(pair):
        for odd in range(2):
            item = 2 * pair + odd
            result = product(source(item, me), item) + first[item, side(odd)[5]].astype(F32)
            second_copy(item, odd).wait_recv()
            out[item] = (result + second[item].astype(F32)).astype(out.dtype)

    def fetch(item, _):
        weight_copy(item).start()
        return 0

    if own_weights:
        lax.fori_loop(0, 2 * pairs, fetch, 0)
    greet(x_other, y_other)

    def step(number, _):
        for lag, stage in enumerate((send_first, send_second, finish)):

            @pl.when((number >= lag) & (number < pairs + lag))
            def _(lag=lag, stage=stage):
                stage(number - lag)

        return 0

    lax.fori_loop(0, pairs + 2, step, 0)

    def drain(pair, _):
        for odd in range(2):
            item = 2 * pair + odd
            first_copy(item, odd).wait_send()
            second_copy(item, odd).wait_send()
        return 0

    lax.fori_loop(0, pairs, drain, 0)


def square_sum(rows, weight, base, items, number, transposed, by_quarter, kind):
    slots, depth = rows.shape[2:]
    own_weights = weight.ndim == 3
    width = weight.shape[-2] if transposed else weight.shape[-1]
    vmem = pl.BlockSpec(memory_space=pltpu.VMEM)
    dma = pltpu.SemaphoreType.DMA
    held = (items,) + weight.shape[1:] if own_weights else (8, 128)
    return pl.pallas_call(
        functools.partial(sum_kernel, base, by_quarter, own_weights, transposed),
        in_specs=[vmem, pl.BlockSpec(memory_space=pl.ANY) if own_weights else vmem],
        out_specs=vmem,
        out_shape=jax.ShapeDtypeStruct((items, slots, width), kind),
        scratch_shapes=[
            pltpu.VMEM((items, 2, slots, width), BF16),
            pltpu.VMEM((items, 2, slots, width), BF16),
            pltpu.VMEM((items, slots, width), BF16),
            pltpu.VMEM(held, BF16),
        ]
        + [dma((items,))] * 5,
        compiler_params=pltpu.CompilerParams(
            collective_id=number, has_side_effects=True, vmem_limit_bytes=VMEM_LIMIT
        ),
        cost_estimate=cost(13.5 * items if own_weights else 20 + 25 * width // 512),
        name="square_sum",
    )(rows, weight)


def band_total(rows, weight, number, transposed=False, kind=F32):
    if not square():
        whole = (dot_nt(rows, weight) if transposed else dot(rows, weight)).astype(BF16)
        return lax.psum_scatter(whole, "gx", scatter_dimension=0, tiled=True).astype(kind)
    source = rows.reshape(4, 4, rows.shape[0] // 16, rows.shape[1])
    out = square_sum(source, weight, 0, 4, number, transposed, True, kind)
    return out.reshape(-1, out.shape[2])


def small_kernel(both, inner_ref, outer_ref, inner_out, outer_out, inner_land, outer_land, send, recv, far_send, far_recv):
    x, y, x_other, y_other = neighbours()
    me = 2 * y + x
    peers = (x_other, y_other, 3 - me)
    here = lax.axis_index("gy")
    size = outer_land.shape[0]
    barrier = pltpu.get_barrier_semaphore()
    for other in peers:
        pl.semaphore_signal(barrier, inc=1, device_id={"gx": other}, device_id_type=pl.DeviceIdType.MESH)
    for step in range(1, size if both else 1):
        pl.semaphore_signal(
            barrier, inc=1, device_id={"gy": (here + step) % size}, device_id_type=pl.DeviceIdType.MESH
        )
    pl.semaphore_wait(barrier, 3 + (size - 1 if both else 0))

    inner_land[me] = inner_ref[...]

    def inner_copy(number):
        return remote(inner_ref, inner_land.at[me], send.at[number], recv.at[number], peers[number])

    for number in range(3):
        inner_copy(number).start()
    for number in range(3):
        inner_copy(number).wait()
    total = inner_land[0]
    for number in range(1, 4):
        total = total + inner_land[number]
    inner_out[...] = total
    if not both:
        outer_out[...] = outer_ref[...]
        return
    outer_land[here, 0:8] = outer_ref[...]
    outer_land[here, 8:16] = total

    def outer_copy(step):
        return pltpu.make_async_remote_copy(
            src_ref=outer_land.at[here],
            dst_ref=outer_land.at[here],
            send_sem=far_send.at[step - 1],
            recv_sem=far_recv.at[step - 1],
            device_id={"gy": (here + step) % size},
            device_id_type=pl.DeviceIdType.MESH,
        )

    for step in range(1, size):
        outer_copy(step).start()
    for step in range(1, size):
        outer_copy(step).wait()
    total = outer_land[0]
    for number in range(1, size):
        total = total + outer_land[number]
    outer_out[...] = total


def small_totals(inner, outer, number):
    both = outer is not None
    size = lax.axis_size("gy")
    dma = pltpu.SemaphoreType.DMA
    vmem = pl.BlockSpec(memory_space=pltpu.VMEM)
    return pl.pallas_call(
        functools.partial(small_kernel, both),
        in_specs=[vmem, vmem],
        out_specs=[vmem, vmem],
        out_shape=[
            jax.ShapeDtypeStruct((8, 128), F32),
            jax.ShapeDtypeStruct((16, 128) if both else (8, 128), F32),
        ],
        scratch_shapes=[
            pltpu.VMEM((4, 8, 128), F32),
            pltpu.VMEM((size, 16, 128), F32),
            dma((3,)),
            dma((3,)),
            dma((size - 1,)),
            dma((size - 1,)),
        ],
        compiler_params=pltpu.CompilerParams(
            collective_id=number, has_side_effects=True, vmem_limit_bytes=VMEM_LIMIT
        ),
        cost_estimate=cost(6),
        name="small_totals",
    )(inner, outer if both else jnp.zeros((8, 128), F32))


def shared_sums_kernel(parts, gate, up, down):
    width = gate.shape[0]
    wide = parts.shape[2] // 3
    total = parts[0].astype(F32)
    for number in range(1, parts.shape[0]):
        total = total + parts[number].astype(F32)
    total = total.T
    gate[...] = total[:width]
    up[...] = total[wide : wide + width]
    down[...] = total[2 * wide : 2 * wide + width]


def shared_sums(parts, width):
    rows = parts.shape[1]
    block = 128
    many = parts.shape[0]
    return pl.pallas_call(
        shared_sums_kernel,
        grid=(rows // block,),
        in_specs=[pl.BlockSpec((many, block, parts.shape[2]), lambda i: (0, i, 0))],
        out_specs=[pl.BlockSpec((width, block), lambda i: (0, i))] * 3,
        out_shape=[jax.ShapeDtypeStruct((width, rows), F32)] * 3,
        compiler_params=params(),
        cost_estimate=cost(5),
        name="shared_sums",
    )(parts)


def group_specs(groups):
    specs, values = [], []
    base = groups[0][0]
    for first, count, blocks in groups:
        for value, start in blocks:

            def index(e, p, low=first - base, top=count - 1, start=start):
                return (jnp.clip(e - low, 0, top) + start, 0, 0, 0)

            specs.append(pl.BlockSpec((1,) + value.shape[1:], index))
            values.append(value)
    return specs, values


def for_group(groups, refs, body):
    base = groups[0][0]
    each = len(groups[0][2])
    if len(groups) == 1:
        body(refs[:each])
        return
    step = pl.program_id(0)
    for number, (first, count, _) in enumerate(groups):
        low = first - base

        @pl.when((step >= low) & (step < low + count))
        def _(number=number):
            body(refs[number * each : (number + 1) * each])


def back_kernel(groups, transposed, picks_ref, *refs):
    terms, slots = groups[0][2][0][1:3]
    out_ref = refs[-1]
    weights = refs[-1 - terms : -1]

    def body(pieces):
        total = None
        for term in range(terms):
            source = jnp.concatenate([ref[0, term] for ref in pieces], axis=0)
            part = dot_nt(source, weights[term][0]) if transposed else dot(source, weights[term][0])
            total = part if total is None else total + part
        total = total.astype(BF16)
        for quarter in range(len(pieces)):
            rows = total[quarter * slots : (quarter + 1) * slots]
            out_ref[0, pl.ds(picks_ref[quarter], 1)] = rows[None]

    for_group(groups, refs, body)


def shapes_of(groups):
    return tuple(
        (first, count, tuple(b.shape for b, _ in blocks))
        for first, count, blocks in groups
    )


def back(groups, picks, weights, transposed):
    first = groups[0][0]
    count = sum(g[1] for g in groups)
    quarters = len(groups[0][2])
    terms, slots, depth = groups[0][2][0][0].shape[1:]
    width = weights[0].shape[1] if transposed else weights[0].shape[2]
    specs, values = group_specs(groups)
    specs += [pl.BlockSpec((1,) + w.shape[1:], lambda e, p: (first + e, 0, 0)) for w in weights]
    return pl.pallas_call(
        functools.partial(back_kernel, shapes_of(groups), transposed),
        grid_spec=pltpu.PrefetchScalarGridSpec(
            num_scalar_prefetch=1,
            grid=(count,),
            in_specs=specs,
            out_specs=pl.BlockSpec((1, quarters, slots, width), lambda e, p: (e, 0, 0, 0)),
        ),
        out_shape=jax.ShapeDtypeStruct((count, quarters, slots, width), BF16),
        compiler_params=params(),
        cost_estimate=cost(4 * count),
        name="back",
    )(picks, *values, *weights)


def weight_grad_kernel(groups, flip, scaled, picks_ref, *refs):
    terms = groups[0][2][0][1]
    quarters = len(groups[0][2])
    outs = refs[-terms:]
    rows = [ref[0, 0] for ref in refs[:quarters]]
    if scaled:
        scales = refs[quarters : 2 * quarters]
        rows = [(row.astype(F32) * ref[0, 0]).astype(BF16) for row, ref in zip(rows, scales)]
        refs = refs[quarters:]
    rows = jnp.concatenate(rows, axis=0)

    def body(pieces):
        for term in range(terms):
            others = jnp.concatenate([ref[0, term] for ref in pieces], axis=0)
            outs[term][0] = dot_tn(others, rows) if flip else dot_tn(rows, others)

    for_group(groups, refs[quarters:], body)


def weight_grad(rows, groups, picks, flip, scale=None):
    first = groups[0][0]
    count = sum(g[1] for g in groups)
    quarters = len(groups[0][2])
    slots, depth = rows.shape[2:]
    terms, _, width = groups[0][2][0][0].shape[1:]
    specs = [
        pl.BlockSpec((1, 1, slots, depth), lambda e, p, q=quarter: (first + e, p[q], 0, 0))
        for quarter in range(quarters)
    ]
    values = [rows] * quarters
    if scale is not None:
        specs += [
            pl.BlockSpec((1, 1, slots, 1), lambda e, p, q=quarter: (first + e, p[q], 0, 0))
            for quarter in range(quarters)
        ]
        values += [scale] * quarters
    more, others = group_specs(groups)
    shape = (width, depth) if flip else (depth, width)
    return pl.pallas_call(
        functools.partial(weight_grad_kernel, shapes_of(groups), flip, scale is not None),
        grid_spec=pltpu.PrefetchScalarGridSpec(
            num_scalar_prefetch=1,
            grid=(count,),
            in_specs=specs + more,
            out_specs=[pl.BlockSpec((1,) + shape, lambda e, p: (e, 0, 0))] * terms,
        ),
        out_shape=[jax.ShapeDtypeStruct((count,) + shape, F32)] * terms,
        compiler_params=params(),
        cost_estimate=cost(1),
        name="weight_grad",
    )(picks, *values, *others)


def side_by_side_kernel(gate, up, down, out):
    width = gate.shape[1]
    wide = out.shape[1] // 3
    out[...] = jnp.zeros_like(out)
    out[:, :width] = gate[...]
    out[:, wide : wide + width] = up[...]
    out[:, 2 * wide : 2 * wide + width] = down[...].T


def side_by_side(gate, up, down, wide):
    return pl.pallas_call(
        side_by_side_kernel,
        out_shape=jax.ShapeDtypeStruct((gate.shape[0], 3 * wide), BF16),
        compiler_params=params(),
        cost_estimate=cost(3),
        name="side_by_side",
    )(gate, up, down)


def shared_kernel(picks_ref, norm, scale, grad, *refs):
    blocks, (hidden_out, grads_out, part_out, forward_out, weight) = refs[:-5], refs[-5:]
    wide = hidden_out.shape[1]

    @pl.when(pl.program_id(0) == 0)
    def _():
        rows = blocks[0].shape[0]
        if len(blocks) == 1:
            weight[...] = blocks[0][...]
        else:
            half = rows // 2
            for number in range(3):
                start = pl.multiple_of(picks_ref[number] * rows, rows)
                weight[pl.ds(start, rows)] = blocks[number][...]
            start = pl.multiple_of(picks_ref[3] * rows, rows)
            weight[pl.ds(start, half)] = blocks[3][...]
            weight[pl.ds(start + half, half)] = blocks[4][...]

    both = dot(norm[...], weight[:, : 2 * wide]) * scale[...]
    gate_pre, up_pre = both[:, :wide], both[:, wide:]
    grad_hidden = dot(grad[...], weight[:, 2 * wide :])
    sigma = jax.nn.sigmoid(gate_pre)
    act = gate_pre * sigma
    hidden = (act * up_pre).astype(BF16)
    hidden_out[...] = hidden
    forward_out[...] = dot_nt(hidden, weight[:, 2 * wide :]).astype(BF16)
    grads = jnp.concatenate(
        [
            (grad_hidden * up_pre * sigma * (1.0 + gate_pre * (1.0 - sigma))).astype(BF16),
            (grad_hidden * act).astype(BF16),
        ],
        axis=1,
    )
    grads_out[...] = (grads.astype(F32) * scale[...]).astype(BF16)
    part_out[...] = dot_nt(grads, weight[:, : 2 * wide]).astype(BF16)


def shared_experts(norm, scale, grad, weights, picks):
    rows, depth = norm.shape
    wide = weights[0].shape[1] // 3
    block = 256
    return pl.pallas_call(
        shared_kernel,
        grid_spec=pltpu.PrefetchScalarGridSpec(
            num_scalar_prefetch=1,
            grid=(rows // block,),
            in_specs=[
                pl.BlockSpec((block, depth), lambda i, p: (i, 0)),
                pl.BlockSpec((block, 1), lambda i, p: (i, 0)),
                pl.BlockSpec((block, depth), lambda i, p: (i, 0)),
            ]
            + [pl.BlockSpec(weight.shape, lambda i, p: (0, 0)) for weight in weights],
            out_specs=[
                pl.BlockSpec((block, wide), lambda i, p: (i, 0)),
                pl.BlockSpec((block, 2 * wide), lambda i, p: (i, 0)),
                pl.BlockSpec((block, depth), lambda i, p: (i, 0)),
                pl.BlockSpec((block, depth), lambda i, p: (i, 0)),
            ],
            scratch_shapes=[pltpu.VMEM((depth, 3 * wide), BF16)],
        ),
        out_shape=[
            jax.ShapeDtypeStruct((rows, wide), BF16),
            jax.ShapeDtypeStruct((rows, 2 * wide), BF16),
            jax.ShapeDtypeStruct((rows, depth), BF16),
            jax.ShapeDtypeStruct((rows, depth), BF16),
        ],
        compiler_params=params(),
        cost_estimate=cost(16),
        name="shared_experts",
    )(picks, norm, scale, grad, *weights)


def shared_weights_kernel(norm, grads, grad, hidden, out):
    both = grads.shape[1]
    out[:, :both] = dot_tn(norm[...], grads[...]).astype(BF16)
    out[:, both:] = dot_tn(grad[...], hidden[...]).astype(BF16)


def shared_weights(norm, grads, grad, hidden):
    rows, depth = norm.shape
    block = 256
    width = grads.shape[1] + hidden.shape[1]
    return pl.pallas_call(
        shared_weights_kernel,
        grid=(depth // block,),
        in_specs=[
            pl.BlockSpec((rows, block), lambda i: (0, i)),
            pl.BlockSpec(grads.shape, lambda i: (0, 0)),
            pl.BlockSpec((rows, block), lambda i: (0, i)),
            pl.BlockSpec(hidden.shape, lambda i: (0, 0)),
        ],
        out_specs=pl.BlockSpec((block, width), lambda i: (i, 0)),
        out_shape=jax.ShapeDtypeStruct((depth, width), BF16),
        compiler_params=params(),
        cost_estimate=cost(10),
        name="shared_weights",
    )(norm, grads, grad, hidden)


def rope_tables(length):
    half = DR // 2
    position = jnp.arange(length).astype(F32)
    inverse = jnp.exp(-math.log(10000.0) * jnp.arange(half).astype(F32) / half)
    angle = position[:, None] * inverse[None, :]
    cosine, sine = jnp.cos(angle), jnp.sin(angle)
    return jnp.concatenate([cosine, cosine], axis=1), jnp.concatenate([-sine, sine], axis=1)


def turn(value, cosine, sine):
    half = DR // 2
    other = jnp.concatenate([value[:, half:], value[:, :half]], axis=1)
    return value * cosine + other * sine


def query_blocks(starts_ref, sequence):
    blocks = []
    for first in range(0, SEQ_LEN, PIECE):
        keys = min(SEQ_LEN, first + 2 * PIECE)
        query = first + lax.broadcasted_iota(jnp.int32, (PIECE, 1), 0)
        key = lax.broadcasted_iota(jnp.int32, (1, keys), 1)
        seen = key <= query
        for number in range(2):
            low = starts_ref[sequence, number]
            seen |= ((query >= low) & (query < low + PIECE)) & ((key >= low) & (key < low + PIECE))
        blocks.append((first, keys, seen))
    return blocks


def attention_kernel(heads, starts_ref, proj_ref, rows_scale, latent, gain, w_expand, cos, sin, out, logs, q_out, k_out, v_out, n_out):
    scale = (DN + DR) ** (-0.5)
    cosine, sine = cos[...], sin[...]
    proj = proj_ref[...] * rows_scale[...]
    lat = latent[...].astype(F32)
    compressed = lat[:, :L]
    root = lax.rsqrt(jnp.mean(compressed * compressed, axis=1, keepdims=True) + EPS)
    normed = (compressed * root * gain[...].astype(F32)).astype(BF16)
    n_out[...] = normed
    key_rope = turn(lat[:, L:], cosine, sine).astype(BF16)
    expanded = dot(normed, w_expand[...]).astype(BF16)
    blocks = query_blocks(starts_ref, pl.program_id(0))
    for head in range(heads):
        plain = proj[:, head * DN : (head + 1) * DN].astype(BF16)
        start = heads * DN + head * DR
        query = jnp.concatenate([plain, turn(proj[:, start : start + DR], cosine, sine).astype(BF16)], axis=1)
        start = head * (DN + DV)
        key = jnp.concatenate([expanded[:, start : start + DN], key_rope], axis=1)
        value = expanded[:, start + DN : start + DN + DV]
        q_out[0, head] = query
        k_out[0, head] = key
        v_out[0, head] = value
        for first, keys, seen in blocks:
            rows = slice(first, first + PIECE)
            scores = jnp.where(seen, dot_nt(query[rows], key[:keys]) * scale, -1e30)
            peak = jnp.max(scores, axis=1, keepdims=True)
            expo = jnp.exp(scores - peak)
            total = jnp.sum(expo, axis=1, keepdims=True)
            weights = (expo * (1.0 / total)).astype(BF16)
            out[rows, head * DV : (head + 1) * DV] = dot(weights, value[:keys]).astype(BF16)
            logs[0, head, rows] = peak + jnp.log(total)


def attention_forward(starts, proj, rows_scale, latent, gain, w_expand, cosine, sine, heads):
    band = proj.shape[0]
    seqs = band // SEQ_LEN

    def rows(width):
        return pl.BlockSpec((SEQ_LEN, width), lambda s, p: (s, 0))

    def whole(shape):
        return pl.BlockSpec(shape, lambda s, p: (0, 0))

    def by_head(width):
        return pl.BlockSpec((1, heads, SEQ_LEN, width), lambda s, p: (s, 0, 0, 0))

    def head_shape(width, kind=BF16):
        return jax.ShapeDtypeStruct((seqs, heads, SEQ_LEN, width), kind)

    return pl.pallas_call(
        functools.partial(attention_kernel, heads),
        grid_spec=pltpu.PrefetchScalarGridSpec(
            num_scalar_prefetch=1,
            grid=(seqs,),
            in_specs=[
                rows(proj.shape[1]),
                rows(1),
                rows(L + DR),
                whole((1, L)),
                whole(w_expand.shape),
                whole((SEQ_LEN, DR)),
                whole((SEQ_LEN, DR)),
            ],
            out_specs=[rows(heads * DV), by_head(1), by_head(DN + DR), by_head(DN + DR), by_head(DV), rows(L)],
        ),
        out_shape=[
            jax.ShapeDtypeStruct((band, heads * DV), BF16),
            head_shape(1, F32),
            head_shape(DN + DR),
            head_shape(DN + DR),
            head_shape(DV),
            jax.ShapeDtypeStruct((band, L), BF16),
        ],
        compiler_params=params(),
        cost_estimate=cost(12),
        name="attention",
    )(starts, proj, rows_scale, latent, gain[None], w_expand, cosine, sine)


def longer(total, part):
    if total is None:
        return part
    rows = total.shape[0]
    if rows == part.shape[0]:
        return total + part
    return jnp.concatenate([total + part[:rows], part[rows:]], axis=0)


def attention_back_kernel(heads, starts_ref, q_ref, k_ref, v_ref, logs, grad, w_expand, cos, sin, dq_out, de_out, dl_out):
    scale = (DN + DR) ** (-0.5)
    cosine, sine = cos[...], -sin[...]
    blocks = query_blocks(starts_ref, pl.program_id(0))
    rope = None
    latent = None
    for head in range(heads):
        query, key, value = q_ref[0, head], k_ref[0, head], v_ref[0, head]
        grad_here = grad[:, head * DV : (head + 1) * DV]
        grad_key = grad_value = None
        for first, keys, seen in blocks:
            rows = slice(first, first + PIECE)
            scores = jnp.where(seen, dot_nt(query[rows], key[:keys]) * scale, -1e30)
            weights = jnp.exp(scores - logs[0, head, rows])
            grad_weights = dot_nt(grad_here[rows], value[:keys])
            centre = jnp.sum(weights * grad_weights, axis=1, keepdims=True)
            grad_scores = (weights * (grad_weights - centre)).astype(BF16)
            grad_query = dot(grad_scores, key[:keys]) * scale
            dq_out[rows, head * DN : (head + 1) * DN] = grad_query[:, :DN].astype(BF16)
            start = heads * DN + head * DR
            turned = turn(grad_query[:, DN:], cosine[rows], sine[rows])
            dq_out[rows, start : start + DR] = turned.astype(BF16)
            grad_key = longer(grad_key, dot_tn(grad_scores, query[rows]))
            grad_value = longer(grad_value, dot_tn(weights.astype(BF16), grad_here[rows]))
        grad_key = grad_key * scale
        part = turn(grad_key[:, DN:], cosine, sine)
        rope = part if rope is None else rope + part
        both = jnp.concatenate([grad_key[:, :DN].astype(BF16), grad_value.astype(BF16)], axis=1)
        start = head * (DN + DV)
        de_out[:, start : start + DN + DV] = both
        part = dot_nt(both, w_expand[:, start : start + DN + DV])
        latent = part if latent is None else latent + part
    dl_out[:, :L] = latent.astype(BF16)
    dl_out[:, L:] = rope.astype(BF16)


def attention_backward(starts, query, key, value, logs, grad, w_expand, cosine, sine):
    seqs, heads = query.shape[:2]
    band = seqs * SEQ_LEN

    def rows(width):
        return pl.BlockSpec((SEQ_LEN, width), lambda s, p: (s, 0))

    def whole(shape):
        return pl.BlockSpec(shape, lambda s, p: (0, 0))

    def by_head(width):
        return pl.BlockSpec((1, heads, SEQ_LEN, width), lambda s, p: (s, 0, 0, 0))

    widths = (heads * (DN + DR), heads * (DN + DV), L + DR)
    return pl.pallas_call(
        functools.partial(attention_back_kernel, heads),
        grid_spec=pltpu.PrefetchScalarGridSpec(
            num_scalar_prefetch=1,
            grid=(seqs,),
            in_specs=[
                by_head(DN + DR),
                by_head(DN + DR),
                by_head(DV),
                by_head(1),
                rows(heads * DV),
                whole(w_expand.shape),
                whole((SEQ_LEN, DR)),
                whole((SEQ_LEN, DR)),
            ],
            out_specs=[rows(width) for width in widths],
        ),
        out_shape=[jax.ShapeDtypeStruct((band, width), BF16) for width in widths],
        compiler_params=params(),
        cost_estimate=cost(14),
        name="attention_back",
    )(starts, query, key, value, logs, grad, w_expand, cosine, sine)


def norm_products_kernel(picks_ref, *refs):
    query, latent = refs[:5], refs[5:10]
    weight, whole_out, part_out = refs[10:]
    half = query[3].shape[0]

    def write(number, start, query_rows, latent_rows):
        both = jnp.concatenate([query_rows, latent_rows], axis=1)
        place_of = pl.ds(picks_ref[number], 1)
        whole_out[place_of, start : start + half] = both[None]
        part_out[place_of, start : start + half] = dot_nt(both, weight[...]).astype(BF16)[None]

    for number in range(3):
        for start in (0, half):
            rows = slice(start, start + half)
            write(number, start, query[number][rows], latent[number][rows])
    write(3, 0, query[3][...], latent[3][...])
    write(3, half, query[4][...], latent[4][...])


def norm_products(query, latent, weight, picks):
    rows = query[0].shape[0]
    width = weight.shape[1]
    vmem = pl.BlockSpec(memory_space=pltpu.VMEM)
    return pl.pallas_call(
        norm_products_kernel,
        in_specs=[pl.BlockSpec(memory_space=pltpu.SMEM)] + [vmem] * 11,
        out_specs=[vmem, vmem],
        out_shape=[
            jax.ShapeDtypeStruct((4, rows, width), BF16),
            jax.ShapeDtypeStruct((4, rows, weight.shape[0]), BF16),
        ],
        compiler_params=params(),
        cost_estimate=cost(8),
        name="norm_products",
    )(picks, *query, *latent, weight)


def norm_backward(value, scale, gain, grad_norm, row_total, width):
    return (
        scale[:, None] * gain * grad_norm - value * (scale**3 / width)[:, None] * row_total[:, None]
    )


def widen(value, width):
    return jnp.pad(value, ((0, 0), (0, width - value.shape[1])))


def up_to(width):
    return 128 * ((width + 127) // 128)


def per_device(
    hidden_in,
    expert_routes,
    piece_starts,
    query_weight,
    latent_weight,
    latent_gain,
    expand_weight,
    output_weight,
    attention_gain,
    ffn_gain,
    router_weight,
    gate_weight,
    up_weight,
    down_weight,
    shared_gate,
    shared_up,
    shared_down,
    grad_out,
):
    row_parts = lax.axis_size("gx")
    column_parts = lax.axis_size("gy")
    here_x = lax.axis_index("gx")
    here_y = lax.axis_index("gy")
    local_rows, local_width = hidden_in.shape
    all_tokens = local_rows * column_parts
    band_rows = all_tokens // row_parts
    head_width = query_weight.shape[1]
    heads_here = head_width // (DN + DR)
    latent_width = latent_weight.shape[1]
    experts_here = gate_weight.shape[0]
    shared_width = shared_gate.shape[1]
    cap = 16 * ((local_rows * TOPK * 5 + 64 * EXPERTS - 1) // (64 * EXPERTS))
    blocks = column_parts
    quarter_blocks = blocks // row_parts
    quarter_slots = quarter_blocks * cap
    on_square = square()
    if on_square:
        order_of = numbers(here_x, here_x ^ 1, here_x ^ 2, here_x ^ 3)
    else:
        order_of = jnp.arange(row_parts, dtype=jnp.int32)

    waited.clear()
    hidden_all = spread_rows(hidden_in)
    hidden = hidden_in.astype(F32)
    grad_top = grad_out.astype(F32)
    wide = up_to(shared_width)
    shared_weight = side_by_side(shared_gate, shared_up, shared_down, wide)
    scale_one = lax.rsqrt(feature_total(jnp.sum(hidden * hidden, axis=1)) / D + EPS)
    sent = jnp.concatenate([expert_routes.T.astype(F32), scale_one[None]], axis=0)
    gathered = jnp.broadcast_to(sent[None], (column_parts,) + sent.shape)
    gathered = lax.all_to_all(gathered, "gy", split_axis=0, concat_axis=0, tiled=True)
    grad_top_tokens = to_tokens(after(grad_out, gathered))
    gathered = gathered.transpose(1, 0, 2).reshape(TOPK + 1, all_tokens)
    routes_all = gathered[:TOPK].astype(jnp.int32)
    scale_one_all = gathered[TOPK]
    mine = here_y * experts_here + jnp.arange(experts_here, dtype=jnp.int32)
    named = jnp.any(routes_all[:, :, None] == mine[None, None, :], axis=0)
    named_blocks = named.astype(BF16).reshape(blocks, local_rows, experts_here)
    order = jnp.arange(local_rows, dtype=jnp.int32)
    earlier = (order[None, :] < order[:, None]).astype(BF16)
    slot = jnp.einsum("ts,bse->bte", earlier, named_blocks, preferred_element_type=F32)
    code = jnp.where(named, slot.reshape(all_tokens, experts_here), -1.0)
    chosen = one_hot(code, cap, blocks)
    code_here = pick(code.reshape(row_parts, quarter_blocks, local_rows, experts_here), here_x, 0)
    spots = jnp.arange(cap, dtype=jnp.int32).astype(F32)
    at_slot = code_here[:, :, :, None] == spots
    by_head = query_weight.reshape(-1, heads_here, DN + DR)
    used = head_width + latent_width
    in_weight = jnp.concatenate(
        [
            by_head[:, :, :DN].reshape(-1, heads_here * DN),
            by_head[:, :, DN:].reshape(-1, heads_here * DR),
            widen(latent_weight, up_to(used) - head_width),
        ],
        axis=1,
    )
    cosine, sine = rope_tables(SEQ_LEN)
    if on_square:
        shared_weight = after(shared_weight, gathered)
        shared_x, shared_y = swap(shared_weight, 1), swap(shared_weight, 2)
        hidden_all, shared_x, shared_y, chosen = together(hidden_all, shared_x, shared_y, chosen)
    hidden_all, in_weight, cosine, sine = together(hidden_all, in_weight, cosine, sine)

    gained_one_all = (hidden_all.astype(F32) * attention_gain).astype(BF16)
    projected = band_total(gained_one_all, in_weight, 1)
    band_one = pick(scale_one_all.reshape(row_parts, band_rows), here_x, 0)[:, None]
    grad_top_all = spread_rows(after(grad_out, hidden_all))
    latent_part = (projected[:, head_width:used] * band_one).astype(BF16)
    latent_part = after(latent_part, grad_top_all)
    latent_all = lax.all_gather(latent_part, "gy", axis=1, tiled=True)


    if on_square:
        middle = shared_weight.shape[0] // 2
        shared_x, shared_y = after((shared_x, shared_y), latent_part)
        far = swap(shared_y[:middle], 1), swap(shared_x[middle:], 2)
    else:
        weights_of_shared = (lax.all_gather(shared_weight, "gx", axis=0, tiled=True),)
    grad_top_band = spread_rows(after(grad_top_tokens, latent_all))

    attended, logs, query_seq, key_seq, value_seq, latent_norm = attention_forward(
        piece_starts, projected, band_one, latent_all, latent_gain, expand_weight, cosine, sine, heads_here
    )
    if on_square:
        attended, *far = together(attended, *far)
        weights_of_shared = (shared_weight, shared_x, shared_y, *far)
    grad_rows = dispatch(after(chosen, attended), grad_top_all, cap, blocks)
    grad_rows = grad_rows.reshape(experts_here, row_parts, quarter_slots, -1)
    attended_all = after(collect_rows(attended), grad_rows)
    attention_part = dot(attended_all, output_weight).astype(BF16)
    after_attention = hidden + outer_total(attention_part).astype(F32)

    if on_square:
        half = experts_here // 2
        rows = after(grad_rows, attention_part, grad_top_band)
        grad_hidden_low = square_sum(rows, down_weight, 0, half, 2, True, False, BF16)
        after_attention = after(after_attention, grad_hidden_low)

    gained = (after_attention * ffn_gain).astype(BF16)
    gained_all = spread_rows(gained)
    gained_tokens = to_tokens(gained)
    gained_band = spread_rows(gained_tokens)
    squares = jnp.sum(after_attention * after_attention, axis=1)[None]
    logits = lax.dot_general(
        router_weight, gained, (((0,), (1,)), ((), ())), preferred_element_type=F32
    )
    totals = jnp.concatenate([logits, squares, jnp.zeros((7, local_rows), F32)], axis=0)
    if on_square:
        norm_one_all = hidden_all.astype(F32) * scale_one_all[:, None] * attention_gain
        norm_one_all = after(norm_one_all.astype(BF16), totals)
        rows, norm_one_all = together(after(grad_rows, totals), norm_one_all)
        grad_hidden_high = square_sum(rows, down_weight, half, half, 3, True, False, BF16)
    totals = square_total(totals)
    scale_two = lax.rsqrt(totals[EXPERTS] / D + EPS)
    probs_across = jax.nn.softmax(totals[:EXPERTS] * scale_two[None], axis=0)
    probs = probs_across.T
    norm_two = (after_attention * scale_two[:, None] * ffn_gain).astype(BF16)
    sent = jnp.concatenate(
        [
            probs_across.reshape(column_parts, experts_here, local_rows),
            jnp.broadcast_to(scale_two[None, None], (column_parts, 1, local_rows)),
        ],
        axis=1,
    )
    received = lax.all_to_all(sent, "gy", split_axis=0, concat_axis=0, tiled=True)
    received = received.transpose(0, 2, 1)
    scale_two_all = received[:, :, experts_here].reshape(all_tokens)
    received = pick(received.reshape(row_parts, quarter_blocks, local_rows, experts_here + 1), here_x, 0)
    factors = jnp.stack(
        [
            jnp.sum(jnp.where(at_slot, value[:, :, :, None], 0.0), axis=1)
            .transpose(1, 0, 2)
            .reshape(experts_here, quarter_slots)
            for value in (received[:, :, :experts_here], received[:, :, experts_here:])
        ],
        axis=2,
    )
    if on_square:
        gained_all, factors = lax.optimization_barrier((gained_all, factors, grad_hidden_high))[:2]
    rows_two, slot_scale = dispatch(chosen, gained_all, cap, blocks, scale_two_all[:, None])
    rows_two = rows_two.reshape(experts_here, row_parts, quarter_slots, -1)
    slot_scale = slot_scale.reshape(experts_here, row_parts, quarter_slots, 1)

    band_scale = scale_two_all.reshape(blocks, row_parts, -1)
    band_scale = pick(band_scale, here_x, 1).reshape(-1, 1)
    shared_hidden, grad_shared_both, grad_shared_part, shared_part = shared_experts(
        after(gained_band, rows_two), band_scale, grad_top_band, weights_of_shared, order_of
    )
    grad_norm_shared = outer_total(grad_shared_part)
    shared_out = outer_total(shared_part)

    both_weights = (gate_weight, up_weight)
    if on_square:
        own, from_x, from_y, across, scaled, grad_norm_part, slot_grad, pair_x, pair_y = routed_experts(
            after(rows_two, shared_part), gate_weight, up_weight, grad_hidden_low, grad_hidden_high, factors, chosen, blocks
        )
        whole = [(own, 0), (from_x, 0), (from_y, 0), (across, 0)]
        grad_groups = [(0, experts_here, whole)]
    else:
        everything = order_of

        def whole_total(rows, weight, transposed):
            out = group(rows, everything, row_parts, (weight,), 0, experts_here, transposed)
            out = out.reshape((experts_here,) + out.shape[2:])
            return lax.psum_scatter(out, "gx", scatter_dimension=1, tiled=True)[:, 0].astype(F32)

        scale = factors[:, :, 1:2]
        scaled, grad_gate_pre, grad_up_pre, slot_grad = expert_body(
            whole_total(rows_two, gate_weight, False) * scale,
            whole_total(rows_two, up_weight, False) * scale,
            whole_total(grad_rows, down_weight, True),
            factors[:, :, 0:1],
        )
        grads = jnp.stack([grad_gate_pre, grad_up_pre], axis=1)
        whole = lax.all_gather(grads, "gx", axis=0, tiled=False)
        grad_groups = [(0, experts_here, [(whole[q], 0) for q in range(row_parts)])]
        whole = lax.all_gather(scaled[:, None], "gx", axis=0, tiled=False)
        hidden_groups = [(0, experts_here, [(whole[q], 0) for q in range(row_parts)])]

        back_rows = back(grad_groups, order_of, both_weights, True)
        back_rows = back_rows.reshape(experts_here, blocks * cap, -1)
        grad_norm_part = combine(chosen, [back_rows], cap, blocks)

    grad_norm_part = after(grad_norm_part, shared_out)
    grad_norm_routed = outer_total(grad_norm_part)

    both_shared = after(jnp.stack([grad_norm_shared, shared_out]), grad_norm_part)
    both_shared = lax.all_to_all(both_shared, "gx", split_axis=2, concat_axis=1, tiled=True)
    grad_norm_shared, shared_out = both_shared[0].astype(F32), both_shared[1].astype(F32)
    if on_square:
        scaled = after(scaled, grad_norm_shared)
        low, high = scaled[2:half], scaled[half:]
        low_x, low_y, high_x, high_y = swap(low, 1), swap(low, 2), swap(high, 1), swap(high, 2)
    slot_grad = after(slot_grad, grad_norm_part)
    slot_grad = slot_grad.reshape(experts_here, quarter_blocks, cap).transpose(1, 0, 2)
    grad_probs = jnp.sum(jnp.where(at_slot, slot_grad[:, None], 0.0), axis=3)
    grad_probs = grad_probs.reshape(band_rows, experts_here)
    grad_probs = collect(grad_probs.T).transpose(0, 2, 1).reshape(blocks, local_rows, experts_here)
    grad_probs = lax.all_to_all(grad_probs, "gy", split_axis=0, concat_axis=2, tiled=True)
    grad_probs = grad_probs.reshape(local_rows, EXPERTS)
    centre = jnp.sum(probs * grad_probs, axis=1, keepdims=True)
    grad_logits = (probs * (grad_probs - centre)).astype(BF16)
    grad_norm_router = dot_nt(grad_logits, router_weight)
    grad_router_part = dot_tn(norm_two, grad_logits)
    grad_norm_routed, grad_norm_router = together(grad_norm_routed, grad_norm_router)
    grad_norm_two = grad_norm_routed.astype(F32) + grad_norm_shared + grad_norm_router

    scaled_after = after_attention * ffn_gain
    row_two = jnp.sum(scaled_after * grad_norm_two, axis=1)
    if on_square and local_rows == 512:
        row_two = small_totals(jnp.pad(row_two.reshape(4, 128), ((0, 4), (0, 0))), None, 4)[0][:4].reshape(-1)
    else:
        row_two = feature_total(row_two)
    grad_after = grad_top + norm_backward(
        after_attention, scale_two, ffn_gain, grad_norm_two, row_two, D
    )
    grad_ffn_part = jnp.sum(grad_norm_two * after_attention * scale_two[:, None], axis=0)
    grad_after_sent = grad_after.astype(BF16)
    grad_after_all = spread_rows(grad_after_sent)

    grad_router = tower_step(after(grad_router_part, grad_after_sent), 0)
    grad_after_all, grad_router = together(grad_after_all, grad_router)
    waiting = after(rows_two, grad_after_sent)
    grad_gate, grad_up = weight_grad(waiting, grad_groups, order_of, False, slot_scale)
    grad_shared = shared_weights(
        after(gained_band, grad_gate), grad_shared_both, grad_top_band, shared_hidden
    )
    grad_after_all, grad_gate, grad_up, grad_shared = together(
        grad_after_all, grad_gate, grad_up, grad_shared
    )
    if on_square:
        grad_after_all, low_x, low_y, high_x, high_y = together(
            grad_after_all, low_x, low_y, high_x, high_y
        )

    grad_attended = band_total(grad_after_all, output_weight, 6, True, BF16)
    if on_square:
        pair_far, low_y, high_x = after((pair_y, low_y, high_x), grad_attended)
        pair_far, low_far, high_far = swap(pair_far, 1), swap(low_y, 1), swap(high_x, 2)
        hidden_groups = [
            (0, 2, [(scaled, 0), (pair_x, 0), (pair_y, 0), (pair_far, 0)]),
            (2, half - 2, [(low, 0), (low_x, 0), (low_y, 0), (low_far, 0)]),
            (half, half, [(high, 0), (high_x, 0), (high_y, 0), (high_far, 0)]),
        ]
    grad_query_pre, grad_expanded, latent_grads = attention_backward(
        piece_starts, query_seq, key_seq, value_seq, logs, grad_attended, expand_weight, cosine, sine
    )
    own_rows = band_rows // column_parts
    latent_sums = outer_total(latent_grads).astype(F32)
    grad_router = tower_step(after(grad_router, latent_grads), 1)
    expand_part = dot_tn(latent_norm, grad_expanded).astype(BF16)
    if on_square:
        expand_away = swap(expand_part, 1)

    if on_square:
        query_x, query_y = swap(grad_query_pre, 1), swap(grad_query_pre, 2)
    waiting = after(down_weight, latent_grads)
    out = back(hidden_groups, order_of, (waiting,), False)
    if on_square:
        out, query_x, query_y = together(out, query_x, query_y)
        middle = band_rows // 2
        far = swap(query_y[:middle], 1), swap(query_x[middle:], 2)
        query_blocks = (grad_query_pre, query_x, query_y, *far)
    out = out.reshape(experts_here, blocks * cap, -1)
    routed_part = combine(chosen, [out], cap, blocks)
    if on_square:
        routed_part, expand_away = together(routed_part, expand_away)
        expand_x = expand_part + expand_away
    routed_part, grad_router = together(routed_part, grad_router)
    latent_sums, routed_part = together(latent_sums, routed_part)
    routed = outer_total(routed_part)
    latent_f32 = lax.dynamic_slice_in_dim(latent_all, here_y * own_rows, own_rows, 0).astype(F32)
    compressed = latent_f32[:, :L]
    latent_scale = lax.rsqrt(jnp.mean(compressed * compressed, axis=1) + EPS)
    grad_latent_norm, grad_rope_key = latent_sums[:, :L], latent_sums[:, L:]
    latent_row = jnp.sum(compressed * latent_gain * grad_latent_norm, axis=1)
    grad_compressed = norm_backward(
        compressed, latent_scale, latent_gain, grad_latent_norm, latent_row, L
    )
    grad_gain_part = jnp.sum(grad_latent_norm * compressed * latent_scale[:, None], axis=0)
    grad_latent_pre = jnp.concatenate([grad_compressed, grad_rope_key], axis=1).astype(BF16)
    grad_latent_own = grad_latent_pre.reshape(own_rows, column_parts, latent_width).transpose(1, 0, 2)
    grad_latent_own = lax.all_to_all(grad_latent_own, "gy", split_axis=0, concat_axis=0, tiled=True)
    if on_square:
        expand_y = swap(after(expand_x, grad_latent_pre), 2)
        grad_latent_own, expand_y = together(grad_latent_own, expand_y)
    grad_latent_own = grad_latent_own.reshape(band_rows, latent_width)
    grad_latent_own = widen(grad_latent_own, up_to(used) - head_width)
    if on_square:
        latent_blocks = (grad_latent_own, *from_others(grad_latent_own))
        grad_projected_all, grad_norm_part = norm_products(
            query_blocks, latent_blocks, in_weight, order_of
        )
        grad_projected_all = grad_projected_all.reshape(all_tokens, -1)
        grad_norm_part = grad_norm_part.reshape(all_tokens, -1)
    else:
        grad_projected = jnp.concatenate([grad_query_pre, grad_latent_own], axis=1)
        grad_projected_all = collect_rows(grad_projected)
        grad_norm_part = dot_nt(grad_projected_all, in_weight).astype(BF16)
    grad_norm_one = outer_total(grad_norm_part).astype(F32)

    mixed = (after_attention + routed.astype(F32) + shared_out).astype(BF16)
    if not on_square:
        norm_one_all = hidden_all.astype(F32) * scale_one_all[:, None] * attention_gain
        norm_one_all = norm_one_all.astype(BF16)
    norm_one_all = after(norm_one_all, grad_norm_part)
    grad_projected = dot_tn(norm_one_all, grad_projected_all)
    grad_query = grad_projected[:, :head_width]
    grad_query = jnp.concatenate(
        [
            grad_query[:, : heads_here * DN].reshape(-1, heads_here, DN),
            grad_query[:, heads_here * DN :].reshape(-1, heads_here, DR),
        ],
        axis=2,
    ).reshape(-1, head_width)
    grad_latent = grad_projected[:, head_width:used]
    grad_output = dot_tn(attended_all, after(grad_after_all, grad_norm_part))
    if on_square:
        grad_expand = expand_x.astype(F32) + expand_y.astype(F32)
    else:
        grad_expand = lax.psum(expand_part, "gx").astype(F32)
    grad_router = tower_step(tower_step(after(grad_router, grad_norm_part), 2), 3)
    grad_shared = inner_rows(after(grad_shared, grad_norm_part))
    (grad_down,) = weight_grad(after(grad_rows, grad_norm_part), hidden_groups, order_of, True)
    grad_norm_one, grad_query, grad_latent, grad_output, grad_expand, grad_down = together(
        grad_norm_one, grad_query, grad_latent, grad_output, grad_expand, grad_down
    )
    row_one = jnp.sum(hidden * attention_gain * grad_norm_one, axis=1)
    grad_attention_part = jnp.sum(grad_norm_one * hidden * scale_one[:, None], axis=0)
    if on_square and local_rows == 512 and local_width == 512:
        inner = jnp.concatenate([row_one, grad_gain_part]).reshape(8, 128)
        outer = jnp.concatenate([grad_attention_part, grad_ffn_part]).reshape(8, 128)
        inner, outer = small_totals(inner, outer, 5)
        row_one = inner[:4].reshape(-1)
        grad_attention_gain = outer[:4].reshape(-1)
        grad_ffn_gain = outer[4:8].reshape(-1)
        grad_latent_gain = outer[12:].reshape(-1)
    else:
        row_one, grad_latent_gain = feature_total((row_one, grad_gain_part))
        grad_attention_gain, grad_ffn_gain, grad_latent_gain = lax.psum(
            (grad_attention_part, grad_ffn_part, grad_latent_gain), "gy"
        )
    grad_hidden = grad_after + norm_backward(
        hidden, scale_one, attention_gain, grad_norm_one, row_one, D
    )
    grad_shared_gate, grad_shared_up, grad_shared_down = shared_sums(
        after(grad_shared, row_one), shared_width
    )
    grad_shared_gate, grad_shared_up = grad_shared_gate.T, grad_shared_up.T
    grad_latent_gain = settle(grad_latent_gain)
    return (
        mixed,
        grad_hidden,
        grad_query,
        grad_latent,
        grad_latent_gain,
        grad_expand,
        grad_output,
        grad_attention_gain,
        grad_ffn_gain,
        grad_router,
        grad_gate,
        grad_up,
        grad_down,
        grad_shared_gate,
        grad_shared_up,
        grad_shared_down,
    )


def solution(mesh):
    return jax.shard_map(
        per_device,
        mesh=mesh,
        in_specs=(
            P("gy", "gx"),
            P("gy", None),
            P("gx", None),
            P("gx", "gy"),
            P("gx", "gy"),
            P(),
            P(None, "gy"),
            P("gy", "gx"),
            P("gx"),
            P("gx"),
            P("gx", None),
            P("gy", "gx", None),
            P("gy", "gx", None),
            P("gy", None, "gx"),
            P("gx", "gy"),
            P("gx", "gy"),
            P("gy", "gx"),
            P("gy", "gx"),
        ),
        out_specs=(
            P("gy", "gx"),
            P("gy", "gx"),
            P("gx", "gy"),
            P("gx", "gy"),
            P(),
            P(None, "gy"),
            P("gy", "gx"),
            P("gx"),
            P("gx"),
            P("gx", None),
            P("gy", "gx", None),
            P("gy", "gx", None),
            P("gy", None, "gx"),
            P("gx", "gy"),
            P("gx", "gy"),
            P("gy", "gx"),
        ),
        check_vma=False,
    )
```

```python
import functools
import math

import jax
import jax.numpy as jnp
from jax import lax
from jax.experimental import pallas as pl
from jax.experimental.pallas import tpu as pltpu
from jax.sharding import PartitionSpec as P

D = 2048
DN = 128
DR = 64
DV = 128
L = 512
EXPERTS = 64
FF = 1408
TOPK = 6
SEQ_LEN = 1024
PIECE = 256


EPS = 1e-06
BF16 = jnp.bfloat16
F32 = jnp.float32
VMEM_LIMIT = 56 * 1024 * 1024


def params():
    return pltpu.CompilerParams(vmem_limit_bytes=VMEM_LIMIT)


def cost(microseconds):
    return pl.CostEstimate(flops=int(microseconds * 0.575e9), bytes_accessed=0, transcendentals=0)


waited = []


def after(value, *others):
    value, others = lax.optimization_barrier((value, others))
    waited.extend(jax.tree.leaves(others))
    return value


def together(*values):
    return lax.optimization_barrier(values)


def settle_kernel(value, *refs):
    refs[-1][...] = value[...]


def settle(value):
    vmem = pl.BlockSpec(memory_space=pltpu.VMEM)
    return pl.pallas_call(
        settle_kernel,
        in_specs=[vmem] + [pl.BlockSpec(memory_space=pl.ANY)] * len(waited),
        out_specs=vmem,
        out_shape=jax.ShapeDtypeStruct(value.shape, value.dtype),
        cost_estimate=cost(1),
        name="settle",
    )(value, *waited)


def swap(value, bit):
    return lax.ppermute(value, "gx", [(i, i ^ bit) for i in range(4)])


def square():
    return lax.axis_size("gx") == 4


def place():
    me = lax.axis_index("gx")
    return me & 1, me >> 1


def pick(value, index, axis):
    return lax.dynamic_index_in_dim(value, index, axis, keepdims=False)


def from_others(block):
    half = block.shape[0] // 2
    from_x = swap(block, 1)
    from_y = swap(block, 2)
    return from_x, from_y, swap(from_y[:half], 1), swap(from_x[half:], 2)


def collect(block):
    if not square():
        return lax.all_gather(block, "gx", axis=0, tiled=False)
    return stacked(block, *from_others(block))


def stacked(block, from_x, from_y, low, high):
    across = jnp.concatenate([low, high], axis=0)
    me = lax.axis_index("gx")
    whole = jnp.zeros((4,) + block.shape, block.dtype)
    for index, value in ((me, block), (me ^ 1, from_x), (me ^ 2, from_y), (me ^ 3, across)):
        whole = lax.dynamic_update_index_in_dim(whole, value, index, 0)
    return whole


def collect_rows(block):
    whole = collect(block)
    return whole.reshape((-1,) + block.shape[1:])


def feature_total(value):
    return lax.psum(value, "gx")


def square_total(value):
    if not square():
        return lax.psum(value, "gx")
    value = value + swap(value, 1)
    return value + swap(value, 2)


def inner_rows(value):
    parts = lax.axis_size("gx")
    value = value.reshape(parts, -1, value.shape[1])
    return lax.all_to_all(value, "gx", split_axis=0, concat_axis=0, tiled=True)


def tower_step(value, step):
    size, bit = lax.axis_size("gy"), 2**step
    if bit >= size:
        return value
    return value + lax.ppermute(value, "gy", [(i, i ^ bit) for i in range(size)])


def spread_rows(value):
    return lax.all_gather(value, "gy", axis=0, tiled=True)


def outer_total(partial):
    return lax.psum_scatter(partial.astype(BF16), "gy", scatter_dimension=0, tiled=True)


def to_tokens(value):
    return lax.all_to_all(value, "gx", split_axis=0, concat_axis=1, tiled=True)


def to_features(value):
    return lax.all_to_all(value, "gx", split_axis=1, concat_axis=0, tiled=True)


def dot(a, b):
    return jnp.dot(a, b, preferred_element_type=F32)


def dot_nt(a, b):
    return lax.dot_general(a, b, (((1,), (1,)), ((), ())), preferred_element_type=F32)


def dot_tn(a, b):
    return lax.dot_general(a, b, (((0,), (0,)), ((), ())), preferred_element_type=F32)


def one_hot_kernel(cap, code_ref, out_ref):
    experts = code_ref.shape[1]
    tokens, slots = out_ref.shape
    column = lax.broadcasted_iota(jnp.int32, (experts, slots), 1)
    low = lax.broadcasted_iota(jnp.int32, (experts, slots), 0) * cap
    inside = (column >= low) & (column < low + cap)
    expand = jnp.where(inside, 1.0, 0.0).astype(BF16)
    offset = jnp.sum(jnp.where(inside, column - low, 0).astype(F32), axis=0, keepdims=True)
    wide = dot(code_ref[...].astype(BF16), expand)
    out_ref[...] = jnp.where(wide == offset, 1.0, 0.0).astype(BF16)


def one_hot(code, cap, blocks):
    tokens, experts = code.shape
    block = tokens // blocks
    return pl.pallas_call(
        functools.partial(one_hot_kernel, cap),
        grid=(blocks,),
        in_specs=[pl.BlockSpec((block, experts), lambda b: (b, 0))],
        out_specs=pl.BlockSpec((block, experts * cap), lambda b: (b, 0)),
        out_shape=jax.ShapeDtypeStruct((tokens, experts * cap), BF16),
        compiler_params=params(),
        cost_estimate=cost(7),
        name="one_hot",
    )(code)


def dispatch_kernel(chosen_ref, rows_ref, out_ref):
    moved = dot_tn(chosen_ref[...], rows_ref[...]).astype(BF16)
    out_ref[...] = moved.reshape(out_ref.shape)


def dispatch_scaled_kernel(chosen_ref, rows_ref, scale_ref, out_ref, scale_out_ref):
    dispatch_kernel(chosen_ref, rows_ref, out_ref)
    high, middle, low = thirds(scale_ref[...])
    parts = jnp.concatenate([high, middle, low], axis=1)
    moved = dot_tn(chosen_ref[...], parts)
    moved = moved[:, 0:1] + moved[:, 1:2] + moved[:, 2:3]
    scale_out_ref[...] = moved.reshape(scale_out_ref.shape)


def thirds(value):
    high = value.astype(BF16)
    rest = value - high.astype(F32)
    middle = rest.astype(BF16)
    return high, middle, (rest - middle.astype(F32)).astype(BF16)


def dispatch(chosen, rows, cap, blocks, scale=None):
    tokens, width = rows.shape
    slots = chosen.shape[1]
    experts = slots // cap
    block = tokens // blocks
    specs = [
        pl.BlockSpec((block, slots), lambda b: (b, 0)),
        pl.BlockSpec((block, width), lambda b: (b, 0)),
    ]
    out_specs = [pl.BlockSpec((experts, cap, width), lambda b: (0, b, 0))]
    shapes = [jax.ShapeDtypeStruct((experts, blocks * cap, width), BF16)]
    values = [chosen, rows]
    if scale is not None:
        specs.append(pl.BlockSpec((block, 1), lambda b: (b, 0)))
        out_specs.append(pl.BlockSpec((experts, cap, 1), lambda b: (0, b, 0)))
        shapes.append(jax.ShapeDtypeStruct((experts, blocks * cap, 1), F32))
        values.append(scale)
    outs = pl.pallas_call(
        dispatch_kernel if scale is None else dispatch_scaled_kernel,
        grid=(blocks,),
        in_specs=specs,
        out_specs=out_specs,
        out_shape=shapes,
        compiler_params=params(),
        cost_estimate=cost(10),
        name="dispatch",
    )(*values)
    return outs[0] if scale is None else outs


def combine_kernel(groups, chosen_ref, *refs):
    out_ref = refs[-1]
    width = out_ref.shape[1]
    pieces = [ref[...].reshape(-1, width) for ref in refs[:groups]]
    slots = pieces[0] if groups == 1 else jnp.concatenate(pieces, axis=0)
    total = dot(chosen_ref[...], slots)
    for ref in refs[groups:-1]:
        total += ref[...].astype(F32)
    out_ref[...] = total.astype(out_ref.dtype)


def combine(chosen, pieces, cap, blocks, extra=()):
    tokens, slots = chosen.shape
    block = tokens // blocks
    width = pieces[0].shape[-1]
    specs = [pl.BlockSpec((block, slots), lambda b: (b, 0))]
    specs += [pl.BlockSpec((p.shape[0], cap, width), lambda b: (0, b, 0)) for p in pieces]
    specs += [pl.BlockSpec((block, width), lambda b: (b, 0)) for _ in extra]
    return pl.pallas_call(
        functools.partial(combine_kernel, len(pieces)),
        grid=(blocks,),
        in_specs=specs,
        out_specs=pl.BlockSpec((block, width), lambda b: (b, 0)),
        out_shape=jax.ShapeDtypeStruct((tokens, width), BF16),
        compiler_params=params(),
        cost_estimate=cost(9),
        name="combine",
    )(chosen, *pieces, *extra)


def group_kernel(parts, weights, adds, transposed, picks_ref, *refs):
    rows = [ref[0, 0] for ref in refs[:parts]]
    source = rows[0] if parts == 1 else jnp.concatenate(rows, axis=0)
    out_ref = refs[-1]
    extra = refs[parts + weights : parts + weights + adds]
    for number in range(weights):
        weight = refs[parts + number][0]
        total = dot_nt(source, weight) if transposed else dot(source, weight)
        for ref in extra:
            total += ref[0, number, 0].astype(F32)
        out_ref[0, number] = total.astype(out_ref.dtype).reshape(out_ref.shape[2:])


def group(rows, picks, parts, weights, first, count, transposed=False, adds=(), kind=BF16, by_quarter=False):
    slots, depth = rows.shape[2:]
    width = weights[0].shape[1] if transposed else weights[0].shape[2]
    many = len(weights)

    def row_spec(part):
        if by_quarter:
            return pl.BlockSpec((1, 1, slots, depth), lambda e, p: (p[part], first + e, 0, 0))
        return pl.BlockSpec((1, 1, slots, depth), lambda e, p: (first + e, p[part], 0, 0))

    def add_spec(number):
        return pl.BlockSpec((1, many, 1, slots, width), lambda e, p: (e, 0, p[parts + number], 0, 0))

    specs = [row_spec(part) for part in range(parts)]
    for weight in weights:
        if by_quarter:
            specs.append(pl.BlockSpec((1,) + weight.shape[1:], lambda e, p: (0, 0, 0)))
        else:
            specs.append(pl.BlockSpec((1,) + weight.shape[1:], lambda e, p: (first + e, 0, 0)))
    specs += [add_spec(number) for number in range(len(adds))]
    return pl.pallas_call(
        functools.partial(group_kernel, parts, many, len(adds), transposed),
        grid_spec=pltpu.PrefetchScalarGridSpec(
            num_scalar_prefetch=1,
            grid=(count,),
            in_specs=specs,
            out_specs=pl.BlockSpec((1, many, parts, slots, width), lambda e, p: (e, 0, 0, 0, 0)),
        ),
        out_shape=jax.ShapeDtypeStruct((count, many, parts, slots, width), kind),
        compiler_params=params(),
        cost_estimate=cost(4),
        name="group",
    )(picks, *([rows] * parts), *weights, *adds)


def numbers(*values):
    return jnp.stack([jnp.asarray(value, jnp.int32) for value in values])


def halves(first, count):
    x, y = place()
    half = count // 2
    me = 2 * y + x
    return (
        (first, half, 1, numbers(1 - x, 3 - x), numbers(2 * (1 - y) + x, 1 - y), numbers(me, y, 0)),
        (first + half, half, 2, numbers(2 - 2 * y, 3 - 2 * y), numbers(2 * y + 1 - x, 1 - x), numbers(me, x, 0)),
    )


def expert_body(gate_pre, up_pre, grad_hidden, gate):
    sigma = jax.nn.sigmoid(gate_pre)
    act = gate_pre * sigma
    hidden = (act * up_pre).astype(BF16).astype(F32)
    grad_gate = jnp.sum(hidden * grad_hidden, axis=-1, keepdims=True)
    scaled = (gate * hidden).astype(BF16)
    grad = gate * grad_hidden
    grad_gate_pre = (grad * up_pre * sigma * (1.0 + gate_pre * (1.0 - sigma))).astype(BF16)
    grad_up_pre = (grad * act).astype(BF16)
    return scaled, grad_gate_pre, grad_up_pre, grad_gate


def neighbours():
    me = lax.axis_index("gx")
    x = me % 2
    y = me // 2
    return x, y, me + 1 - 2 * x, me + 2 - 4 * y


def greet(*others):
    barrier = pltpu.get_barrier_semaphore()
    for other in others:
        pl.semaphore_signal(
            barrier, inc=1, device_id={"gx": other}, device_id_type=pl.DeviceIdType.MESH
        )
    pl.semaphore_wait(barrier, len(others))


def remote(source, target, sent, received, other):
    return pltpu.make_async_remote_copy(
        src_ref=source,
        dst_ref=target,
        send_sem=sent,
        recv_sem=received,
        device_id={"gx": other},
        device_id_type=pl.DeviceIdType.MESH,
    )


def experts_kernel(
    rows,
    w_gate,
    w_up,
    grad_low,
    grad_high,
    factors,
    chosen,
    own_out,
    x_out,
    y_out,
    d_out,
    hid_out,
    tokens_out,
    gate_out,
    hidden_x_out,
    hidden_y_out,
    back_out,
    chosen_held,
    first_sent,
    first,
    second,
    weights,
    loaded,
    first_send,
    first_recv,
    second_send,
    second_recv,
    x_send,
    x_recv,
    y_send,
    y_recv,
    d_send,
    d_recv,
    own_sem,
    weight_sem,
    load_sem,
    chosen_sem,
    hidden_x_send,
    hidden_x_recv,
    hidden_y_send,
    hidden_y_recv,
):
    x, y, x_other, y_other = neighbours()
    me = 2 * y + x
    across = 3 - me
    pairs = rows.shape[0] // 2
    slots = rows.shape[2]
    greet(x_other, y_other)

    def side(odd):
        if odd:
            return y_other, x_other, (2 - 2 * y, 3 - 2 * y), 2 * y + 1 - x, 1 - x, x
        return x_other, y_other, (1 - x, 3 - x), 2 * (1 - y) + x, 1 - y, y

    def fetch(pair):
        for odd in range(2):
            expert = 2 * pair + odd
            pltpu.make_async_copy(w_gate.at[expert], weights.at[odd, 0], weight_sem.at[odd, 0]).start()
            pltpu.make_async_copy(w_up.at[expert], weights.at[odd, 1], weight_sem.at[odd, 1]).start()

    def fetched(pair, odd):
        expert = 2 * pair + odd
        pltpu.make_async_copy(w_gate.at[expert], weights.at[odd, 0], weight_sem.at[odd, 0]).wait()
        pltpu.make_async_copy(w_up.at[expert], weights.at[odd, 1], weight_sem.at[odd, 1]).wait()

    def first_copy(pair, odd):
        expert = 2 * pair + odd
        return remote(
            first_sent.at[pair % 2, odd],
            first.at[expert],
            first_send.at[expert],
            first_recv.at[expert],
            side(odd)[0],
        )

    def second_copy(pair, odd):
        expert = 2 * pair + odd
        return remote(
            first.at[expert, side(odd)[4]],
            second.at[expert],
            second_send.at[expert],
            second_recv.at[expert],
            side(odd)[1],
        )

    def x_copy(pair, odd):
        expert = 2 * pair + odd
        source = first.at[expert, side(odd)[5]]
        return remote(source, x_out.at[expert], x_send.at[expert], x_recv.at[expert], x_other)

    def y_copy(pair, odd):
        expert = 2 * pair + odd
        source = first.at[expert, side(odd)[5]]
        return remote(source, y_out.at[expert], y_send.at[expert], y_recv.at[expert], y_other)

    def own_copy(pair, odd):
        expert = 2 * pair + odd
        return pltpu.make_async_copy(
            first.at[expert, side(odd)[5]], own_out.at[expert], own_sem.at[expert]
        )

    def far_copy(pair, odd):
        expert = 2 * pair + odd
        source = x_out if odd else y_out
        return remote(
            source.at[expert],
            d_out.at[expert],
            d_send.at[expert],
            d_recv.at[expert],
            side(odd)[0],
        )

    def send_first(pair):
        fetch(pair)
        for odd in range(2):
            expert = 2 * pair + odd

            @pl.when(pair >= 2)
            def _(odd=odd):
                first_copy(pair - 2, odd).wait_send()

            low, high = side(odd)[2]
            source = jnp.concatenate([rows[expert, low], rows[expert, high]], axis=0)
            fetched(pair, odd)
            for number in range(2):
                out = dot(source, weights[odd, number]).astype(BF16)
                first_sent[pair % 2, odd, 0, number] = out[:slots]
                first_sent[pair % 2, odd, 1, number] = out[slots:]
            first_copy(pair, odd).start()

    def send_second(pair):
        fetch(pair)
        for odd in range(2):
            expert = 2 * pair + odd
            _, _, _, quarter, spot, _ = side(odd)
            fetched(pair, odd)
            first_copy(pair, odd).wait_recv()
            for number in range(2):
                out = dot(rows[expert, quarter], weights[odd, number])
                out += first[expert, spot, number].astype(F32)
                first[expert, spot, number] = out.astype(BF16)
            second_copy(pair, odd).start()

    def hidden_gradient(expert):
        half = grad_low.shape[0]
        low = grad_low[jnp.minimum(expert, half - 1)].astype(F32)
        high = grad_high[jnp.maximum(expert - half, 0)].astype(F32)
        return jnp.where(expert < half, low, high)

    def finish(pair):
        fetch(pair)
        for odd in range(2):
            expert = 2 * pair + odd
            spot = side(odd)[5]
            fetched(pair, odd)
            second_copy(pair, odd).wait_recv()
            scale = factors[expert, :, 1:2]
            source = rows[expert, me]
            gate_pre, up_pre = (
                dot(source, weights[odd, number])
                + first[expert, spot, number].astype(F32)
                + second[expert, number].astype(F32)
                for number in range(2)
            )
            scaled, grad_gate_pre, grad_up_pre, grad_gate = expert_body(
                gate_pre * scale,
                up_pre * scale,
                hidden_gradient(expert),
                factors[expert, :, 0:1],
            )
            first[expert, spot, 0] = grad_gate_pre
            first[expert, spot, 1] = grad_up_pre
            x_copy(pair, odd).start()
            y_copy(pair, odd).start()
            own_copy(pair, odd).start()
            hid_out[expert, 0] = scaled
            gate_out[expert] = grad_gate

    def pass_on(pair):
        for odd in range(2):
            (x_copy if odd else y_copy)(pair, odd).wait_recv()
            far_copy(pair, odd).start()

        @pl.when(pair == pairs - 1)
        def _():
            for odd in range(2):
                hidden_x_copy(odd).start()
                hidden_y_copy(odd).start()

    def hidden_x_copy(odd):
        return remote(
            hid_out.at[odd], hidden_x_out.at[odd], hidden_x_send.at[odd], hidden_x_recv.at[odd], x_other
        )

    def hidden_y_copy(odd):
        return remote(
            hid_out.at[odd], hidden_y_out.at[odd], hidden_y_send.at[odd], hidden_y_recv.at[odd], y_other
        )

    def load(pair, odd, number):
        expert = 2 * pair + odd
        source = (x_out, y_out, d_out)[number]
        return pltpu.make_async_copy(
            source.at[expert], loaded.at[odd, number], load_sem.at[odd, number]
        )

    def send_back(pair):
        fetch(pair)
        for odd in range(2):
            (y_copy if odd else x_copy)(pair, odd).wait_recv()
            load(pair, odd, 0).start()
            load(pair, odd, 1).start()
        for odd in range(2):
            far_copy(pair, odd).wait_recv()
            load(pair, odd, 2).start()
        for odd in range(2):
            expert = 2 * pair + odd
            fetched(pair, odd)
            for number in range(3):
                load(pair, odd, number).wait()
            spot = side(odd)[5]
            total = None
            for number in range(2):
                source = jnp.concatenate(
                    [first[expert, spot, number]] + [loaded[odd, part, number] for part in range(3)],
                    axis=0,
                )
                part = dot_nt(source, weights[odd, number])
                total = part if total is None else total + part
            total = total.astype(BF16)
            for number, quarter in enumerate((me, x_other, y_other, across)):
                back_out[expert, quarter] = total[number * slots : (number + 1) * slots]

    def step(number, _):
        for lag, stage in enumerate((send_first, send_second, finish, pass_on, send_back)):

            @pl.when((number >= lag) & (number < pairs + lag))
            def _(lag=lag, stage=stage):
                stage(number - lag)

        return 0

    experts, quarters = rows.shape[:2]
    block, cap = chosen_held.shape[1], chosen.shape[1] // experts
    per_quarter = slots // cap
    blocks = quarters * per_quarter

    def chosen_copy(number):
        return pltpu.make_async_copy(
            chosen.at[pl.ds(number * block, block)], chosen_held.at[number % 2], chosen_sem.at[number % 2]
        )

    def to_tokens_of(number, _):
        chosen_copy(number).wait()

        @pl.when(number + 1 < blocks)
        def _():
            chosen_copy(number + 1).start()

        spots = pl.ds((number % per_quarter) * cap, cap)
        pieces = [back_out[expert, number // per_quarter, spots] for expert in range(experts)]
        total = dot(chosen_held[number % 2], jnp.concatenate(pieces, axis=0))
        tokens_out[pl.ds(number * block, block)] = total.astype(BF16)
        return 0

    chosen_copy(0).start()
    lax.fori_loop(0, pairs + 4, step, 0)
    lax.fori_loop(0, blocks, to_tokens_of, 0)
    for odd in range(2):
        hidden_x_copy(odd).wait()
        hidden_y_copy(odd).wait()

    def drain(pair, _):
        for odd in range(2):

            @pl.when(pair >= pairs - 2)
            def _(odd=odd):
                first_copy(pair, odd).wait_send()

            second_copy(pair, odd).wait_send()
            own_copy(pair, odd).wait()
            x_copy(pair, odd).wait_send()
            y_copy(pair, odd).wait_send()
            far_copy(pair, odd).wait_send()
        return 0

    lax.fori_loop(0, pairs, drain, 0)


def routed_experts(rows, w_gate, w_up, grad_low, grad_high, factors, chosen, blocks):
    experts, quarters, slots, depth = rows.shape
    width = w_gate.shape[2]
    vmem = pl.BlockSpec(memory_space=pltpu.VMEM)
    anywhere = pl.BlockSpec(memory_space=pl.ANY)
    block = jax.ShapeDtypeStruct((experts, 2, slots, width), BF16)
    dma = pltpu.SemaphoreType.DMA
    return pl.pallas_call(
        experts_kernel,
        in_specs=[vmem, anywhere, anywhere, vmem, vmem, vmem, anywhere],
        out_specs=[anywhere] * 4 + [vmem] * 3 + [anywhere] * 2,
        out_shape=[block] * 4
        + [
            jax.ShapeDtypeStruct((experts, 1, slots, width), BF16),
            jax.ShapeDtypeStruct((chosen.shape[0], depth), BF16),
            jax.ShapeDtypeStruct((experts, slots, 1), F32),
            jax.ShapeDtypeStruct((2, 1, slots, width), BF16),
            jax.ShapeDtypeStruct((2, 1, slots, width), BF16),
        ],
        scratch_shapes=[
            pltpu.VMEM((experts, quarters, slots, depth), BF16),
            pltpu.VMEM((2, chosen.shape[0] // blocks, chosen.shape[1]), BF16),
            pltpu.VMEM((2, 2, 2, 2, slots, width), BF16),
            pltpu.VMEM((experts, 2, 2, slots, width), BF16),
            pltpu.VMEM((experts, 2, slots, width), BF16),
            pltpu.VMEM((2, 2, depth, width), BF16),
            pltpu.VMEM((2, 3, 2, slots, width), BF16),
        ]
        + [dma((experts,))] * 11
        + [dma((2, 2)), dma((2, 3))]
        + [dma((2,))] * 5,
        compiler_params=pltpu.CompilerParams(
            collective_id=0, has_side_effects=True, vmem_limit_bytes=VMEM_LIMIT
        ),
        cost_estimate=cost(390),
        name="routed_experts",
    )(rows, w_gate, w_up, grad_low, grad_high, factors, chosen)


def sum_kernel(base, by_quarter, own_weights, transposed, rows, weight, out, sent, first, second, held, *sems):
    first_send, first_recv, second_send, second_recv, weight_sem = sems
    x, y, x_other, y_other = neighbours()
    me = 2 * y + x
    pairs = sent.shape[0] // 2
    slots = sent.shape[2]

    def side(odd):
        if odd:
            return y_other, x_other, (2 - 2 * y, 3 - 2 * y), 2 * y + 1 - x, 1 - x, x
        return x_other, y_other, (1 - x, 3 - x), 2 * (1 - y) + x, 1 - y, y

    def source(item, quarter):
        return rows[quarter, item] if by_quarter else rows[base + item, quarter]

    def product(value, item):
        matrix = held[item] if own_weights else weight[...]
        return dot_nt(value, matrix) if transposed else dot(value, matrix)

    def weight_copy(item):
        return pltpu.make_async_copy(weight.at[base + item], held.at[item], weight_sem.at[item])

    def first_copy(item, odd):
        return remote(sent.at[item], first.at[item], first_send.at[item], first_recv.at[item], side(odd)[0])

    def second_copy(item, odd):
        return remote(
            first.at[item, side(odd)[4]],
            second.at[item],
            second_send.at[item],
            second_recv.at[item],
            side(odd)[1],
        )

    def send_first(pair):
        for odd in range(2):
            item = 2 * pair + odd
            low, high = side(odd)[2]
            if own_weights:
                weight_copy(item).wait()
            result = product(jnp.concatenate([source(item, low), source(item, high)], axis=0), item)
            sent[item, 0] = result[:slots].astype(BF16)
            sent[item, 1] = result[slots:].astype(BF16)
            first_copy(item, odd).start()

    def send_second(pair):
        for odd in range(2):
            item = 2 * pair + odd
            _, _, _, quarter, spot, _ = side(odd)
            result = product(source(item, quarter), item)
            first_copy(item, odd).wait_recv()
            first[item, spot] = (result + first[item, spot].astype(F32)).astype(BF16)
            second_copy(item, odd).start()

    def finish(pair):
        for odd in range(2):
            item = 2 * pair + odd
            result = product(source(item, me), item) + first[item, side(odd)[5]].astype(F32)
            second_copy(item, odd).wait_recv()
            out[item] = (result + second[item].astype(F32)).astype(out.dtype)

    def fetch(item, _):
        weight_copy(item).start()
        return 0

    if own_weights:
        lax.fori_loop(0, 2 * pairs, fetch, 0)
    greet(x_other, y_other)

    def step(number, _):
        for lag, stage in enumerate((send_first, send_second, finish)):

            @pl.when((number >= lag) & (number < pairs + lag))
            def _(lag=lag, stage=stage):
                stage(number - lag)

        return 0

    lax.fori_loop(0, pairs + 2, step, 0)

    def drain(pair, _):
        for odd in range(2):
            item = 2 * pair + odd
            first_copy(item, odd).wait_send()
            second_copy(item, odd).wait_send()
        return 0

    lax.fori_loop(0, pairs, drain, 0)


def square_sum(rows, weight, base, items, number, transposed, by_quarter, kind):
    slots, depth = rows.shape[2:]
    own_weights = weight.ndim == 3
    width = weight.shape[-2] if transposed else weight.shape[-1]
    vmem = pl.BlockSpec(memory_space=pltpu.VMEM)
    dma = pltpu.SemaphoreType.DMA
    held = (items,) + weight.shape[1:] if own_weights else (8, 128)
    return pl.pallas_call(
        functools.partial(sum_kernel, base, by_quarter, own_weights, transposed),
        in_specs=[vmem, pl.BlockSpec(memory_space=pl.ANY) if own_weights else vmem],
        out_specs=vmem,
        out_shape=jax.ShapeDtypeStruct((items, slots, width), kind),
        scratch_shapes=[
            pltpu.VMEM((items, 2, slots, width), BF16),
            pltpu.VMEM((items, 2, slots, width), BF16),
            pltpu.VMEM((items, slots, width), BF16),
            pltpu.VMEM(held, BF16),
        ]
        + [dma((items,))] * 5,
        compiler_params=pltpu.CompilerParams(
            collective_id=number, has_side_effects=True, vmem_limit_bytes=VMEM_LIMIT
        ),
        cost_estimate=cost(13.5 * items if own_weights else 20 + 25 * width // 512),
        name="square_sum",
    )(rows, weight)


def band_total(rows, weight, number, transposed=False, kind=F32):
    if not square():
        whole = (dot_nt(rows, weight) if transposed else dot(rows, weight)).astype(BF16)
        return lax.psum_scatter(whole, "gx", scatter_dimension=0, tiled=True).astype(kind)
    source = rows.reshape(4, 4, rows.shape[0] // 16, rows.shape[1])
    out = square_sum(source, weight, 0, 4, number, transposed, True, kind)
    return out.reshape(-1, out.shape[2])


def small_kernel(both, inner_ref, outer_ref, inner_out, outer_out, inner_land, outer_land, send, recv, far_send, far_recv):
    x, y, x_other, y_other = neighbours()
    me = 2 * y + x
    peers = (x_other, y_other, 3 - me)
    here = lax.axis_index("gy")
    size = outer_land.shape[0]
    barrier = pltpu.get_barrier_semaphore()
    for other in peers:
        pl.semaphore_signal(barrier, inc=1, device_id={"gx": other}, device_id_type=pl.DeviceIdType.MESH)
    for step in range(1, size if both else 1):
        pl.semaphore_signal(
            barrier, inc=1, device_id={"gy": (here + step) % size}, device_id_type=pl.DeviceIdType.MESH
        )
    pl.semaphore_wait(barrier, 3 + (size - 1 if both else 0))

    inner_land[me] = inner_ref[...]

    def inner_copy(number):
        return remote(inner_ref, inner_land.at[me], send.at[number], recv.at[number], peers[number])

    for number in range(3):
        inner_copy(number).start()
    for number in range(3):
        inner_copy(number).wait()
    total = inner_land[0]
    for number in range(1, 4):
        total = total + inner_land[number]
    inner_out[...] = total
    if not both:
        outer_out[...] = outer_ref[...]
        return
    outer_land[here, 0:8] = outer_ref[...]
    outer_land[here, 8:16] = total

    def outer_copy(step):
        return pltpu.make_async_remote_copy(
            src_ref=outer_land.at[here],
            dst_ref=outer_land.at[here],
            send_sem=far_send.at[step - 1],
            recv_sem=far_recv.at[step - 1],
            device_id={"gy": (here + step) % size},
            device_id_type=pl.DeviceIdType.MESH,
        )

    for step in range(1, size):
        outer_copy(step).start()
    for step in range(1, size):
        outer_copy(step).wait()
    total = outer_land[0]
    for number in range(1, size):
        total = total + outer_land[number]
    outer_out[...] = total


def small_totals(inner, outer, number):
    both = outer is not None
    size = lax.axis_size("gy")
    dma = pltpu.SemaphoreType.DMA
    vmem = pl.BlockSpec(memory_space=pltpu.VMEM)
    return pl.pallas_call(
        functools.partial(small_kernel, both),
        in_specs=[vmem, vmem],
        out_specs=[vmem, vmem],
        out_shape=[
            jax.ShapeDtypeStruct((8, 128), F32),
            jax.ShapeDtypeStruct((16, 128) if both else (8, 128), F32),
        ],
        scratch_shapes=[
            pltpu.VMEM((4, 8, 128), F32),
            pltpu.VMEM((size, 16, 128), F32),
            dma((3,)),
            dma((3,)),
            dma((size - 1,)),
            dma((size - 1,)),
        ],
        compiler_params=pltpu.CompilerParams(
            collective_id=number, has_side_effects=True, vmem_limit_bytes=VMEM_LIMIT
        ),
        cost_estimate=cost(6),
        name="small_totals",
    )(inner, outer if both else jnp.zeros((8, 128), F32))


def shared_sums_kernel(parts, gate, up, down):
    width = gate.shape[0]
    wide = parts.shape[2] // 3
    total = parts[0].astype(F32)
    for number in range(1, parts.shape[0]):
        total = total + parts[number].astype(F32)
    total = total.T
    gate[...] = total[:width]
    up[...] = total[wide : wide + width]
    down[...] = total[2 * wide : 2 * wide + width]


def shared_sums(parts, width):
    rows = parts.shape[1]
    block = 128
    many = parts.shape[0]
    return pl.pallas_call(
        shared_sums_kernel,
        grid=(rows // block,),
        in_specs=[pl.BlockSpec((many, block, parts.shape[2]), lambda i: (0, i, 0))],
        out_specs=[pl.BlockSpec((width, block), lambda i: (0, i))] * 3,
        out_shape=[jax.ShapeDtypeStruct((width, rows), F32)] * 3,
        compiler_params=params(),
        cost_estimate=cost(5),
        name="shared_sums",
    )(parts)


def group_specs(groups):
    specs, values = [], []
    base = groups[0][0]
    for first, count, blocks in groups:
        for value, start in blocks:

            def index(e, p, low=first - base, top=count - 1, start=start):
                return (jnp.clip(e - low, 0, top) + start, 0, 0, 0)

            specs.append(pl.BlockSpec((1,) + value.shape[1:], index))
            values.append(value)
    return specs, values


def for_group(groups, refs, body):
    base = groups[0][0]
    each = len(groups[0][2])
    if len(groups) == 1:
        body(refs[:each])
        return
    step = pl.program_id(0)
    for number, (first, count, _) in enumerate(groups):
        low = first - base

        @pl.when((step >= low) & (step < low + count))
        def _(number=number):
            body(refs[number * each : (number + 1) * each])


def back_kernel(groups, transposed, picks_ref, *refs):
    terms, slots = groups[0][2][0][1:3]
    out_ref = refs[-1]
    weights = refs[-1 - terms : -1]

    def body(pieces):
        total = None
        for term in range(terms):
            source = jnp.concatenate([ref[0, term] for ref in pieces], axis=0)
            part = dot_nt(source, weights[term][0]) if transposed else dot(source, weights[term][0])
            total = part if total is None else total + part
        total = total.astype(BF16)
        for quarter in range(len(pieces)):
            rows = total[quarter * slots : (quarter + 1) * slots]
            out_ref[0, pl.ds(picks_ref[quarter], 1)] = rows[None]

    for_group(groups, refs, body)


def shapes_of(groups):
    return tuple(
        (first, count, tuple(b.shape for b, _ in blocks))
        for first, count, blocks in groups
    )


def back(groups, picks, weights, transposed):
    first = groups[0][0]
    count = sum(g[1] for g in groups)
    quarters = len(groups[0][2])
    terms, slots, depth = groups[0][2][0][0].shape[1:]
    width = weights[0].shape[1] if transposed else weights[0].shape[2]
    specs, values = group_specs(groups)
    specs += [pl.BlockSpec((1,) + w.shape[1:], lambda e, p: (first + e, 0, 0)) for w in weights]
    return pl.pallas_call(
        functools.partial(back_kernel, shapes_of(groups), transposed),
        grid_spec=pltpu.PrefetchScalarGridSpec(
            num_scalar_prefetch=1,
            grid=(count,),
            in_specs=specs,
            out_specs=pl.BlockSpec((1, quarters, slots, width), lambda e, p: (e, 0, 0, 0)),
        ),
        out_shape=jax.ShapeDtypeStruct((count, quarters, slots, width), BF16),
        compiler_params=params(),
        cost_estimate=cost(4 * count),
        name="back",
    )(picks, *values, *weights)


def weight_grad_kernel(groups, flip, scaled, picks_ref, *refs):
    terms = groups[0][2][0][1]
    quarters = len(groups[0][2])
    outs = refs[-terms:]
    rows = [ref[0, 0] for ref in refs[:quarters]]
    if scaled:
        scales = refs[quarters : 2 * quarters]
        rows = [(row.astype(F32) * ref[0, 0]).astype(BF16) for row, ref in zip(rows, scales)]
        refs = refs[quarters:]
    rows = jnp.concatenate(rows, axis=0)

    def body(pieces):
        for term in range(terms):
            others = jnp.concatenate([ref[0, term] for ref in pieces], axis=0)
            outs[term][0] = dot_tn(others, rows) if flip else dot_tn(rows, others)

    for_group(groups, refs[quarters:], body)


def weight_grad(rows, groups, picks, flip, scale=None):
    first = groups[0][0]
    count = sum(g[1] for g in groups)
    quarters = len(groups[0][2])
    slots, depth = rows.shape[2:]
    terms, _, width = groups[0][2][0][0].shape[1:]
    specs = [
        pl.BlockSpec((1, 1, slots, depth), lambda e, p, q=quarter: (first + e, p[q], 0, 0))
        for quarter in range(quarters)
    ]
    values = [rows] * quarters
    if scale is not None:
        specs += [
            pl.BlockSpec((1, 1, slots, 1), lambda e, p, q=quarter: (first + e, p[q], 0, 0))
            for quarter in range(quarters)
        ]
        values += [scale] * quarters
    more, others = group_specs(groups)
    shape = (width, depth) if flip else (depth, width)
    return pl.pallas_call(
        functools.partial(weight_grad_kernel, shapes_of(groups), flip, scale is not None),
        grid_spec=pltpu.PrefetchScalarGridSpec(
            num_scalar_prefetch=1,
            grid=(count,),
            in_specs=specs + more,
            out_specs=[pl.BlockSpec((1,) + shape, lambda e, p: (e, 0, 0))] * terms,
        ),
        out_shape=[jax.ShapeDtypeStruct((count,) + shape, F32)] * terms,
        compiler_params=params(),
        cost_estimate=cost(1),
        name="weight_grad",
    )(picks, *values, *others)


def side_by_side_kernel(gate, up, down, out):
    width = gate.shape[1]
    wide = out.shape[1] // 3
    out[...] = jnp.zeros_like(out)
    out[:, :width] = gate[...]
    out[:, wide : wide + width] = up[...]
    out[:, 2 * wide : 2 * wide + width] = down[...].T


def side_by_side(gate, up, down, wide):
    return pl.pallas_call(
        side_by_side_kernel,
        out_shape=jax.ShapeDtypeStruct((gate.shape[0], 3 * wide), BF16),
        compiler_params=params(),
        cost_estimate=cost(3),
        name="side_by_side",
    )(gate, up, down)


def shared_kernel(picks_ref, norm, scale, grad, *refs):
    blocks, (hidden_out, grads_out, part_out, forward_out, weight) = refs[:-5], refs[-5:]
    wide = hidden_out.shape[1]

    @pl.when(pl.program_id(0) == 0)
    def _():
        rows = blocks[0].shape[0]
        if len(blocks) == 1:
            weight[...] = blocks[0][...]
        else:
            half = rows // 2
            for number in range(3):
                start = pl.multiple_of(picks_ref[number] * rows, rows)
                weight[pl.ds(start, rows)] = blocks[number][...]
            start = pl.multiple_of(picks_ref[3] * rows, rows)
            weight[pl.ds(start, half)] = blocks[3][...]
            weight[pl.ds(start + half, half)] = blocks[4][...]

    both = dot(norm[...], weight[:, : 2 * wide]) * scale[...]
    gate_pre, up_pre = both[:, :wide], both[:, wide:]
    grad_hidden = dot(grad[...], weight[:, 2 * wide :])
    sigma = jax.nn.sigmoid(gate_pre)
    act = gate_pre * sigma
    hidden = (act * up_pre).astype(BF16)
    hidden_out[...] = hidden
    forward_out[...] = dot_nt(hidden, weight[:, 2 * wide :]).astype(BF16)
    grads = jnp.concatenate(
        [
            (grad_hidden * up_pre * sigma * (1.0 + gate_pre * (1.0 - sigma))).astype(BF16),
            (grad_hidden * act).astype(BF16),
        ],
        axis=1,
    )
    grads_out[...] = (grads.astype(F32) * scale[...]).astype(BF16)
    part_out[...] = dot_nt(grads, weight[:, : 2 * wide]).astype(BF16)


def shared_experts(norm, scale, grad, weights, picks):
    rows, depth = norm.shape
    wide = weights[0].shape[1] // 3
    block = 256
    return pl.pallas_call(
        shared_kernel,
        grid_spec=pltpu.PrefetchScalarGridSpec(
            num_scalar_prefetch=1,
            grid=(rows // block,),
            in_specs=[
                pl.BlockSpec((block, depth), lambda i, p: (i, 0)),
                pl.BlockSpec((block, 1), lambda i, p: (i, 0)),
                pl.BlockSpec((block, depth), lambda i, p: (i, 0)),
            ]
            + [pl.BlockSpec(weight.shape, lambda i, p: (0, 0)) for weight in weights],
            out_specs=[
                pl.BlockSpec((block, wide), lambda i, p: (i, 0)),
                pl.BlockSpec((block, 2 * wide), lambda i, p: (i, 0)),
                pl.BlockSpec((block, depth), lambda i, p: (i, 0)),
                pl.BlockSpec((block, depth), lambda i, p: (i, 0)),
            ],
            scratch_shapes=[pltpu.VMEM((depth, 3 * wide), BF16)],
        ),
        out_shape=[
            jax.ShapeDtypeStruct((rows, wide), BF16),
            jax.ShapeDtypeStruct((rows, 2 * wide), BF16),
            jax.ShapeDtypeStruct((rows, depth), BF16),
            jax.ShapeDtypeStruct((rows, depth), BF16),
        ],
        compiler_params=params(),
        cost_estimate=cost(16),
        name="shared_experts",
    )(picks, norm, scale, grad, *weights)


def shared_weights_kernel(norm, grads, grad, hidden, out):
    both = grads.shape[1]
    out[:, :both] = dot_tn(norm[...], grads[...]).astype(BF16)
    out[:, both:] = dot_tn(grad[...], hidden[...]).astype(BF16)


def shared_weights(norm, grads, grad, hidden):
    rows, depth = norm.shape
    block = 256
    width = grads.shape[1] + hidden.shape[1]
    return pl.pallas_call(
        shared_weights_kernel,
        grid=(depth // block,),
        in_specs=[
            pl.BlockSpec((rows, block), lambda i: (0, i)),
            pl.BlockSpec(grads.shape, lambda i: (0, 0)),
            pl.BlockSpec((rows, block), lambda i: (0, i)),
            pl.BlockSpec(hidden.shape, lambda i: (0, 0)),
        ],
        out_specs=pl.BlockSpec((block, width), lambda i: (i, 0)),
        out_shape=jax.ShapeDtypeStruct((depth, width), BF16),
        compiler_params=params(),
        cost_estimate=cost(10),
        name="shared_weights",
    )(norm, grads, grad, hidden)


def rope_tables(length):
    half = DR // 2
    position = jnp.arange(length).astype(F32)
    inverse = jnp.exp(-math.log(10000.0) * jnp.arange(half).astype(F32) / half)
    angle = position[:, None] * inverse[None, :]
    cosine, sine = jnp.cos(angle), jnp.sin(angle)
    return jnp.concatenate([cosine, cosine], axis=1), jnp.concatenate([-sine, sine], axis=1)


def turn(value, cosine, sine):
    half = DR // 2
    other = jnp.concatenate([value[:, half:], value[:, :half]], axis=1)
    return value * cosine + other * sine


def query_blocks(starts_ref, sequence):
    blocks = []
    for first in range(0, SEQ_LEN, PIECE):
        keys = min(SEQ_LEN, first + 2 * PIECE)
        query = first + lax.broadcasted_iota(jnp.int32, (PIECE, 1), 0)
        key = lax.broadcasted_iota(jnp.int32, (1, keys), 1)
        seen = key <= query
        for number in range(2):
            low = starts_ref[sequence, number]
            seen |= ((query >= low) & (query < low + PIECE)) & ((key >= low) & (key < low + PIECE))
        blocks.append((first, keys, seen))
    return blocks


def attention_kernel(heads, starts_ref, proj_ref, rows_scale, latent, gain, w_expand, cos, sin, out, logs, q_out, k_out, v_out, n_out):
    scale = (DN + DR) ** (-0.5)
    cosine, sine = cos[...], sin[...]
    proj = proj_ref[...] * rows_scale[...]
    lat = latent[...].astype(F32)
    compressed = lat[:, :L]
    root = lax.rsqrt(jnp.mean(compressed * compressed, axis=1, keepdims=True) + EPS)
    normed = (compressed * root * gain[...].astype(F32)).astype(BF16)
    n_out[...] = normed
    key_rope = turn(lat[:, L:], cosine, sine).astype(BF16)
    expanded = dot(normed, w_expand[...]).astype(BF16)
    blocks = query_blocks(starts_ref, pl.program_id(0))
    for head in range(heads):
        plain = proj[:, head * DN : (head + 1) * DN].astype(BF16)
        start = heads * DN + head * DR
        query = jnp.concatenate([plain, turn(proj[:, start : start + DR], cosine, sine).astype(BF16)], axis=1)
        start = head * (DN + DV)
        key = jnp.concatenate([expanded[:, start : start + DN], key_rope], axis=1)
        value = expanded[:, start + DN : start + DN + DV]
        q_out[0, head] = query
        k_out[0, head] = key
        v_out[0, head] = value
        for first, keys, seen in blocks:
            rows = slice(first, first + PIECE)
            scores = jnp.where(seen, dot_nt(query[rows], key[:keys]) * scale, -1e30)
            peak = jnp.max(scores, axis=1, keepdims=True)
            expo = jnp.exp(scores - peak)
            total = jnp.sum(expo, axis=1, keepdims=True)
            weights = (expo * (1.0 / total)).astype(BF16)
            out[rows, head * DV : (head + 1) * DV] = dot(weights, value[:keys]).astype(BF16)
            logs[0, head, rows] = peak + jnp.log(total)


def attention_forward(starts, proj, rows_scale, latent, gain, w_expand, cosine, sine, heads):
    band = proj.shape[0]
    seqs = band // SEQ_LEN

    def rows(width):
        return pl.BlockSpec((SEQ_LEN, width), lambda s, p: (s, 0))

    def whole(shape):
        return pl.BlockSpec(shape, lambda s, p: (0, 0))

    def by_head(width):
        return pl.BlockSpec((1, heads, SEQ_LEN, width), lambda s, p: (s, 0, 0, 0))

    def head_shape(width, kind=BF16):
        return jax.ShapeDtypeStruct((seqs, heads, SEQ_LEN, width), kind)

    return pl.pallas_call(
        functools.partial(attention_kernel, heads),
        grid_spec=pltpu.PrefetchScalarGridSpec(
            num_scalar_prefetch=1,
            grid=(seqs,),
            in_specs=[
                rows(proj.shape[1]),
                rows(1),
                rows(L + DR),
                whole((1, L)),
                whole(w_expand.shape),
                whole((SEQ_LEN, DR)),
                whole((SEQ_LEN, DR)),
            ],
            out_specs=[rows(heads * DV), by_head(1), by_head(DN + DR), by_head(DN + DR), by_head(DV), rows(L)],
        ),
        out_shape=[
            jax.ShapeDtypeStruct((band, heads * DV), BF16),
            head_shape(1, F32),
            head_shape(DN + DR),
            head_shape(DN + DR),
            head_shape(DV),
            jax.ShapeDtypeStruct((band, L), BF16),
        ],
        compiler_params=params(),
        cost_estimate=cost(12),
        name="attention",
    )(starts, proj, rows_scale, latent, gain[None], w_expand, cosine, sine)


def longer(total, part):
    if total is None:
        return part
    rows = total.shape[0]
    if rows == part.shape[0]:
        return total + part
    return jnp.concatenate([total + part[:rows], part[rows:]], axis=0)


def attention_back_kernel(heads, starts_ref, q_ref, k_ref, v_ref, logs, grad, w_expand, cos, sin, dq_out, de_out, dl_out):
    scale = (DN + DR) ** (-0.5)
    cosine, sine = cos[...], -sin[...]
    blocks = query_blocks(starts_ref, pl.program_id(0))
    rope = None
    latent = None
    for head in range(heads):
        query, key, value = q_ref[0, head], k_ref[0, head], v_ref[0, head]
        grad_here = grad[:, head * DV : (head + 1) * DV]
        grad_key = grad_value = None
        for first, keys, seen in blocks:
            rows = slice(first, first + PIECE)
            scores = jnp.where(seen, dot_nt(query[rows], key[:keys]) * scale, -1e30)
            weights = jnp.exp(scores - logs[0, head, rows])
            grad_weights = dot_nt(grad_here[rows], value[:keys])
            centre = jnp.sum(weights * grad_weights, axis=1, keepdims=True)
            grad_scores = (weights * (grad_weights - centre)).astype(BF16)
            grad_query = dot(grad_scores, key[:keys]) * scale
            dq_out[rows, head * DN : (head + 1) * DN] = grad_query[:, :DN].astype(BF16)
            start = heads * DN + head * DR
            turned = turn(grad_query[:, DN:], cosine[rows], sine[rows])
            dq_out[rows, start : start + DR] = turned.astype(BF16)
            grad_key = longer(grad_key, dot_tn(grad_scores, query[rows]))
            grad_value = longer(grad_value, dot_tn(weights.astype(BF16), grad_here[rows]))
        grad_key = grad_key * scale
        part = turn(grad_key[:, DN:], cosine, sine)
        rope = part if rope is None else rope + part
        both = jnp.concatenate([grad_key[:, :DN].astype(BF16), grad_value.astype(BF16)], axis=1)
        start = head * (DN + DV)
        de_out[:, start : start + DN + DV] = both
        part = dot_nt(both, w_expand[:, start : start + DN + DV])
        latent = part if latent is None else latent + part
    dl_out[:, :L] = latent.astype(BF16)
    dl_out[:, L:] = rope.astype(BF16)


def attention_backward(starts, query, key, value, logs, grad, w_expand, cosine, sine):
    seqs, heads = query.shape[:2]
    band = seqs * SEQ_LEN

    def rows(width):
        return pl.BlockSpec((SEQ_LEN, width), lambda s, p: (s, 0))

    def whole(shape):
        return pl.BlockSpec(shape, lambda s, p: (0, 0))

    def by_head(width):
        return pl.BlockSpec((1, heads, SEQ_LEN, width), lambda s, p: (s, 0, 0, 0))

    widths = (heads * (DN + DR), heads * (DN + DV), L + DR)
    return pl.pallas_call(
        functools.partial(attention_back_kernel, heads),
        grid_spec=pltpu.PrefetchScalarGridSpec(
            num_scalar_prefetch=1,
            grid=(seqs,),
            in_specs=[
                by_head(DN + DR),
                by_head(DN + DR),
                by_head(DV),
                by_head(1),
                rows(heads * DV),
                whole(w_expand.shape),
                whole((SEQ_LEN, DR)),
                whole((SEQ_LEN, DR)),
            ],
            out_specs=[rows(width) for width in widths],
        ),
        out_shape=[jax.ShapeDtypeStruct((band, width), BF16) for width in widths],
        compiler_params=params(),
        cost_estimate=cost(14),
        name="attention_back",
    )(starts, query, key, value, logs, grad, w_expand, cosine, sine)


def norm_products_kernel(picks_ref, *refs):
    query, latent = refs[:5], refs[5:10]
    weight, whole_out, part_out = refs[10:]
    half = query[3].shape[0]

    def write(number, start, query_rows, latent_rows):
        both = jnp.concatenate([query_rows, latent_rows], axis=1)
        place_of = pl.ds(picks_ref[number], 1)
        whole_out[place_of, start : start + half] = both[None]
        part_out[place_of, start : start + half] = dot_nt(both, weight[...]).astype(BF16)[None]

    for number in range(3):
        for start in (0, half):
            rows = slice(start, start + half)
            write(number, start, query[number][rows], latent[number][rows])
    write(3, 0, query[3][...], latent[3][...])
    write(3, half, query[4][...], latent[4][...])


def norm_products(query, latent, weight, picks):
    rows = query[0].shape[0]
    width = weight.shape[1]
    vmem = pl.BlockSpec(memory_space=pltpu.VMEM)
    return pl.pallas_call(
        norm_products_kernel,
        in_specs=[pl.BlockSpec(memory_space=pltpu.SMEM)] + [vmem] * 11,
        out_specs=[vmem, vmem],
        out_shape=[
            jax.ShapeDtypeStruct((4, rows, width), BF16),
            jax.ShapeDtypeStruct((4, rows, weight.shape[0]), BF16),
        ],
        compiler_params=params(),
        cost_estimate=cost(8),
        name="norm_products",
    )(picks, *query, *latent, weight)


def norm_backward(value, scale, gain, grad_norm, row_total, width):
    return (
        scale[:, None] * gain * grad_norm - value * (scale**3 / width)[:, None] * row_total[:, None]
    )


def widen(value, width):
    return jnp.pad(value, ((0, 0), (0, width - value.shape[1])))


def up_to(width):
    return 128 * ((width + 127) // 128)


def per_device(
    hidden_in,
    expert_routes,
    piece_starts,
    query_weight,
    latent_weight,
    latent_gain,
    expand_weight,
    output_weight,
    attention_gain,
    ffn_gain,
    router_weight,
    gate_weight,
    up_weight,
    down_weight,
    shared_gate,
    shared_up,
    shared_down,
    grad_out,
):
    row_parts = lax.axis_size("gx")
    column_parts = lax.axis_size("gy")
    here_x = lax.axis_index("gx")
    here_y = lax.axis_index("gy")
    local_rows, local_width = hidden_in.shape
    all_tokens = local_rows * column_parts
    band_rows = all_tokens // row_parts
    head_width = query_weight.shape[1]
    heads_here = head_width // (DN + DR)
    latent_width = latent_weight.shape[1]
    experts_here = gate_weight.shape[0]
    shared_width = shared_gate.shape[1]
    cap = 16 * ((local_rows * TOPK * 5 + 64 * EXPERTS - 1) // (64 * EXPERTS))
    blocks = column_parts
    quarter_blocks = blocks // row_parts
    quarter_slots = quarter_blocks * cap
    on_square = square()
    if on_square:
        order_of = numbers(here_x, here_x ^ 1, here_x ^ 2, here_x ^ 3)
    else:
        order_of = jnp.arange(row_parts, dtype=jnp.int32)

    waited.clear()
    hidden_all = spread_rows(hidden_in)
    hidden = hidden_in.astype(F32)
    grad_top = grad_out.astype(F32)
    wide = up_to(shared_width)
    shared_weight = side_by_side(shared_gate, shared_up, shared_down, wide)
    scale_one = lax.rsqrt(feature_total(jnp.sum(hidden * hidden, axis=1)) / D + EPS)
    sent = jnp.concatenate([expert_routes.T.astype(F32), scale_one[None]], axis=0)
    gathered = jnp.broadcast_to(sent[None], (column_parts,) + sent.shape)
    gathered = lax.all_to_all(gathered, "gy", split_axis=0, concat_axis=0, tiled=True)
    grad_top_tokens = to_tokens(after(grad_out, gathered))
    gathered = gathered.transpose(1, 0, 2).reshape(TOPK + 1, all_tokens)
    routes_all = gathered[:TOPK].astype(jnp.int32)
    scale_one_all = gathered[TOPK]
    mine = here_y * experts_here + jnp.arange(experts_here, dtype=jnp.int32)
    named = jnp.any(routes_all[:, :, None] == mine[None, None, :], axis=0)
    named_blocks = named.astype(BF16).reshape(blocks, local_rows, experts_here)
    order = jnp.arange(local_rows, dtype=jnp.int32)
    earlier = (order[None, :] < order[:, None]).astype(BF16)
    slot = jnp.einsum("ts,bse->bte", earlier, named_blocks, preferred_element_type=F32)
    code = jnp.where(named, slot.reshape(all_tokens, experts_here), -1.0)
    chosen = one_hot(code, cap, blocks)
    code_here = pick(code.reshape(row_parts, quarter_blocks, local_rows, experts_here), here_x, 0)
    spots = jnp.arange(cap, dtype=jnp.int32).astype(F32)
    at_slot = code_here[:, :, :, None] == spots
    by_head = query_weight.reshape(-1, heads_here, DN + DR)
    used = head_width + latent_width
    in_weight = jnp.concatenate(
        [
            by_head[:, :, :DN].reshape(-1, heads_here * DN),
            by_head[:, :, DN:].reshape(-1, heads_here * DR),
            widen(latent_weight, up_to(used) - head_width),
        ],
        axis=1,
    )
    cosine, sine = rope_tables(SEQ_LEN)
    if on_square:
        shared_weight = after(shared_weight, gathered)
        shared_x, shared_y = swap(shared_weight, 1), swap(shared_weight, 2)
        hidden_all, shared_x, shared_y, chosen = together(hidden_all, shared_x, shared_y, chosen)
    hidden_all, in_weight, cosine, sine = together(hidden_all, in_weight, cosine, sine)

    gained_one_all = (hidden_all.astype(F32) * attention_gain).astype(BF16)
    projected = band_total(gained_one_all, in_weight, 1)
    band_one = pick(scale_one_all.reshape(row_parts, band_rows), here_x, 0)[:, None]
    grad_top_all = spread_rows(after(grad_out, hidden_all))
    latent_part = (projected[:, head_width:used] * band_one).astype(BF16)
    latent_part = after(latent_part, grad_top_all)
    latent_all = lax.all_gather(latent_part, "gy", axis=1, tiled=True)


    if on_square:
        middle = shared_weight.shape[0] // 2
        shared_x, shared_y = after((shared_x, shared_y), latent_part)
        far = swap(shared_y[:middle], 1), swap(shared_x[middle:], 2)
    else:
        weights_of_shared = (lax.all_gather(shared_weight, "gx", axis=0, tiled=True),)
    grad_top_band = spread_rows(after(grad_top_tokens, latent_all))

    attended, logs, query_seq, key_seq, value_seq, latent_norm = attention_forward(
        piece_starts, projected, band_one, latent_all, latent_gain, expand_weight, cosine, sine, heads_here
    )
    if on_square:
        attended, *far = together(attended, *far)
        weights_of_shared = (shared_weight, shared_x, shared_y, *far)
    grad_rows = dispatch(after(chosen, attended), grad_top_all, cap, blocks)
    grad_rows = grad_rows.reshape(experts_here, row_parts, quarter_slots, -1)
    attended_all = after(collect_rows(attended), grad_rows)
    attention_part = dot(attended_all, output_weight).astype(BF16)
    after_attention = hidden + outer_total(attention_part).astype(F32)

    if on_square:
        half = experts_here // 2
        rows = after(grad_rows, attention_part, grad_top_band)
        grad_hidden_low = square_sum(rows, down_weight, 0, half, 2, True, False, BF16)
        after_attention = after(after_attention, grad_hidden_low)

    gained = (after_attention * ffn_gain).astype(BF16)
    gained_all = spread_rows(gained)
    gained_tokens = to_tokens(gained)
    gained_band = spread_rows(gained_tokens)
    squares = jnp.sum(after_attention * after_attention, axis=1)[None]
    logits = lax.dot_general(
        router_weight, gained, (((0,), (1,)), ((), ())), preferred_element_type=F32
    )
    totals = jnp.concatenate([logits, squares, jnp.zeros((7, local_rows), F32)], axis=0)
    if on_square:
        norm_one_all = hidden_all.astype(F32) * scale_one_all[:, None] * attention_gain
        norm_one_all = after(norm_one_all.astype(BF16), totals)
        rows, norm_one_all = together(after(grad_rows, totals), norm_one_all)
        grad_hidden_high = square_sum(rows, down_weight, half, half, 3, True, False, BF16)
    totals = square_total(totals)
    scale_two = lax.rsqrt(totals[EXPERTS] / D + EPS)
    probs_across = jax.nn.softmax(totals[:EXPERTS] * scale_two[None], axis=0)
    probs = probs_across.T
    norm_two = (after_attention * scale_two[:, None] * ffn_gain).astype(BF16)
    sent = jnp.concatenate(
        [
            probs_across.reshape(column_parts, experts_here, local_rows),
            jnp.broadcast_to(scale_two[None, None], (column_parts, 1, local_rows)),
        ],
        axis=1,
    )
    received = lax.all_to_all(sent, "gy", split_axis=0, concat_axis=0, tiled=True)
    received = received.transpose(0, 2, 1)
    scale_two_all = received[:, :, experts_here].reshape(all_tokens)
    received = pick(received.reshape(row_parts, quarter_blocks, local_rows, experts_here + 1), here_x, 0)
    factors = jnp.stack(
        [
            jnp.sum(jnp.where(at_slot, value[:, :, :, None], 0.0), axis=1)
            .transpose(1, 0, 2)
            .reshape(experts_here, quarter_slots)
            for value in (received[:, :, :experts_here], received[:, :, experts_here:])
        ],
        axis=2,
    )
    if on_square:
        gained_all, factors = lax.optimization_barrier((gained_all, factors, grad_hidden_high))[:2]
    rows_two, slot_scale = dispatch(chosen, gained_all, cap, blocks, scale_two_all[:, None])
    rows_two = rows_two.reshape(experts_here, row_parts, quarter_slots, -1)
    slot_scale = slot_scale.reshape(experts_here, row_parts, quarter_slots, 1)

    band_scale = scale_two_all.reshape(blocks, row_parts, -1)
    band_scale = pick(band_scale, here_x, 1).reshape(-1, 1)
    shared_hidden, grad_shared_both, grad_shared_part, shared_part = shared_experts(
        after(gained_band, rows_two), band_scale, grad_top_band, weights_of_shared, order_of
    )
    grad_norm_shared = outer_total(grad_shared_part)
    shared_out = outer_total(shared_part)

    both_weights = (gate_weight, up_weight)
    if on_square:
        own, from_x, from_y, across, scaled, grad_norm_part, slot_grad, pair_x, pair_y = routed_experts(
            after(rows_two, shared_part), gate_weight, up_weight, grad_hidden_low, grad_hidden_high, factors, chosen, blocks
        )
        whole = [(own, 0), (from_x, 0), (from_y, 0), (across, 0)]
        grad_groups = [(0, experts_here, whole)]
    else:
        everything = order_of

        def whole_total(rows, weight, transposed):
            out = group(rows, everything, row_parts, (weight,), 0, experts_here, transposed)
            out = out.reshape((experts_here,) + out.shape[2:])
            return lax.psum_scatter(out, "gx", scatter_dimension=1, tiled=True)[:, 0].astype(F32)

        scale = factors[:, :, 1:2]
        scaled, grad_gate_pre, grad_up_pre, slot_grad = expert_body(
            whole_total(rows_two, gate_weight, False) * scale,
            whole_total(rows_two, up_weight, False) * scale,
            whole_total(grad_rows, down_weight, True),
            factors[:, :, 0:1],
        )
        grads = jnp.stack([grad_gate_pre, grad_up_pre], axis=1)
        whole = lax.all_gather(grads, "gx", axis=0, tiled=False)
        grad_groups = [(0, experts_here, [(whole[q], 0) for q in range(row_parts)])]
        whole = lax.all_gather(scaled[:, None], "gx", axis=0, tiled=False)
        hidden_groups = [(0, experts_here, [(whole[q], 0) for q in range(row_parts)])]

        back_rows = back(grad_groups, order_of, both_weights, True)
        back_rows = back_rows.reshape(experts_here, blocks * cap, -1)
        grad_norm_part = combine(chosen, [back_rows], cap, blocks)

    grad_norm_part = after(grad_norm_part, shared_out)
    grad_norm_routed = outer_total(grad_norm_part)

    both_shared = after(jnp.stack([grad_norm_shared, shared_out]), grad_norm_part)
    both_shared = lax.all_to_all(both_shared, "gx", split_axis=2, concat_axis=1, tiled=True)
    grad_norm_shared, shared_out = both_shared[0].astype(F32), both_shared[1].astype(F32)
    if on_square:
        scaled = after(scaled, grad_norm_shared)
        low, high = scaled[2:half], scaled[half:]
        low_x, low_y, high_x, high_y = swap(low, 1), swap(low, 2), swap(high, 1), swap(high, 2)
    slot_grad = after(slot_grad, grad_norm_part)
    slot_grad = slot_grad.reshape(experts_here, quarter_blocks, cap).transpose(1, 0, 2)
    grad_probs = jnp.sum(jnp.where(at_slot, slot_grad[:, None], 0.0), axis=3)
    grad_probs = grad_probs.reshape(band_rows, experts_here)
    grad_probs = collect(grad_probs.T).transpose(0, 2, 1).reshape(blocks, local_rows, experts_here)
    grad_probs = lax.all_to_all(grad_probs, "gy", split_axis=0, concat_axis=2, tiled=True)
    grad_probs = grad_probs.reshape(local_rows, EXPERTS)
    centre = jnp.sum(probs * grad_probs, axis=1, keepdims=True)
    grad_logits = (probs * (grad_probs - centre)).astype(BF16)
    grad_norm_router = dot_nt(grad_logits, router_weight)
    grad_router_part = dot_tn(norm_two, grad_logits)
    grad_norm_routed, grad_norm_router = together(grad_norm_routed, grad_norm_router)
    grad_norm_two = grad_norm_routed.astype(F32) + grad_norm_shared + grad_norm_router

    scaled_after = after_attention * ffn_gain
    row_two = jnp.sum(scaled_after * grad_norm_two, axis=1)
    if on_square and local_rows == 512:
        row_two = small_totals(jnp.pad(row_two.reshape(4, 128), ((0, 4), (0, 0))), None, 4)[0][:4].reshape(-1)
    else:
        row_two = feature_total(row_two)
    grad_after = grad_top + norm_backward(
        after_attention, scale_two, ffn_gain, grad_norm_two, row_two, D
    )
    grad_ffn_part = jnp.sum(grad_norm_two * after_attention * scale_two[:, None], axis=0)
    grad_after_sent = grad_after.astype(BF16)
    grad_after_all = spread_rows(grad_after_sent)

    grad_router = tower_step(after(grad_router_part, grad_after_sent), 0)
    grad_after_all, grad_router = together(grad_after_all, grad_router)
    waiting = after(rows_two, grad_after_sent)
    grad_gate, grad_up = weight_grad(waiting, grad_groups, order_of, False, slot_scale)
    grad_after_all, grad_gate, grad_up = together(grad_after_all, grad_gate, grad_up)
    if on_square:
        grad_after_all, low_x, low_y, high_x, high_y = together(
            grad_after_all, low_x, low_y, high_x, high_y
        )

    grad_attended = band_total(grad_after_all, output_weight, 6, True, BF16)
    if on_square:
        pair_far, low_y, high_x = after((pair_y, low_y, high_x), grad_attended)
        pair_far, low_far, high_far = swap(pair_far, 1), swap(low_y, 1), swap(high_x, 2)
        hidden_groups = [
            (0, 2, [(scaled, 0), (pair_x, 0), (pair_y, 0), (pair_far, 0)]),
            (2, half - 2, [(low, 0), (low_x, 0), (low_y, 0), (low_far, 0)]),
            (half, half, [(high, 0), (high_x, 0), (high_y, 0), (high_far, 0)]),
        ]
    grad_query_pre, grad_expanded, latent_grads = attention_backward(
        piece_starts, query_seq, key_seq, value_seq, logs, grad_attended, expand_weight, cosine, sine
    )
    own_rows = band_rows // column_parts
    latent_sums = outer_total(latent_grads).astype(F32)
    grad_router = tower_step(after(grad_router, latent_grads), 1)
    expand_part = dot_tn(latent_norm, grad_expanded).astype(BF16)
    if on_square:
        expand_away = swap(expand_part, 1)

    if on_square:
        query_x, query_y = swap(grad_query_pre, 1), swap(grad_query_pre, 2)
    grad_shared = shared_weights(
        after(gained_band, latent_grads), grad_shared_both, grad_top_band, shared_hidden
    )
    waiting = after(down_weight, latent_grads, grad_shared)
    out = back(hidden_groups, order_of, (waiting,), False)
    if on_square:
        out, query_x, query_y = together(out, query_x, query_y)
        middle = band_rows // 2
        far = swap(query_y[:middle], 1), swap(query_x[middle:], 2)
        query_blocks = (grad_query_pre, query_x, query_y, *far)
    out = out.reshape(experts_here, blocks * cap, -1)
    routed_part = combine(chosen, [out], cap, blocks)
    if on_square:
        routed_part, expand_away = together(routed_part, expand_away)
        expand_x = expand_part + expand_away
    routed_part, grad_router = together(routed_part, grad_router)
    latent_sums, routed_part = together(latent_sums, routed_part)
    routed = outer_total(routed_part)
    latent_f32 = lax.dynamic_slice_in_dim(latent_all, here_y * own_rows, own_rows, 0).astype(F32)
    compressed = latent_f32[:, :L]
    latent_scale = lax.rsqrt(jnp.mean(compressed * compressed, axis=1) + EPS)
    grad_latent_norm, grad_rope_key = latent_sums[:, :L], latent_sums[:, L:]
    latent_row = jnp.sum(compressed * latent_gain * grad_latent_norm, axis=1)
    grad_compressed = norm_backward(
        compressed, latent_scale, latent_gain, grad_latent_norm, latent_row, L
    )
    grad_gain_part = jnp.sum(grad_latent_norm * compressed * latent_scale[:, None], axis=0)
    grad_latent_pre = jnp.concatenate([grad_compressed, grad_rope_key], axis=1).astype(BF16)
    grad_latent_own = grad_latent_pre.reshape(own_rows, column_parts, latent_width).transpose(1, 0, 2)
    grad_latent_own = lax.all_to_all(grad_latent_own, "gy", split_axis=0, concat_axis=0, tiled=True)
    if on_square:
        expand_y = swap(after(expand_x, grad_latent_pre), 2)
        grad_latent_own, expand_y = together(grad_latent_own, expand_y)
    grad_latent_own = grad_latent_own.reshape(band_rows, latent_width)
    grad_latent_own = widen(grad_latent_own, up_to(used) - head_width)
    if on_square:
        latent_blocks = (grad_latent_own, *from_others(grad_latent_own))
        grad_projected_all, grad_norm_part = norm_products(
            query_blocks, latent_blocks, in_weight, order_of
        )
        grad_projected_all = grad_projected_all.reshape(all_tokens, -1)
        grad_norm_part = grad_norm_part.reshape(all_tokens, -1)
    else:
        grad_projected = jnp.concatenate([grad_query_pre, grad_latent_own], axis=1)
        grad_projected_all = collect_rows(grad_projected)
        grad_norm_part = dot_nt(grad_projected_all, in_weight).astype(BF16)
    grad_norm_one = outer_total(grad_norm_part).astype(F32)

    mixed = (after_attention + routed.astype(F32) + shared_out).astype(BF16)
    if not on_square:
        norm_one_all = hidden_all.astype(F32) * scale_one_all[:, None] * attention_gain
        norm_one_all = norm_one_all.astype(BF16)
    norm_one_all = after(norm_one_all, grad_norm_part)
    grad_projected = dot_tn(norm_one_all, grad_projected_all)
    grad_query = grad_projected[:, :head_width]
    grad_query = jnp.concatenate(
        [
            grad_query[:, : heads_here * DN].reshape(-1, heads_here, DN),
            grad_query[:, heads_here * DN :].reshape(-1, heads_here, DR),
        ],
        axis=2,
    ).reshape(-1, head_width)
    grad_latent = grad_projected[:, head_width:used]
    grad_output = dot_tn(attended_all, after(grad_after_all, grad_norm_part))
    if on_square:
        grad_expand = expand_x.astype(F32) + expand_y.astype(F32)
    else:
        grad_expand = lax.psum(expand_part, "gx").astype(F32)
    grad_router = tower_step(tower_step(after(grad_router, grad_norm_part), 2), 3)
    grad_shared = inner_rows(after(grad_shared, grad_norm_part))
    (grad_down,) = weight_grad(after(grad_rows, grad_norm_part), hidden_groups, order_of, True)
    grad_norm_one, grad_query, grad_latent, grad_output, grad_expand, grad_down = together(
        grad_norm_one, grad_query, grad_latent, grad_output, grad_expand, grad_down
    )
    row_one = jnp.sum(hidden * attention_gain * grad_norm_one, axis=1)
    grad_attention_part = jnp.sum(grad_norm_one * hidden * scale_one[:, None], axis=0)
    if on_square and local_rows == 512 and local_width == 512:
        inner = jnp.concatenate([row_one, grad_gain_part]).reshape(8, 128)
        outer = jnp.concatenate([grad_attention_part, grad_ffn_part]).reshape(8, 128)
        inner, outer = small_totals(inner, outer, 5)
        row_one = inner[:4].reshape(-1)
        grad_attention_gain = outer[:4].reshape(-1)
        grad_ffn_gain = outer[4:8].reshape(-1)
        grad_latent_gain = outer[12:].reshape(-1)
    else:
        row_one, grad_latent_gain = feature_total((row_one, grad_gain_part))
        grad_attention_gain, grad_ffn_gain, grad_latent_gain = lax.psum(
            (grad_attention_part, grad_ffn_part, grad_latent_gain), "gy"
        )
    grad_hidden = grad_after + norm_backward(
        hidden, scale_one, attention_gain, grad_norm_one, row_one, D
    )
    grad_shared_gate, grad_shared_up, grad_shared_down = shared_sums(
        after(grad_shared, row_one), shared_width
    )
    grad_shared_gate, grad_shared_up = grad_shared_gate.T, grad_shared_up.T
    grad_latent_gain = settle(grad_latent_gain)
    return (
        mixed,
        grad_hidden,
        grad_query,
        grad_latent,
        grad_latent_gain,
        grad_expand,
        grad_output,
        grad_attention_gain,
        grad_ffn_gain,
        grad_router,
        grad_gate,
        grad_up,
        grad_down,
        grad_shared_gate,
        grad_shared_up,
        grad_shared_down,
    )


def solution(mesh):
    return jax.shard_map(
        per_device,
        mesh=mesh,
        in_specs=(
            P("gy", "gx"),
            P("gy", None),
            P("gx", None),
            P("gx", "gy"),
            P("gx", "gy"),
            P(),
            P(None, "gy"),
            P("gy", "gx"),
            P("gx"),
            P("gx"),
            P("gx", None),
            P("gy", "gx", None),
            P("gy", "gx", None),
            P("gy", None, "gx"),
            P("gx", "gy"),
            P("gx", "gy"),
            P("gy", "gx"),
            P("gy", "gx"),
        ),
        out_specs=(
            P("gy", "gx"),
            P("gy", "gx"),
            P("gx", "gy"),
            P("gx", "gy"),
            P(),
            P(None, "gy"),
            P("gy", "gx"),
            P("gx"),
            P("gx"),
            P("gx", None),
            P("gy", "gx", None),
            P("gy", "gx", None),
            P("gy", None, "gx"),
            P("gx", "gy"),
            P("gx", "gy"),
            P("gy", "gx"),
        ),
        check_vma=False,
    )
```
